32 devices in a mesh: dp: 8 (over z, y), tensor: 4 (over x, core).
Axes of the slice: x: 2, y: 2, z: 4, core: 2. Of those that a mesh axis runs over, the one named last changes fastest.
Arguments:
- content: bfloat16 [16384, 768], P(('dp', 'tensor')), may hold values from -6 to 6
- query_stream: bfloat16 [16384, 768], P(('dp', 'tensor')), may hold values from -6 to 6
- cot_content: bfloat16 [16384, 768], P(('dp', 'tensor')), may hold values from -6 to 6
- cot_query: bfloat16 [16384, 768], P(('dp', 'tensor')), may hold values from -6 to 6
- doc_lengths: int32 [32, 8], P('dp'), may hold values from 1 to 256, as said below
- rank_order: int32 [32, 512], P('dp'), may hold values from 0 to 511, as said below
- pred_counts: int32 [32], P('dp'), may hold values from 64 to 127
- w_qkv: bfloat16 [3, 768, 768], P(None, None, 'tensor'), may hold values from -0.21875 to 0.21875
- bias_qv: bfloat16 [2, 768], P(None, 'tensor'), may hold values from -1.5 to 1.5
- w_attn_out: bfloat16 [768, 768], P('tensor'), may hold values from -0.875 to 0.875
- b_attn_out: bfloat16 [768], replicated, may hold values from -2.5 to 2.5
- norm1_gain: float32 [768], replicated, may hold values from 0.1 to 1.9
- norm1_shift: float32 [768], replicated, may hold values from -2.5 to 2.5
- w_in: bfloat16 [768, 3072], P(None, 'tensor'), may hold values from -0.21875 to 0.21875
- b_in: bfloat16 [3072], P('tensor'), may hold values from -2.5 to 2.5
- w_out: bfloat16 [3072, 768], P('tensor'), may hold values from -0.109375 to 0.109375
- b_out: bfloat16 [768], replicated, may hold values from -2.5 to 2.5
- norm2_gain: float32 [768], replicated, may hold values from 0.1 to 1.9
- norm2_shift: float32 [768], replicated, may hold values from -2.5 to 2.5
- rel_table: bfloat16 [32, 12], P(None, 'tensor'), may hold values from -4 to 4
Outputs:
- out_content: bfloat16 [16384, 768], P(('dp', 'tensor'))
- out_query: bfloat16 [16384, 768], P(('dp', 'tensor'))
- grad_content: float32 [16384, 768], P(('dp', 'tensor'))
- grad_query: float32 [16384, 768], P(('dp', 'tensor'))
- grad_w_qkv: float32 [3, 768, 768], P(None, 'dp', 'tensor')
- grad_bias_qv: float32 [2, 768], P(None, 'tensor')
- grad_w_attn_out: float32 [768, 768], P('tensor', 'dp')
- grad_b_attn_out: float32 [768], replicated
- grad_norm1_gain: float32 [768], replicated
- grad_norm1_shift: float32 [768], replicated
- grad_w_in: float32 [768, 3072], P('dp', 'tensor')
- grad_b_in: float32 [3072], P('tensor')
- grad_w_out: float32 [3072, 768], P('tensor', 'dp')
- grad_b_out: float32 [768], replicated
- grad_norm2_gain: float32 [768], replicated
- grad_norm2_shift: float32 [768], replicated
- grad_rel_table: float32 [32, 12], P(None, 'tensor')
The draws below stay inside these ranges and needn't reach their ends.
Inputs may be any that keep to these rules, and one draw needn't show every extreme that they name: `doc_lengths`: each row's 8 lengths sum to 512; one of them is 256. `rank_order`: each row is a permutation of 0 to 511; the first position of every document has a rank below 8.
All inputs are finite; a program needn't handle non-finite values.
Results may differ from the reference program's by a relative error of at most 0.015.
The reference program's roundings to bfloat16 on the way count: a program that leaves them out, or rounds other values in their place, can miss the bound.
Values may be sent and summed in bfloat16 or wider, within the bound.
A program may use at most 192 MiB of HBM per device.

```python
import math
import jax
import jax.numpy as jnp
from jax import lax

D = 768
HEADS = 12
FF = 3072
BUCKETS = 32
SEQ_LEN = 512
DOCS = 8
SEQS = 32
TOKENS = 16384


def row_layout(key):
    half_len = SEQ_LEN // 2
    key_slot, key_cuts, key_order = jax.random.split(key, 3)
    doc_slot = jax.random.randint(key_slot, (), 0, DOCS)
    shuffled = jax.random.permutation(key_cuts, half_len - 1)
    flagged = shuffled < DOCS - 2
    cut_places = jnp.nonzero(flagged, size=DOCS - 2)[0].astype(jnp.int32) + 1
    boundary = jnp.concatenate([jnp.zeros((1,), jnp.int32), cut_places, jnp.full((1,), half_len, jnp.int32)])
    pieces = boundary[1:] - boundary[:-1]
    places = jnp.arange(DOCS, dtype=jnp.int32)
    source = jnp.clip(jnp.where(places < doc_slot, places, places - 1), 0, DOCS - 2)
    lengths = jnp.where(places == doc_slot, half_len, pieces[source]).astype(jnp.int32)
    doc_ends = jnp.cumsum(lengths)
    starts = doc_ends - lengths
    positions = jnp.arange(SEQ_LEN, dtype=jnp.int32)
    is_start = jnp.any(positions[:, None] == starts[None, :], axis=1).astype(jnp.int32)
    scores = jax.random.permutation(key_order, SEQ_LEN).astype(jnp.int32) - SEQ_LEN * is_start
    rank_rows = jnp.argsort(jnp.argsort(scores, stable=True), stable=True).astype(jnp.int32)
    return (lengths, rank_rows)


def shared_layout(key):
    row_keys = jax.random.split(key, SEQS)
    return jax.vmap(row_layout)(row_keys)


def draw_doc_lengths(key, part):
    lengths, rank_rows = shared_layout(key)
    return lengths


def draw_rank_order(key, part):
    lengths, rank_rows = shared_layout(key)
    return rank_rows


def touch_ends(drawn, stream_key, low, top_value):
    shape = drawn.shape
    index_at = [jax.random.randint(jax.random.fold_in(stream_key, axis), (), 0, shape[axis]) for axis in range(len(shape))]
    drawn = drawn.at[tuple(index_at)].set(low)
    longest = shape.index(max(shape))
    index_at[longest] = (index_at[longest] + 1) % shape[longest]
    return drawn.at[tuple(index_at)].set(top_value)


def with_spikes(drawn, own_key, source, target, blocks, factor):
    def block_of(axis_at):
        return (jnp.arange(drawn.shape[axis_at]) // (drawn.shape[axis_at] // blocks)).reshape((-1,) + (1,) * (drawn.ndim - 1 - axis_at))

    near = jax.random.permutation(own_key, blocks)[block_of(target)]
    far = (block_of(target) + blocks // 2) % blocks
    return jnp.where((block_of(source) == near) | (block_of(source) == far), factor * drawn, drawn)


def shard_levels(key, dims, cuts, least, high):
    level = 1.0
    for dim, parts in cuts:
        draws = jax.random.uniform(jax.random.fold_in(jax.random.fold_in(key, 6), dim), (parts,), jnp.float32, least / len(cuts), high / len(cuts))
        level = level * jnp.repeat(jnp.exp(draws), dims[dim] // parts).reshape((-1,) + (1,) * (len(dims) - 1 - dim))
    return level


def bell_draw(rng, shape, width, bound, cuts=(), kind=jnp.bfloat16):
    values = jax.random.normal(rng, shape, jnp.float32) * width
    if len(cuts) > 0:
        values = shard_levels(rng, shape, cuts, -0.22, 0.18) * values
    return jnp.clip(values, min=-bound, max=bound).astype(kind)


def bell_draw_with(rng, shape, spread, bound, cuts, heavy, held_as=jnp.bfloat16):
    drawn = spread * jax.random.normal(rng, shape, jnp.float32)
    if cuts:
        drawn = drawn * shard_levels(rng, shape, cuts, -0.22, 0.18)
    return jnp.clip(with_spikes(drawn, jax.random.fold_in(rng, 3), *heavy), -bound, bound).astype(held_as)


def setup_inputs(seed: int = 0) -> dict:
    keys = jax.random.split(jax.random.key(seed), 21)
    return {
        "content": bell_draw(keys[0], (TOKENS, D), 1.0, 6.0, ((0, 32),)),
        "query_stream": bell_draw(keys[1], (TOKENS, D), 1.0, 6.0, ((0, 32),)),
        "cot_content": bell_draw_with(keys[2], (TOKENS, D), 1.0, 6.0, ((0, 32),), (0, 1, 32, 2.75)),
        "cot_query": bell_draw(keys[3], (TOKENS, D), 1.0, 6.0, ((0, 32),)),
        "doc_lengths": draw_doc_lengths(jax.random.fold_in(keys[20], 71), 0),
        "rank_order": draw_rank_order(jax.random.fold_in(keys[20], 71), 0),
        "pred_counts": touch_ends(jax.random.randint(keys[6], (SEQS,), SEQ_LEN // 8, SEQ_LEN // 4), jax.random.fold_in(keys[6], 1), SEQ_LEN // 8, (SEQ_LEN // 4) - 1).astype(jnp.int32),
        "w_qkv": bell_draw(keys[7], (3, D, D), D ** -0.5, 0.21875, ((2, 4),)),
        "bias_qv": bell_draw(keys[8], (2, D), 0.3, 1.5, ((1, 4),)),
        "w_attn_out": bell_draw(keys[9], (D, D), (D // 16) ** -0.5, 0.875, ((0, 4),)),
        "b_attn_out": bell_draw(keys[10], (D,), 0.5, 2.5),
        "norm1_gain": jnp.clip(1.0 + 0.18 * jax.random.normal(keys[11], (D,), jnp.float32), 0.1, 1.9),
        "norm1_shift": bell_draw(keys[12], (D,), 0.5, 2.5, (), jnp.float32),
        "w_in": bell_draw(keys[13], (D, FF), D ** -0.5, 0.21875, ((1, 4),)),
        "b_in": bell_draw(keys[14], (FF,), 0.5, 2.5, ((0, 4),)),
        "w_out": bell_draw(keys[15], (FF, D), FF ** -0.5, 0.109375, ((0, 4),)),
        "b_out": bell_draw(keys[16], (D,), 0.5, 2.5),
        "norm2_gain": jnp.clip(1.0 + 0.18 * jax.random.normal(keys[17], (D,), jnp.float32), 0.1, 1.9),
        "norm2_shift": bell_draw(keys[18], (D,), 0.5, 2.5, (), jnp.float32),
        "rel_table": bell_draw(keys[19], (BUCKETS, HEADS), 1.0, 4.0, ((1, 4),)),
    }


@jax.custom_vjp
def low(v):
    return lax.optimization_barrier(v.astype(jnp.bfloat16)).astype(jnp.float32)

@jax.custom_vjp
def low_back(v):
    return v

def low_keep(v):
    return (low(v), None)

def low_pass(kept, grad):
    return (grad,)

def back_keep(v):
    return (v, None)

def back_low(kept, grad):
    return (low(grad),)
low.defvjp(low_keep, low_pass)
low_back.defvjp(back_keep, back_low)
HIGHEST = lax.Precision.HIGHEST
EDGES = (1, 2, 3, 4, 5, 6, 7, 8, 12, 16, 23, 32, 46, 64, 91)
NEGATIVE = -1e+30
EPSILON = 1e-05

def matmul(left_rows, right_rows):
    return jnp.dot(left_rows, right_rows, precision=HIGHEST, preferred_element_type=jnp.float32)

def bucket_ids(length):
    places = jnp.arange(length, dtype=jnp.int32)
    offsets = places[None, :] - places[:, None]
    distance = jnp.abs(offsets)
    result = jnp.where(offsets > 0, 16, 0).astype(jnp.int32)
    for boundary in EDGES:
        result = result + (distance >= boundary).astype(jnp.int32)
    return result

def stream_masks(lengths_row, rank_row, pred_count):
    length = rank_row.shape[0]
    places = jnp.arange(length, dtype=jnp.int32)
    doc_ends = jnp.cumsum(lengths_row)
    doc_ids = lax.optimization_barrier(jnp.sum((places[:, None] >= doc_ends[None, :]).astype(jnp.int32), axis=1))
    same_doc = doc_ids[:, None] == doc_ids[None, :]
    unmasked = rank_row[None, :] < length - pred_count
    earlier = rank_row[None, :] < rank_row[:, None]
    itself = places[:, None] == places[None, :]
    content_mask = same_doc & (unmasked | earlier | itself)
    query_mask = same_doc & (unmasked | earlier)
    return (content_mask, query_mask)

def layer_norm(rows_in, gain_vec, norm_shift):
    mean_row = lax.optimization_barrier(jnp.mean(rows_in, axis=-1, keepdims=True))
    centred = rows_in - mean_row
    variance = lax.optimization_barrier(jnp.mean(centred * centred, axis=-1, keepdims=True))
    return centred * lax.rsqrt(variance + EPSILON) * gain_vec + norm_shift

def attend(queries, keys_all, values, pos_bias, vis_mask):
    scale = 1.0 / math.sqrt(queries.shape[-1])
    scores = jnp.einsum('ihd,jhd->hij', queries, keys_all, precision=HIGHEST) * scale + pos_bias
    scores = low_back(scores)
    masked = jnp.where(vis_mask[None], scores, NEGATIVE)
    row_max = lax.optimization_barrier(jnp.max(masked, axis=-1, keepdims=True))
    exp_terms = jnp.exp(masked - row_max)
    probs = exp_terms / lax.optimization_barrier(jnp.sum(exp_terms, axis=-1, keepdims=True))
    return jnp.einsum('hij,jhd->ihd', low(probs), values, precision=HIGHEST)

def layer_forward(rows_one, rows_two, weight_set, buckets, masks_c, masks_g):
    w_qkv, bias_qv, w_attn_out, b_attn_out, norm1_gain, norm1_shift, w_in, b_in, w_out, b_out, norm2_gain, norm2_shift, rel_table = weight_set
    seq_count = masks_c.shape[0]
    length = buckets.shape[0]
    head_count = rel_table.shape[1]
    width_all = rows_one.shape[1]
    head_size = width_all // head_count

    def project(rows_in, weight, offset):
        return low(low_back(matmul(rows_in, weight) + offset))
    q_content = project(rows_one, w_qkv[0], bias_qv[0])
    keys_all = low(low_back(matmul(rows_one, w_qkv[1])))
    values = project(rows_one, w_qkv[2], bias_qv[1])
    q_query = project(rows_two, w_qkv[0], bias_qv[0])
    pos_bias = jnp.transpose(rel_table[buckets], (2, 0, 1))

    def by_heads(rows_in):
        return rows_in.reshape(seq_count, length, head_count, head_size)

    def both_streams(item_set):
        query_one, query_two, key_rows, value_rows, mask_one, mask_two = item_set
        return (attend(query_one, key_rows, value_rows, pos_bias, mask_one), attend(query_two, key_rows, value_rows, pos_bias, mask_two))
    mixed_c, mixed_g = lax.map(jax.checkpoint(both_streams), (by_heads(q_content), by_heads(q_query), by_heads(keys_all), by_heads(values), masks_c, masks_g))

    def finish(rows_in, mixed):
        attn_rows = low(low_back(mixed.reshape(seq_count * length, width_all)))
        res_one = rows_in + low_back(matmul(attn_rows, w_attn_out)) + b_attn_out
        hidden = low(layer_norm(res_one, norm1_gain, norm1_shift))
        pre_act = low_back(matmul(hidden, w_in) + b_in)
        act_rows = low(jax.nn.gelu(pre_act, approximate=False))
        res_two = hidden + low_back(matmul(act_rows, w_out)) + b_out
        return layer_norm(res_two, norm2_gain, norm2_shift)
    return (finish(rows_one, mixed_c), finish(rows_two, mixed_g))

def reference(content, query_stream, cot_content, cot_query, doc_lengths, rank_order, pred_counts, w_qkv, bias_qv, w_attn_out, b_attn_out, norm1_gain, norm1_shift, w_in, b_in, w_out, b_out, norm2_gain, norm2_shift, rel_table):
    seq_total, length = rank_order.shape
    group_size = math.gcd(seq_total, 8)
    rounds = seq_total // group_size
    width_all = content.shape[1]
    buckets = bucket_ids(length)
    params = tuple((param.astype(jnp.float32) for param in (w_qkv, bias_qv, w_attn_out, b_attn_out, norm1_gain, norm1_shift, w_in, b_in, w_out, b_out, norm2_gain, norm2_shift, rel_table)))

    def regroup(array_in):
        return array_in.reshape(rounds, group_size * length, width_all)

    def scan_step(accum, item_set):
        rows_c, rows_g, cot_c, cot_g, lengths_g, ranks_g, counts_g = item_set
        masks_c, masks_g = jax.vmap(stream_masks)(lengths_g, ranks_g, counts_g)

        def forward(rows_one, rows_two, *weight_set):
            return layer_forward(rows_one, rows_two, weight_set, buckets, masks_c, masks_g)
        outputs, pullback = jax.vjp(forward, rows_c.astype(jnp.float32), rows_g.astype(jnp.float32), *params)
        grad_set = pullback((cot_c.astype(jnp.float32), cot_g.astype(jnp.float32)))
        accum = tuple((earlier_sum + addition for earlier_sum, addition in zip(accum, grad_set[2:])))
        return (accum, (outputs[0].astype(jnp.bfloat16), outputs[1].astype(jnp.bfloat16), grad_set[0], grad_set[1]))
    zeros_init = tuple((jnp.zeros_like(param) for param in params))
    totals, stacked = lax.scan(scan_step, zeros_init, (regroup(content), regroup(query_stream), regroup(cot_content), regroup(cot_query), doc_lengths.reshape(rounds, group_size, doc_lengths.shape[1]), rank_order.reshape(rounds, group_size, length), pred_counts.reshape(rounds, group_size)))
    token_total = seq_total * length
    out_content = stacked[0].reshape(token_total, width_all)
    out_query = stacked[1].reshape(token_total, width_all)
    grad_content = stacked[2].reshape(token_total, width_all)
    grad_query = stacked[3].reshape(token_total, width_all)
    return (out_content, out_query, grad_content, grad_query, totals[0], totals[1], totals[2], totals[3], totals[4], totals[5], totals[6], totals[7], totals[8], totals[9], totals[10], totals[11], totals[12])
```

```python
import functools

import jax
import jax.numpy as jnp
from jax import lax
from jax.experimental import pallas as pl
from jax.experimental.pallas import tpu as pltpu
from jax.sharding import PartitionSpec as P

EDGES = (1, 2, 3, 4, 5, 6, 7, 8, 12, 16, 23, 32, 46, 64, 91)
EPSILON = 1e-05
F32 = jnp.float32
BF16 = jnp.bfloat16
S = 512
HALF = 256
D = 768
HD = 64
SLOTS = 4
SLOT_HEADS = 3
QW = SLOT_HEADS * HD
NEGATIVE = -1e30
ROWS = D // 8
HROWS = D // 2
MESH = pl.DeviceIdType.MESH


def nn(a, b):
    return jnp.dot(a, b, preferred_element_type=F32)


def nt(a, b):
    return lax.dot_general(a, b, (((1,), (1,)), ((), ())), preferred_element_type=F32)


def tn(a, b):
    return lax.dot_general(a, b, (((0,), (0,)), ((), ())), preferred_element_type=F32)


def iota(shape, axis):
    return lax.broadcasted_iota(jnp.int32, shape, axis)


def bucket_onehot():
    lanes = iota((32, S), 1)
    offset = jnp.where(lanes < HALF, -lanes, S - lanes)
    distance = jnp.abs(offset)
    bucket = jnp.where(offset > 0, 16, 0)
    for edge in EDGES:
        bucket = bucket + (distance >= edge).astype(jnp.int32)
    return (bucket == iota((32, S), 0)).astype(F32)


def gelu_pair(v):
    cdf = 0.5 + 0.5 * lax.erf(v * 0.7071067811865476)
    return v * cdf, cdf + v * (jnp.exp(-0.5 * v * v) * 0.3989422804014327)


def row_mean(v):
    return jnp.sum(v, axis=-1, keepdims=True) * (1.0 / D)


def col_sum(v):
    return jnp.sum(v, axis=0, keepdims=True)


def kernel(
    stride,
    dl, pc, rank, x_hbm, g_hbm, cc_hbm, cg_hbm, wq_in, wo_in, wi_in, w2_in, sm_in, vectors,
    oc_hbm, og_hbm, gc_hbm, gg_hbm, stash, g_res, sm_res,
    perm, unperm, xin, hid, tA, tB, attn, qkv, qg, xhat, rstd1, act, dg, acc,
    mask, square, lines, wq, wo, wi, w2, wsm,
    ga, gb, rca, rcb, rxa, ryb, smx, smy, smz, smw, r1, r2, r3, r4,
    lsem, xs, xr, cs, cr, ss, sr, os, orr, ps, pr, credit,
):
    b_attn, n1g, n1s, b_out, n2g, n2s = (vectors.at[k:k + 1] for k in range(6))
    bias = dsacc = square
    text = diag = lines
    t = lax.axis_index("tensor")
    d = lax.axis_index("dp")
    yb = lax.rem(lax.div(d, stride), 2)
    zb = lax.rem(lax.div(d, 2 * stride), 4)
    zbit = lax.rem(zb, 2)
    z_of = (zb, zb + 1 - 2 * zbit, lax.rem(zb + 2, 4), 3 - zb)
    core = (d, t + 1 - 2 * lax.rem(t, 2))
    xdev = (d, lax.rem(t + 2, 4))
    diagonal = (d, 3 - t)
    ydev = (d + stride - 2 * stride * yb, t)
    zdev = [None] + [(d + 2 * stride * (z_of[k] - zb), t) for k in (1, 2, 3)]

    barrier = pltpu.get_barrier_semaphore()
    for who in (core, xdev, diagonal, ydev, zdev[1], zdev[2], zdev[3]):
        pl.semaphore_signal(barrier, inc=1, device_id=who, device_id_type=MESH)
    pl.semaphore_wait(barrier, 7)

    def remote(src, dst, send, recv, who):
        return pltpu.make_async_remote_copy(
            src_ref=src, dst_ref=dst, send_sem=send, recv_sem=recv, device_id=who, device_id_type=MESH
        )

    parts = (
        (wq_in, lambda s, lo, n: wq.at[s, pl.ds(lo, n)], 3 * QW, 2),
        (wo_in, lambda s, lo, n: wo.at[pl.ds(s * QW + lo, n)], QW, 1),
        (wi_in, lambda s, lo, n: wi.at[s, pl.ds(lo, n)], D, 2),
        (w2_in, lambda s, lo, n: w2.at[s, pl.ds(lo, n)], D, 2),
    )
    items = []
    for p, (_, _, n, count) in enumerate(parts):
        for i in range(count):
            items.append((p, n // 2, i * (n // 2 // count), n // 2 // count))

    def mine(i, other):
        p, half, lo, n = items[i]
        return pl.multiple_of((1 - yb if other else yb) * half + lo, 16), n

    def x_copy(i):
        src, place, _, _ = parts[items[i][0]]
        lo, n = mine(i, False)
        return remote(src.at[pl.ds(lo, n)], place(2, lo, n), xs.at[i, 0], xr.at[i, 0], xdev)

    def y_copy(i):
        place = parts[items[i][0]][1]
        lo, n = mine(i, False)
        return remote(place(2, lo, n), place(2, lo, n), xs.at[i, 1], xr.at[i, 1], ydev)

    def c_copy(i, other):
        place = parts[items[i][0]][1]
        lo, n = mine(i, other)
        k = 3 if other else 2
        return remote(place(2, lo, n), place(3, lo, n), xs.at[i, k], xr.at[i, k], core)

    def core_copy(p):
        src, place, n, _ = parts[p]
        return remote(src, place(1, 0, n), cs.at[p], cr.at[p], core)

    def small_copy(k):
        return remote(sm_in, wsm.at[k], ss.at[k - 1], sr.at[k - 1], (core, xdev, diagonal)[k - 1])

    def own_copy(p):
        src, place, n, _ = parts[p]
        return pltpu.make_async_copy(src, place(0, 0, n), lsem.at[2 + p])

    def small_own():
        return pltpu.make_async_copy(sm_in, wsm.at[0], lsem.at[6])

    def arrived_x(i):
        x_copy(i).wait_recv()
        y_copy(i).start()
        c_copy(i, False).start()

    def arrived_y(i):
        y_copy(i).wait_recv()
        c_copy(i, True).start()

    def arrived_core(i):
        c_copy(i, False).wait_recv()
        c_copy(i, True).wait_recv()

    def fetch(one, two):
        return [
            pltpu.make_async_copy(one, xin.at[0:S], lsem.at[0]),
            pltpu.make_async_copy(two, xin.at[S:2 * S], lsem.at[1]),
        ]

    def stash_copy(s, back):
        ends = (stash.at[s], dg.at[s]) if back else (dg.at[s], stash.at[s])
        return pltpu.make_async_copy(ends[0], ends[1], lsem.at[7 + s])

    small_own().start()
    own_copy(0).start()
    rows_in = fetch(x_hbm, g_hbm)
    for copy in rows_in:
        copy.start()
    for k in (1, 2, 3):
        small_copy(k).start()
    core_copy(0).start()
    for i in range(len(items)):
        x_copy(i).start()
    for p in (1, 2, 3):
        core_copy(p).start()
        own_copy(p).start()

    end = jnp.int32(0)
    start = jnp.int32(0)
    ends = []
    for k in range(8):
        length = dl[t, k]
        start = jnp.where(length == HALF, end, start)
        end = end + length
        ends.append(end)
    limit = (S - pc[t]).astype(F32)
    rows = iota((S, 1), 0)
    lanes = iota((1, S), 1)
    source_r = (rows + start) & (S - 1)
    source_l = (lanes + start) & (S - 1)
    perm[...] = jnp.where(source_r == lanes, 1.0, 0.0).astype(BF16)
    unperm[...] = jnp.where(((rows - start) & (S - 1)) == lanes, 1.0, 0.0).astype(BF16)
    doc_r = jnp.zeros((S, 1), F32)
    doc_l = jnp.zeros((1, S), F32)
    for e in ends:
        doc_r = doc_r + jnp.where(source_r >= e, 1.0, 0.0)
        doc_l = doc_l + jnp.where(source_l >= e, 1.0, 0.0)
    rank_row = rank[pl.ds(t, 1), :]
    sub = iota((16, S), 0)
    pieces = jnp.where(sub == 0, rank_row >> 4, jnp.where(sub == 1, rank_row & 15, 0))
    pieces = pieces.astype(F32).astype(BF16)
    ranks = nt(pieces, perm[...])
    rank_l = 16.0 * ranks[0:1] + ranks[1:2]
    ranks = nt(perm[...], pieces)
    rank_r = 16.0 * ranks[:, 0:1] + ranks[:, 1:2]
    lim_c = jnp.maximum(limit - 1.0, rank_l)
    lim_g = jnp.maximum(limit, rank_l) - 1.0
    for b in range(2):
        c = slice(HALF * b, HALF * b + HALF)
        same = doc_r[c] == doc_l[:, c]
        mask[b, :, 0:HALF] = jnp.where(same & (rank_r[c] <= lim_c[:, c]), 0.0, NEGATIVE).astype(BF16)
        mask[b, :, HALF:S] = jnp.where(same & (rank_r[c] <= lim_g[:, c]), 0.0, NEGATIVE).astype(BF16)
    onehot = bucket_onehot()
    smx[...] = jnp.zeros(smx.shape, F32)

    def transposed(dst, src):
        for st in range(2):
            r = slice(st * S, st * S + S)
            flipped = src[r].T
            for k in range(8):
                to = (k % 2) * 4 * ROWS + (k // 2) * ROWS
                dst[to:to + ROWS, r] = flipped[k * ROWS:k * ROWS + ROWS]

    def permuted(dst):
        for copy in rows_in:
            copy.wait()
        for st in range(2):
            r = slice(st * S, st * S + S)
            for f in (slice(0, HROWS), slice(HROWS, D)):
                dst[r, f] = nn(perm[...], xin[r, f]).astype(BF16)

    xp = hid
    permuted(xp)
    small_own().wait()
    own_copy(0).wait()

    def prob_at(s, h, b, st):
        k = 2 * b + st
        return dg.at[s, k * HALF:k * HALF + HALF, pl.ds(pl.multiple_of(h * HALF, HALF), HALF)]

    @pl.loop(0, SLOTS)
    def _(s):
        @pl.when(s == 1)
        def _():
            core_copy(0).wait_recv()
            small_copy(1).wait_recv()
            arrived_x(0)

        @pl.when(s == 2)
        def _():
            arrived_x(1)
            small_copy(2).wait_recv()
            arrived_y(0)
            arrived_y(1)

        @pl.when(s == 3)
        def _():
            arrived_x(2)
            small_copy(3).wait_recv()
            arrived_core(0)
            arrived_core(1)

        small = wsm[s].astype(BF16)
        table = nn(small[:, 0:32], onehot.astype(BF16))
        text[pl.ds(pl.multiple_of(8 * s, 8), 8), :] = table[3:11]
        sel = jnp.where(iota((16, 128), 0) == 1, 1.0, 0.0).astype(BF16)
        bq = tn(small[:, 0:QW], sel)[:, 0:1]
        sel = jnp.where(iota((16, 128), 0) == 2, 1.0, 0.0).astype(BF16)
        bv = tn(small[:, 0:QW], sel)[:, 0:1]
        r = nt(wq[s], xp[0:S])
        qkv[s, 0:QW] = ((r[0:QW] + bq).astype(BF16) * 0.125).astype(BF16)
        qkv[s, QW:2 * QW] = r[QW:2 * QW].astype(BF16)
        qkv[s, 2 * QW:3 * QW] = (r[2 * QW:3 * QW] + bv).astype(BF16)
        qg[s] = ((nt(wq[s, 0:QW], xp[S:2 * S]) + bq).astype(BF16) * 0.125).astype(BF16)

        @pl.loop(0, SLOT_HEADS)
        def _(h):
            hr = pl.multiple_of(h * HD, HD)
            rowvec = text[pl.ds(8 * s + h, 1), :]
            rolled = pltpu.roll(jnp.broadcast_to(rowvec, (HALF, S)), 0, 1, stride=1, stride_axis=0)
            bias[...] = rolled[:, 0:HALF]
            for b in range(2):
                c = slice(HALF * b, HALF * b + HALF)
                kT = qkv[s, pl.ds(QW + hr, HD), c]
                vT = qkv[s, pl.ds(2 * QW + hr, HD), c]
                for st in range(2):
                    qT = qkv[s, pl.ds(hr, HD), c] if st == 0 else qg[s, pl.ds(hr, HD), c]
                    l = slice(HALF * st, HALF * st + HALF)
                    sc = tn(kT, qT) + bias[...] + mask[b, :, l].astype(F32)
                    e = jnp.exp(sc - jnp.max(sc, axis=0, keepdims=True))
                    p = (e * (1.0 / jnp.sum(e, axis=0, keepdims=True))).astype(BF16)
                    prob_at(s, h, b, st)[...] = p
                    to = slice(st * S + HALF * b, st * S + HALF * b + HALF)
                    tA[pl.ds(pl.multiple_of(s * QW + hr, HD), HD), to] = nn(vT, p).astype(BF16)

        for k in range(SLOTS):
            @pl.when(s == k)
            def _():
                stash_copy(k, False).start()

    arrived_y(2)
    own_copy(1).wait()
    core_copy(1).wait_recv()
    for st in range(2):
        r = slice(st * S, st * S + S)
        attn[r] = nt(unperm[...], tA[:, r]).astype(BF16)
    arrived_core(2)
    for r in (slice(k * HALF, k * HALF + HALF) for k in range(4)):
        res = xin[r].astype(F32) + nn(attn[r], wo[...]) + b_attn[...]
        cen = res - row_mean(res)
        rs = lax.rsqrt(row_mean(cen * cen) + EPSILON)
        xh = cen * rs
        xhat[r] = xh.astype(BF16)
        rstd1[r] = rs
        hid[r] = (xh * n1g[...] + n1s[...]).astype(BF16)
    transposed(tB, hid)
    rows_in = fetch(cc_hbm, cg_hbm)
    for copy in rows_in:
        copy.start()

    own_copy(2).wait()
    own_copy(3).wait()

    @pl.loop(0, SLOTS)
    def _(s):
        @pl.when(s == 0)
        def _():
            arrived_x(3)

        @pl.when(s == 1)
        def _():
            core_copy(2).wait_recv()

        @pl.when(s == 2)
        def _():
            arrived_x(4)
            arrived_y(3)
            arrived_y(4)

        @pl.when(s == 3)
        def _():
            arrived_x(5)
            arrived_core(3)
            arrived_core(4)

        for k in range(SLOTS):
            @pl.when(s == k)
            def _():
                stash_copy(k, False).wait()
        for st in range(2):
            r = slice(st * S, st * S + S)
            for j in range(0, D, 256):
                pre = nn(hid[r], wi[s, :, j:j + 256]) + wsm[s, 0:1, j:j + 256]
                a, g = gelu_pair(pre)
                act[s, r, j:j + 256] = a.astype(BF16)
                dg[s, r, j:j + 256] = g.astype(BF16)

    for r in (slice(0, S), slice(S, 2 * S)):
        acc[r] = nn(act[0, r], w2[0])

    @pl.loop(1, SLOTS)
    def _(s):
        @pl.when(s == 1)
        def _():
            core_copy(3).wait_recv()

        @pl.when(s == 2)
        def _():
            arrived_x(6)
            arrived_y(5)
            arrived_y(6)

        @pl.when(s == 3)
        def _():
            arrived_core(5)
            arrived_core(6)

        for r in (slice(0, S), slice(S, 2 * S)):
            acc[r] += nn(act[s, r], w2[s])

    for copy in rows_in:
        copy.wait()

    @pl.loop(0, 4)
    def _(i):
        r = pl.ds(pl.multiple_of(i * HALF, HALF), HALF)
        res = hid[r, :].astype(F32) + acc[r, :] + b_out[...]
        cen = res - row_mean(res)
        rs = lax.rsqrt(row_mean(cen * cen) + EPSILON)
        xh = cen * rs
        cot = xin[r, :].astype(F32)
        hid[r, :] = (xh * n2g[...] + n2s[...]).astype(BF16)
        dxh = cot * n2g[...]
        dres = rs * (dxh - row_mean(dxh) - xh * row_mean(dxh * xh))
        acc[r, :] = dres
        xin[r, :] = dres.astype(BF16)
        smx[2, 3:4] += col_sum(dres)
        smx[2, 4:5] += col_sum(cot * xh)
        smx[2, 5:6] += col_sum(cot)

    dlow = xin
    transposed(tA, dlow)
    rows_out = [
        pltpu.make_async_copy(hid.at[0:S], oc_hbm, lsem.at[0]),
        pltpu.make_async_copy(hid.at[S:2 * S], og_hbm, lsem.at[1]),
    ]
    for copy in rows_out:
        copy.start()

    own_half = pl.ds(pl.multiple_of(yb * HROWS, HROWS), HROWS)
    other_half = pl.ds(pl.multiple_of((1 - yb) * HROWS, HROWS), HROWS)

    def block(k):
        return pl.ds(pl.multiple_of(yb * HROWS + z_of[k] * ROWS, ROWS), ROWS)

    def add(dst, src, rows_d=None, rows_s=None):
        count = dst.shape[0] if rows_d is None else HROWS

        @pl.loop(0, count // ROWS)
        def _(i):
            step = pl.multiple_of(i * ROWS, ROWS)
            a = pl.ds(step + (0 if rows_d is None else rows_d.start), ROWS)
            b = pl.ds(step + (0 if rows_s is None else rows_s.start), ROWS)
            dst[a, :] = (dst[a, :].astype(F32) + src[b, :].astype(F32)).astype(BF16)

    def rz_at(n, k, cols):
        return wi.at[(0, 1, 3, 3)[n], (k - 1) * ROWS:k * ROWS, cols]

    class Chunk:
        def __init__(self, index, even, odd, rc, rx, ry, cols, x_first):
            self.n, self.even, self.odd, self.rc = index, even, odd, rc
            self.rx, self.ry, self.cols, self.x_first = rx, ry, cols, x_first

        def sems(self, k):
            return os.at[self.n, k], orr.at[self.n, k]

        def core_send(self, k):
            return remote(self.odd[k], self.rc[k], *self.sems(k), core)

        def x_send(self):
            if self.x_first:
                return remote(self.even[1], self.rx, *self.sems(2), xdev)
            return remote(self.even[1].at[own_half], self.rx, *self.sems(2), xdev)

        def y_send(self, k):
            return remote(self.even[k].at[other_half], self.ry[k], *self.sems(3 + k), ydev)

        def z_send(self, k):
            return remote(
                self.even[0].at[block(k)], rz_at(self.n, k, self.cols), *self.sems(4 + k), zdev[k]
            )

        def core_sum(self, k):
            self.core_send(k).wait_recv()
            add(self.even[k], self.rc[k])
            if self.x_first:
                if k == 1:
                    self.x_send().start()
            else:
                self.y_send(k).start()

        def middle(self):
            if self.x_first:
                self.x_send().wait_recv()
                add(self.even[0], self.rx)
                self.y_send(0).start()
            else:
                self.y_send(1).wait_recv()
                add(self.even[1], self.ry[1], own_half)
                self.x_send().start()

        def last(self):
            self.y_send(0).wait_recv()
            add(self.even[0], self.ry[0], own_half)
            if not self.x_first:
                self.x_send().wait_recv()
                add(self.even[0], self.rx, own_half)
            for k in (1, 2, 3):
                self.z_send(k).start()

        def finish(self, out):
            total = self.even[0][block(0), :].astype(F32)
            for k in (1, 2, 3):
                self.z_send(k).wait_recv()
                total = total + rz_at(self.n, k, self.cols)[...].astype(F32)
            g_res[out, :, self.cols] = total

        def sent(self):
            for k in (0, 1) if self.n > 1 else (0,):
                self.core_send(k).wait_send()
            self.x_send().wait_send()
            self.y_send(0).wait_send()
            if not self.x_first:
                self.y_send(1).wait_send()
            for k in (1, 2, 3):
                self.z_send(k).wait_send()

    whole = pl.ds(0, D)
    first, second = pl.ds(0, D // 2), pl.ds(D // 2, D // 2)
    A = Chunk(0, (ga.at[0], ga.at[1]), (ga.at[2], ga.at[2]), (rca.at[0], rca.at[1]), rxa, (w2.at[0, HROWS:D], None), whole, True)
    B = Chunk(1, (gb.at[0], gb.at[1]), (gb.at[2], gb.at[2]), (rcb.at[0], rcb.at[1]), w2.at[0, 0:HROWS], (ryb.at[0], ryb.at[1]), whole, False)

    def c_part(index, cols, x_first):
        g = lambda s: act.at[s, 0:D, cols]
        r = lambda ref: ref.at[:, cols]
        if x_first:
            rx, ry = w2.at[1, :, cols], (w2.at[3, 0:HROWS, cols], None)
        else:
            rx, ry = w2.at[1, 0:HROWS, cols], (w2.at[3, 0:HROWS, cols], w2.at[3, HROWS:D, cols])
        return Chunk(index, (g(0), g(2)), (g(1), g(3)), (r(rca.at[0]), r(rca.at[1])), rx, ry, cols, x_first)

    C1 = c_part(2, first, True)
    C2 = c_part(3, second, False)

    def buffer_of(s):
        odd = lax.rem(s, 2)
        return 2 * odd + (1 - odd) * lax.div(s, 2)

    def after(chunks, s):
        for k in (1, 0):
            @pl.when(s == 2 * k + 1)
            def _():
                for chunk in chunks:
                    chunk.core_send(k).start()

            @pl.when(s == 2 * k)
            def _():
                for chunk in chunks:
                    chunk.core_sum(k)

    @pl.loop(0, SLOTS)
    def _(i):
        s = 3 - i

        @pl.when(s == 1)
        def _():
            A.core_send(1).wait_send()

        for r in (slice(0, HROWS), slice(HROWS, D)):
            ga[buffer_of(s), r] = nn(tA[r], act[s]).astype(BF16)
        after((A,), s)

    @pl.loop(0, SLOTS)
    def _(i):
        s = 3 - i
        place = lax.rem(s, 2) * lax.div(s, 2) + (1 - lax.rem(s, 2)) * (3 + lax.div(s, 2))
        for j in range(0, D, 256):
            part = jnp.zeros((1, 256), F32)
            for st in range(2):
                r = slice(st * S, st * S + S)
                dact = nt(dlow[r], w2[s, j:j + 256, :])
                low = (dact * dg[s, r, j:j + 256].astype(F32)).astype(BF16)
                dg[s, r, j:j + 256] = low
                part = part + col_sum(low.astype(F32))
            smx[place, 0:1, j:j + 256] = part

        @pl.when(s == 1)
        def _():
            B.core_send(1).wait_send()

        for r in (slice(0, HROWS), slice(HROWS, D)):
            gb[buffer_of(s), r] = nn(tB[r], dg[s]).astype(BF16)
        after((B,), s)
        for r in (slice(0, S), slice(S, 2 * S)):
            acc[r] += nt(dg[s, r], wi[s])
        for k in range(SLOTS):
            @pl.when(s == k)
            def _():
                stash_copy(k, True).start()

    for k, who in enumerate((core, xdev, ydev, zdev[1], zdev[2], zdev[3])):
        pl.semaphore_signal(credit.at[k], inc=1, device_id=who, device_id_type=MESH)

    @pl.loop(0, 4)
    def _(i):
        r = pl.ds(pl.multiple_of(i * HALF, HALF), HALF)
        dy = acc[r, :]
        xh = xhat[r, :].astype(F32)
        dxh = dy * n1g[...]
        dres = rstd1[r, :] * (dxh - row_mean(dxh) - xh * row_mean(dxh * xh))
        acc[r, :] = dres
        xin[r, :] = dres.astype(BF16)
        smx[2, 0:1] += col_sum(dres)
        smx[2, 1:2] += col_sum(dy * xh)
        smx[2, 2:3] += col_sum(dy)

    transposed(tB, dlow)
    for r in (slice(0, HROWS), slice(HROWS, D)):
        tA[r] = nt(wo[r], dlow[...]).astype(BF16)
    for copy in rows_out:
        copy.wait()
    rows_in = fetch(x_hbm, g_hbm)
    for copy in rows_in:
        copy.start()
    for k in range(6):
        pl.semaphore_wait(credit.at[k], 1)
    B.middle()
    for r in (slice(0, HROWS), slice(HROWS, D)):
        gwo = nn(tB[r], attn[...]).astype(BF16)
        for s in range(SLOTS):
            act[s, r, 3 * QW:D] = gwo[:, s * QW:s * QW + QW]
    for st in range(2):
        r = slice(st * S, st * S + S)
        for f in (slice(0, HROWS), slice(HROWS, D)):
            tA[f, r] = nt(tA[f, r], perm[...]).astype(BF16)
    permuted(attn)
    transposed(tB, attn)
    xpT = tB

    ones = jnp.ones((16, S), BF16)
    @pl.loop(0, SLOTS)
    def _(i):
        s = 3 - i
        for k in range(SLOTS):
            @pl.when(s == k)
            def _():
                stash_copy(k, True).wait()

        @pl.loop(0, SLOT_HEADS)
        def _(h):
            hr = pl.multiple_of(h * HD, HD)
            for b in range(2):
                c = slice(HALF * b, HALF * b + HALF)
                kT = qkv[s, pl.ds(QW + hr, HD), c]
                vT = qkv[s, pl.ds(2 * QW + hr, HD), c]
                dk = dv = None
                for st in range(2):
                    qT = qkv[s, pl.ds(hr, HD), c] if st == 0 else qg[s, pl.ds(hr, HD), c]
                    dOT = tA[pl.ds(pl.multiple_of(s * QW + hr, HD), HD), st * S + HALF * b:st * S + HALF * b + HALF]
                    p = prob_at(s, h, b, st)[...]
                    pf = p.astype(F32)
                    dp = tn(vT, dOT)
                    dsl = (pf * (dp - jnp.sum(dp * pf, axis=0, keepdims=True))).astype(BF16)
                    if b == 0 and st == 0:
                        dsacc[...] = dsl.astype(F32)
                    else:
                        dsacc[...] += dsl.astype(F32)
                    dq = (nn(kT, dsl) * 0.125).astype(BF16)
                    dk1 = nt(qT, dsl)
                    dv1 = nt(dOT, p)
                    dk = dk1 if dk is None else dk + dk1
                    dv = dv1 if dv is None else dv + dv1
                    if st == 0:
                        qkv[s, pl.ds(hr, HD), c] = dq
                    else:
                        qg[s, pl.ds(hr, HD), c] = dq
                qkv[s, pl.ds(QW + hr, HD), c] = dk.astype(BF16)
                qkv[s, pl.ds(2 * QW + hr, HD), c] = dv.astype(BF16)
            total = jnp.zeros((8, S), F32)
            for a in range(HALF // 8):
                wide = jnp.concatenate([dsacc[8 * a:8 * a + 8, :], jnp.zeros((8, HALF), F32)], axis=1)
                total = total + (wide if a == 0 else pltpu.roll(wide, S - 8 * a, 1))
            flipped = jnp.concatenate([total[7 - i:8 - i] for i in range(8)], axis=0)
            unskew = pltpu.roll(flipped, S - 7, 1, stride=1, stride_axis=0)
            diag[pl.ds(8 * s + h, 1), :] = col_sum(unskew)

        for r in (slice(0, HROWS), slice(HROWS, D)):
            gq = nt(xpT[r, 0:S], qkv[s])
            extra = nt(xpT[r, S:2 * S], qg[s])
            act[s, r, 0:QW] = (gq[:, 0:QW] + extra).astype(BF16)
            act[s, r, QW:3 * QW] = gq[:, QW:3 * QW].astype(BF16)
        after((C1, C2), s)
        place = lax.rem(s, 2) * lax.div(s, 2) + (1 - lax.rem(s, 2)) * (3 + lax.div(s, 2))
        smx[place, 1:2, 0:QW] = (nt(ones, qkv[s, 0:QW]) + nt(ones, qg[s]))[0:1]
        smx[place, 1:2, QW:2 * QW] = nt(ones, qkv[s, 2 * QW:3 * QW])[0:1]
        table = lax.dot_general(
            diag[pl.ds(pl.multiple_of(8 * s, 8), 8), :], onehot, (((1,), (1,)), ((), ())),
            precision=lax.Precision.HIGHEST, preferred_element_type=F32,
        )
        smx[place, 2:5, 0:32] = table[0:3]

        @pl.when(s == 2)
        def _():
            A.middle()

        @pl.when(s == 1)
        def _():
            C2.middle()

    def small_send(k):
        if k == 0:
            return remote(smx.at[0:3], r1, ps.at[0], pr.at[0], core)
        if k == 1:
            return remote(smy, r2, ps.at[1], pr.at[1], xdev)
        if k == 2:
            return remote(smz, r3, ps.at[2], pr.at[2], ydev)
        return remote(smw, r4.at[k - 3], ps.at[k], pr.at[k], zdev[k - 2])

    small_send(0).start()
    A.last()
    for s in range(SLOTS):
        dg[s, 0:S, 0:3 * QW] = nt(unperm[...], qkv[s]).astype(BF16)
        dg[s, S:2 * S, 0:QW] = nt(unperm[...], qg[s]).astype(BF16)
    small_send(0).wait_recv()
    smy[0] = smx[4] + r1[1]
    smy[1] = smx[2] + r1[2]
    small_send(1).start()
    smz[0] = smx[3] + r1[0]
    B.last()
    for s in range(SLOTS):
        acc[0:S] += nn(dg[s, 0:S, 0:3 * QW], wq[s])
        acc[S:2 * S] += nn(dg[s, S:2 * S, 0:QW], wq[s, 0:QW])
    rows_out = [
        pltpu.make_async_copy(acc.at[0:S], gc_hbm, lsem.at[0]),
        pltpu.make_async_copy(acc.at[S:2 * S], gg_hbm, lsem.at[1]),
    ]
    for copy in rows_out:
        copy.start()
    small_send(1).wait_recv()
    smz[0] = smz[0] + r2[0]
    smz[1] = smy[1] + r2[1]
    small_send(2).start()
    C1.middle()
    small_send(2).wait_recv()
    smw[...] = smz[...] + r3[...]
    for k in (3, 4, 5):
        small_send(k).start()
    C2.last()
    C1.last()
    for k in (3, 4, 5):
        small_send(k).wait_recv()
    sm_res[...] = smw[...] + r4[0] + r4[1] + r4[2]
    A.finish(0)
    B.finish(1)
    C2.finish(2)
    C1.finish(2)

    for copy in rows_out:
        copy.wait()
    for p in range(4):
        core_copy(p).wait_send()
    for i in range(len(items)):
        x_copy(i).wait_send()
        y_copy(i).wait_send()
        c_copy(i, False).wait_send()
        c_copy(i, True).wait_send()
    for k in (1, 2, 3):
        small_copy(k).wait_send()
    for k in range(6):
        small_send(k).wait_send()
    A.sent()
    B.sent()
    C1.sent()
    C2.sent()


def layer(stride, dl, rank, pc, x, g, cc, cg, wq, wo, wi, w2, small, vectors):
    vmem = pl.BlockSpec(memory_space=pltpu.VMEM)
    smem = pl.BlockSpec(memory_space=pltpu.SMEM)
    hbm = pl.BlockSpec(memory_space=pl.ANY)
    sd = jax.ShapeDtypeStruct
    vm = pltpu.VMEM
    dma = pltpu.SemaphoreType.DMA
    return pl.pallas_call(
        functools.partial(kernel, stride),
        out_shape=(
            sd((S, D), BF16), sd((S, D), BF16), sd((S, D), F32), sd((S, D), F32),
            sd((SLOTS, 2 * S, D), BF16), sd((3, ROWS, D), F32), sd((2, 8, D), F32),
        ),
        in_specs=[smem, smem, vmem] + [hbm] * 9 + [vmem],
        out_specs=(hbm, hbm, hbm, hbm, hbm, vmem, vmem),
        scratch_shapes=[
            vm((S, S), BF16), vm((S, S), BF16), vm((2 * S, D), BF16), vm((2 * S, D), BF16),
            vm((D, 2 * S), BF16), vm((D, 2 * S), BF16), vm((2 * S, D), BF16),
            vm((SLOTS, 3 * QW, S), BF16), vm((SLOTS, QW, S), BF16), vm((2 * S, D), BF16), vm((2 * S, 1), F32),
            vm((SLOTS, 2 * S, D), BF16), vm((SLOTS, 2 * S, D), BF16), vm((2 * S, D), F32),
            vm((2, HALF, S), BF16), vm((HALF, HALF), F32), vm((32, S), F32),
            vm((SLOTS, 3 * QW, D), BF16), vm((D, D), BF16), vm((SLOTS, D, D), BF16), vm((SLOTS, D, D), BF16),
            vm((SLOTS, 16, D), F32),
            vm((3, D, D), BF16), vm((3, D, D), BF16), vm((2, D, D), BF16), vm((2, D, D), BF16),
            vm((D, D), BF16), vm((2, HROWS, D), BF16),
            vm((5, 8, D), F32), vm((2, 8, D), F32), vm((2, 8, D), F32), vm((2, 8, D), F32),
            vm((3, 8, D), F32), vm((2, 8, D), F32), vm((2, 8, D), F32), vm((3, 2, 8, D), F32),
            dma((11,)), dma((7, 4)), dma((7, 4)), dma((4,)), dma((4,)), dma((3,)), dma((3,)),
            dma((4, 8)), dma((4, 8)), dma((6,)), dma((6,)), pltpu.SemaphoreType.REGULAR((6,)),
        ],
        compiler_params=pltpu.CompilerParams(
            vmem_limit_bytes=int(63.5 * (1 << 20)), collective_id=0, has_side_effects=True
        ),
    )(dl, pc, rank, x, g, cc, cg, wq, wo, wi, w2, small, vectors)


def local(
    stride,
    content, query_stream, cot_content, cot_query, doc_lengths, rank_order, pred_counts, w_qkv, bias_qv,
    w_attn_out, b_attn_out, norm1_gain, norm1_shift, w_in, b_in, w_out, b_out, norm2_gain, norm2_shift, rel_table,
):
    wide = lambda v: jnp.pad(v.astype(F32), ((0, 0), (0, D - v.shape[1])))
    line = lambda v: v.astype(F32).reshape(1, D)
    small = jnp.concatenate([line(b_in), wide(bias_qv), wide(rel_table.T), jnp.zeros((10, D), F32)], axis=0)
    vectors = jnp.concatenate(
        [line(v) for v in (b_attn_out, norm1_gain, norm1_shift, b_out, norm2_gain, norm2_shift)]
        + [jnp.zeros((2, D), F32)],
        axis=0,
    )
    outs = layer(
        stride, doc_lengths, rank_order, pred_counts, content, query_stream, cot_content, cot_query,
        jnp.transpose(w_qkv, (0, 2, 1)).reshape(3 * QW, D), w_attn_out, w_in, w_out, small, vectors,
    )
    out_c, out_g, gc, gg, _, gw, sm = outs
    if stride > 1:
        groups = [list(range(k * stride, k * stride + stride)) for k in range(8)]
        gw = lax.psum_scatter(gw, "dp", scatter_dimension=1, axis_index_groups=groups, tiled=True)
        sm = lax.psum(sm, "dp") / 8.0
    rows = gw.shape[1]
    own, shared = sm[0], sm[1]
    return (
        out_c, out_g, gc, gg,
        jnp.transpose(gw[2, :, 0:3 * QW].reshape(rows, 3, QW), (1, 0, 2)),
        own[1, 0:2 * QW].reshape(2, QW),
        gw[2, :, 3 * QW:].T,
        shared[0], shared[1], shared[2],
        gw[1], own[0], gw[0].T, shared[3], shared[4], shared[5], own[2:5, 0:32].T,
    )


def solution(mesh):
    in_specs = (
        P(("dp", "tensor"), None),
        P(("dp", "tensor"), None),
        P(("dp", "tensor"), None),
        P(("dp", "tensor"), None),
        P("dp", None),
        P("dp", None),
        P("dp"),
        P(None, None, "tensor"),
        P(None, "tensor"),
        P("tensor", None),
        P(),
        P(),
        P(),
        P(None, "tensor"),
        P("tensor"),
        P("tensor", None),
        P(),
        P(),
        P(),
        P(None, "tensor"),
    )
    out_specs = (
        P(("dp", "tensor"), None),
        P(("dp", "tensor"), None),
        P(("dp", "tensor"), None),
        P(("dp", "tensor"), None),
        P(None, "dp", "tensor"),
        P(None, "tensor"),
        P("tensor", "dp"),
        P(),
        P(),
        P(),
        P("dp", "tensor"),
        P("tensor"),
        P("tensor", "dp"),
        P(),
        P(),
        P(),
        P(None, "tensor"),
    )
    stride = mesh.shape["dp"] // 8
    return jax.shard_map(functools.partial(local, stride), mesh=mesh, in_specs=in_specs, out_specs=out_specs, check_vma=False)
```

```python
import functools

import jax
import jax.numpy as jnp
from jax import lax
from jax.experimental import pallas as pl
from jax.experimental.pallas import tpu as pltpu
from jax.sharding import PartitionSpec as P

EDGES = (1, 2, 3, 4, 5, 6, 7, 8, 12, 16, 23, 32, 46, 64, 91)
EPSILON = 1e-05
F32 = jnp.float32
BF16 = jnp.bfloat16
S = 512
HALF = 256
D = 768
HD = 64
SLOTS = 4
SLOT_HEADS = 3
QW = SLOT_HEADS * HD
NEGATIVE = -1e30
ROWS = D // 8
HROWS = D // 2
MESH = pl.DeviceIdType.MESH


def nn(a, b):
    return jnp.dot(a, b, preferred_element_type=F32)


def nt(a, b):
    return lax.dot_general(a, b, (((1,), (1,)), ((), ())), preferred_element_type=F32)


def tn(a, b):
    return lax.dot_general(a, b, (((0,), (0,)), ((), ())), preferred_element_type=F32)


def iota(shape, axis):
    return lax.broadcasted_iota(jnp.int32, shape, axis)


def bucket_onehot():
    lanes = iota((32, S), 1)
    offset = jnp.where(lanes < HALF, -lanes, S - lanes)
    distance = jnp.abs(offset)
    bucket = jnp.where(offset > 0, 16, 0)
    for edge in EDGES:
        bucket = bucket + (distance >= edge).astype(jnp.int32)
    return (bucket == iota((32, S), 0)).astype(F32)


def gelu_pair(v):
    cdf = 0.5 + 0.5 * lax.erf(v * 0.7071067811865476)
    return v * cdf, cdf + v * (jnp.exp(-0.5 * v * v) * 0.3989422804014327)


def row_mean(v):
    return jnp.sum(v, axis=-1, keepdims=True) * (1.0 / D)


def col_sum(v):
    return jnp.sum(v, axis=0, keepdims=True)


def kernel(
    stride,
    dl, pc, rank, x_hbm, g_hbm, cc_hbm, cg_hbm, wq_in, wo_in, wi_in, w2_in,
    b_in, bias_qv, table_in, b_attn_in, n1g_in, n1s_in, b_out_in, n2g_in, n2s_in,
    oc_hbm, og_hbm, gc_hbm, gg_hbm, stash, g_res, sm_res,
    perm, unperm, xin, hid, tA, tB, attn, qkv, qg, xhat, rstd1, act, dg, acc,
    mask, square, lines, wq, wo, wi, w2, wsm, vectors,
    ga, gb, rca, rcb, rza, rya, rxa, rxb, ryb, smx, smy, smz, smw, r1, r2, r3, r4,
    lsem, xs, xr, cs, cr, ss, sr, os, orr, ps, pr, credit,
):
    b_attn, n1g, n1s, b_out, n2g, n2s = (vectors.at[k:k + 1] for k in range(6))
    for k, ref in enumerate((b_attn_in, n1g_in, n1s_in, b_out_in, n2g_in, n2s_in)):
        vectors[k:k + 1] = ref[...].astype(F32).reshape(1, D)
    wsm[0] = jnp.zeros((8, D), F32)
    wsm[0, 0:1] = b_in[...].astype(F32).reshape(1, D)
    wsm[0, 1:3, 0:QW] = bias_qv[...].astype(F32)
    wsm[0, 3:3 + SLOT_HEADS, 0:32] = table_in[...].astype(F32)
    bias = dsacc = square
    text = diag = lines
    t = lax.axis_index("tensor")
    d = lax.axis_index("dp")
    yb = lax.rem(lax.div(d, stride), 2)
    zb = lax.rem(lax.div(d, 2 * stride), 4)
    zbit = lax.rem(zb, 2)
    z_of = (zb, zb + 1 - 2 * zbit, lax.rem(zb + 2, 4), 3 - zb)
    core = (d, t + 1 - 2 * lax.rem(t, 2))
    xdev = (d, lax.rem(t + 2, 4))
    diagonal = (d, 3 - t)
    ydev = (d + stride - 2 * stride * yb, t)
    zdev = [None] + [(d + 2 * stride * (z_of[k] - zb), t) for k in (1, 2, 3)]

    barrier = pltpu.get_barrier_semaphore()
    for who in (core, xdev, diagonal, ydev, zdev[1], zdev[2], zdev[3]):
        pl.semaphore_signal(barrier, inc=1, device_id=who, device_id_type=MESH)
    pl.semaphore_wait(barrier, 7)

    def remote(src, dst, send, recv, who):
        return pltpu.make_async_remote_copy(
            src_ref=src, dst_ref=dst, send_sem=send, recv_sem=recv, device_id=who, device_id_type=MESH
        )

    parts = (
        (wq_in, lambda s, lo, n: wq.at[s, pl.ds(lo, n)], 3 * QW, 2),
        (wo_in, lambda s, lo, n: wo.at[pl.ds(s * QW + lo, n)], QW, 1),
        (wi_in, lambda s, lo, n: wi.at[s, pl.ds(lo, n)], D, 2),
        (w2_in, lambda s, lo, n: w2.at[s, pl.ds(lo, n)], D, 2),
    )
    items = []
    for p, (_, _, n, count) in enumerate(parts):
        for i in range(count):
            items.append((p, n // 2, i * (n // 2 // count), n // 2 // count))

    def mine(i, other):
        p, half, lo, n = items[i]
        return pl.multiple_of((1 - yb if other else yb) * half + lo, 16), n

    def x_copy(i):
        src, place, _, _ = parts[items[i][0]]
        lo, n = mine(i, False)
        return remote(src.at[pl.ds(lo, n)], place(2, lo, n), xs.at[i, 0], xr.at[i, 0], xdev)

    def y_copy(i):
        place = parts[items[i][0]][1]
        lo, n = mine(i, False)
        return remote(place(2, lo, n), place(2, lo, n), xs.at[i, 1], xr.at[i, 1], ydev)

    def c_copy(i, other):
        place = parts[items[i][0]][1]
        lo, n = mine(i, other)
        k = 3 if other else 2
        return remote(place(2, lo, n), place(3, lo, n), xs.at[i, k], xr.at[i, k], core)

    def core_copy(p):
        src, place, n, _ = parts[p]
        return remote(src, place(1, 0, n), cs.at[p], cr.at[p], core)

    def small_copy(k):
        return remote(wsm.at[0], wsm.at[k], ss.at[k - 1], sr.at[k - 1], (core, xdev, diagonal)[k - 1])

    def own_copy(p):
        src, place, n, _ = parts[p]
        return pltpu.make_async_copy(src, place(0, 0, n), lsem.at[2 + p])

    def arrived_x(i):
        x_copy(i).wait_recv()
        y_copy(i).start()
        c_copy(i, False).start()

    def arrived_y(i):
        y_copy(i).wait_recv()
        c_copy(i, True).start()

    def arrived_core(i):
        c_copy(i, False).wait_recv()
        c_copy(i, True).wait_recv()

    def fetch(one, two):
        return [
            pltpu.make_async_copy(one, xin.at[0:S], lsem.at[0]),
            pltpu.make_async_copy(two, xin.at[S:2 * S], lsem.at[1]),
        ]

    def stash_copy(s, back):
        ends = (stash.at[s], dg.at[s]) if back else (dg.at[s], stash.at[s])
        return pltpu.make_async_copy(ends[0], ends[1], lsem.at[7 + s])

    own_copy(0).start()
    rows_in = fetch(x_hbm, g_hbm)
    for copy in rows_in:
        copy.start()
    for k in (1, 2, 3):
        small_copy(k).start()
    core_copy(0).start()
    for i in range(len(items)):
        x_copy(i).start()
    for p in (1, 2, 3):
        core_copy(p).start()
        own_copy(p).start()

    end = jnp.int32(0)
    start = jnp.int32(0)
    ends = []
    for k in range(8):
        length = dl[t, k]
        start = jnp.where(length == HALF, end, start)
        end = end + length
        ends.append(end)
    limit = (S - pc[t]).astype(F32)
    rows = iota((S, 1), 0)
    lanes = iota((1, S), 1)
    source_r = (rows + start) & (S - 1)
    source_l = (lanes + start) & (S - 1)
    perm[...] = jnp.where(source_r == lanes, 1.0, 0.0).astype(BF16)
    unperm[...] = jnp.where(((rows - start) & (S - 1)) == lanes, 1.0, 0.0).astype(BF16)
    doc_r = jnp.zeros((S, 1), F32)
    doc_l = jnp.zeros((1, S), F32)
    for e in ends:
        doc_r = doc_r + jnp.where(source_r >= e, 1.0, 0.0)
        doc_l = doc_l + jnp.where(source_l >= e, 1.0, 0.0)
    rank_row = rank[pl.ds(t, 1), :]
    sub = iota((16, S), 0)
    pieces = jnp.where(sub == 0, rank_row >> 4, jnp.where(sub == 1, rank_row & 15, 0))
    pieces = pieces.astype(F32).astype(BF16)
    ranks = nt(pieces, perm[...])
    rank_l = 16.0 * ranks[0:1] + ranks[1:2]
    ranks = nt(perm[...], pieces)
    rank_r = 16.0 * ranks[:, 0:1] + ranks[:, 1:2]
    lim_c = jnp.maximum(limit - 1.0, rank_l)
    lim_g = jnp.maximum(limit, rank_l) - 1.0
    for b in range(2):
        c = slice(HALF * b, HALF * b + HALF)
        same = doc_r[c] == doc_l[:, c]
        mask[b, :, 0:HALF] = jnp.where(same & (rank_r[c] <= lim_c[:, c]), 0.0, NEGATIVE).astype(BF16)
        mask[b, :, HALF:S] = jnp.where(same & (rank_r[c] <= lim_g[:, c]), 0.0, NEGATIVE).astype(BF16)
    onehot = bucket_onehot()
    smx[...] = jnp.zeros(smx.shape, F32)

    def transposed(dst, src):
        for st in range(2):
            r = slice(st * S, st * S + S)
            dst[:, r] = src[r].T

    def permuted(dst):
        for copy in rows_in:
            copy.wait()
        for st in range(2):
            r = slice(st * S, st * S + S)
            for f in (slice(0, HROWS), slice(HROWS, D)):
                dst[r, f] = nn(perm[...], xin[r, f]).astype(BF16)

    xp = hid
    permuted(xp)
    own_copy(0).wait()

    def prob_at(s, h, b, st):
        k = 2 * b + st
        return dg.at[s, k * HALF:k * HALF + HALF, pl.ds(pl.multiple_of(h * HALF, HALF), HALF)]

    @pl.loop(0, SLOTS)
    def _(s):
        @pl.when(s == 1)
        def _():
            core_copy(0).wait_recv()
            small_copy(1).wait_recv()
            arrived_x(1)

        @pl.when(s == 2)
        def _():
            small_copy(2).wait_recv()
            arrived_y(1)

        @pl.when(s == 3)
        def _():
            small_copy(3).wait_recv()
            arrived_core(0)
            arrived_core(1)

        small = wsm[s].astype(BF16)
        text[pl.ds(pl.multiple_of(8 * s, 8), 8), :] = nn(small[:, 0:32], onehot.astype(BF16))
        sel = jnp.where(iota((8, 128), 0) == 1, 1.0, 0.0).astype(BF16)
        bq = tn(small[:, 0:QW], sel)[:, 0:1]
        sel = jnp.where(iota((8, 128), 0) == 2, 1.0, 0.0).astype(BF16)
        bv = tn(small[:, 0:QW], sel)[:, 0:1]
        r = nt(wq[s], xp[0:S])
        qkv[s, 0:QW] = ((r[0:QW] + bq).astype(BF16) * 0.125).astype(BF16)
        qkv[s, QW:2 * QW] = r[QW:2 * QW].astype(BF16)
        qkv[s, 2 * QW:3 * QW] = (r[2 * QW:3 * QW] + bv).astype(BF16)
        qg[s] = ((nt(wq[s, 0:QW], xp[S:2 * S]) + bq).astype(BF16) * 0.125).astype(BF16)

        @pl.loop(0, SLOT_HEADS)
        def _(h):
            n = SLOT_HEADS * s + h
            pl.when(n == 1)(lambda: arrived_x(0))

            @pl.when(n == 5)
            def _():
                arrived_x(2)
                arrived_y(0)

            @pl.when(n == 8)
            def _():
                arrived_x(3)
                arrived_y(2)

            hr = pl.multiple_of(h * HD, HD)
            rowvec = text[pl.ds(8 * s + 3 + h, 1), :]
            rolled = pltpu.roll(jnp.broadcast_to(rowvec, (HALF, S)), 0, 1, stride=1, stride_axis=0)
            bias[...] = rolled[:, 0:HALF]
            for b in range(2):
                c = slice(HALF * b, HALF * b + HALF)
                kT = qkv[s, pl.ds(QW + hr, HD), c]
                vT = qkv[s, pl.ds(2 * QW + hr, HD), c]
                for st in range(2):
                    qT = qkv[s, pl.ds(hr, HD), c] if st == 0 else qg[s, pl.ds(hr, HD), c]
                    l = slice(HALF * st, HALF * st + HALF)
                    sc = tn(kT, qT) + bias[...] + mask[b, :, l].astype(F32)
                    e = jnp.exp(sc - jnp.max(sc, axis=0, keepdims=True))
                    p = (e * (1.0 / jnp.sum(e, axis=0, keepdims=True))).astype(BF16)
                    prob_at(s, h, b, st)[...] = p
                    to = slice(st * S + HALF * b, st * S + HALF * b + HALF)
                    tA[pl.ds(pl.multiple_of(s * QW + hr, HD), HD), to] = nn(vT, p).astype(BF16)

        for k in range(SLOTS):
            @pl.when(s == k)
            def _():
                stash_copy(k, False).start()

    own_copy(1).wait()
    core_copy(1).wait_recv()
    for st in range(2):
        r = slice(st * S, st * S + S)
        attn[r] = nt(unperm[...], tA[:, r]).astype(BF16)
    arrived_core(2)
    arrived_x(4)
    for r in (slice(k * HALF, k * HALF + HALF) for k in range(4)):
        res = xin[r].astype(F32) + nn(attn[r], wo[...]) + b_attn[...]
        cen = res - row_mean(res)
        rs = lax.rsqrt(row_mean(cen * cen) + EPSILON)
        xh = cen * rs
        xhat[r] = xh.astype(BF16)
        rstd1[r] = rs
        hid[r] = (xh * n1g[...] + n1s[...]).astype(BF16)
    transposed(tB, hid)
    rows_in = fetch(cc_hbm, cg_hbm)
    for copy in rows_in:
        copy.start()

    own_copy(2).wait()
    own_copy(3).wait()

    @pl.loop(0, SLOTS)
    def _(s):
        @pl.when(s == 1)
        def _():
            core_copy(2).wait_recv()
            arrived_y(3)
            arrived_x(5)

        @pl.when(s == 2)
        def _():
            arrived_y(4)

        @pl.when(s == 3)
        def _():
            arrived_x(6)
            arrived_core(3)
            arrived_core(4)

        for k in range(SLOTS):
            @pl.when(s == k)
            def _():
                stash_copy(k, False).wait()
        for st in range(2):
            r = slice(st * S, st * S + S)
            for j in range(0, D, 256):
                pre = nn(hid[r], wi[s, :, j:j + 256]) + wsm[s, 0:1, j:j + 256]
                a, g = gelu_pair(pre)
                act[s, r, j:j + 256] = a.astype(BF16)
                dg[s, r, j:j + 256] = g.astype(BF16)

    for r in (slice(0, S), slice(S, 2 * S)):
        acc[r] = nn(act[0, r], w2[0])

    @pl.loop(1, SLOTS)
    def _(s):
        @pl.when(s == 1)
        def _():
            core_copy(3).wait_recv()
            arrived_y(5)

        @pl.when(s == 2)
        def _():
            arrived_y(6)

        @pl.when(s == 3)
        def _():
            arrived_core(5)
            arrived_core(6)

        for r in (slice(0, S), slice(S, 2 * S)):
            acc[r] += nn(act[s, r], w2[s])

    for copy in rows_in:
        copy.wait()

    @pl.loop(0, 4)
    def _(i):
        r = pl.ds(pl.multiple_of(i * HALF, HALF), HALF)
        res = hid[r, :].astype(F32) + acc[r, :] + b_out[...]
        cen = res - row_mean(res)
        rs = lax.rsqrt(row_mean(cen * cen) + EPSILON)
        xh = cen * rs
        cot = xin[r, :].astype(F32)
        hid[r, :] = (xh * n2g[...] + n2s[...]).astype(BF16)
        dxh = cot * n2g[...]
        dres = rs * (dxh - row_mean(dxh) - xh * row_mean(dxh * xh))
        acc[r, :] = dres
        xin[r, :] = dres.astype(BF16)
        smx[2, 3:4] += col_sum(dres)
        smx[2, 4:5] += col_sum(cot * xh)
        smx[2, 5:6] += col_sum(cot)

    dlow = xin
    transposed(tA, dlow)
    rows_out = [
        pltpu.make_async_copy(hid.at[0:S], oc_hbm, lsem.at[0]),
        pltpu.make_async_copy(hid.at[S:2 * S], og_hbm, lsem.at[1]),
    ]
    for copy in rows_out:
        copy.start()

    def rows_at(lo, n):
        return pl.ds(pl.multiple_of(lo, ROWS), n)

    own_half = rows_at(yb * HROWS, HROWS)
    other_half = rows_at((1 - yb) * HROWS, HROWS)
    zlow, zhigh = zbit, lax.div(zb, 2)
    z_own = rows_at(zlow * HROWS, HROWS)
    z_other = rows_at((1 - zlow) * HROWS, HROWS)
    zy_own = rows_at(zlow * HROWS + yb * 2 * ROWS, 2 * ROWS)
    zy_other = rows_at(zlow * HROWS + (1 - yb) * 2 * ROWS, 2 * ROWS)
    zyz_own = rows_at(zlow * HROWS + yb * 2 * ROWS + zhigh * ROWS, ROWS)
    zyz_other = rows_at(zlow * HROWS + yb * 2 * ROWS + (1 - zhigh) * ROWS, ROWS)

    def block(k):
        return rows_at(yb * HROWS + z_of[k] * ROWS, ROWS)

    def store(dst, lead, lo, half_index, value, z_first):
        for b in range(4):
            y, z = (4 * half_index + b) % 2, (4 * half_index + b) // 2
            to = ((z % 2) * 4 + y * 2 + z // 2 if z_first else y * 4 + z) * ROWS
            dst[lead, to:to + ROWS, lo:lo + value.shape[1]] = value[b * ROWS:b * ROWS + ROWS, :]

    def add(dst, at, *sources):
        base = 0 if at is None else at.start
        count = dst.shape[0] if at is None else at.size

        @pl.loop(0, count // ROWS)
        def _(i):
            step = pl.multiple_of(i * ROWS, ROWS)
            a = pl.ds(pl.multiple_of(base + step, ROWS), ROWS)
            total = dst[a, :].astype(F32)
            for src in sources:
                total = total + src[pl.ds(step, ROWS), :].astype(F32)
            dst[a, :] = total.astype(BF16)

    class Chunk:
        def __init__(self, index, even, odd, rc, parts, out):
            self.n, self.even, self.odd, self.rc, self.out = index, even, odd, rc, out
            self.moves = {}
            for k, (name, src, dst, who) in enumerate(parts):
                self.moves[name] = (src, dst, k + 2, who)

        def core_send(self, k):
            return remote(self.odd[k], self.rc[k], os.at[self.n, k], orr.at[self.n, k], core)

        def move(self, name):
            src, dst, k, who = self.moves[name]
            return remote(src, dst, os.at[self.n, k], orr.at[self.n, k], who)

        def go(self, *names):
            for name in names:
                self.move(name).start()

        def here(self, *names):
            for name in names:
                self.move(name).wait_recv()
            return [self.moves[name][1] for name in names]

        def core_sum(self, k):
            self.core_send(k).wait_recv()
            add(self.even[k], None, self.rc[k])

        def finish(self, at, *names):
            total = self.even[0][at, :].astype(F32)
            for ref in self.here(*names):
                total = total + ref[...].astype(F32)
            which, cols = self.out
            g_res[which, :, cols] = total

        def sent(self):
            for k in (0, 1) if self.n > 3 else (0,):
                self.core_send(k).wait_send()
            for name in self.moves:
                self.move(name).wait_send()

    whole, first, second = pl.ds(0, D), pl.ds(0, D // 2), pl.ds(D // 2, D // 2)

    def x_flow(index, even, odd, rc, rx, ry, rz, out):
        e0, e2 = even
        parts = [("x", e2, rx, xdev), ("y", e0.at[other_half], ry, ydev)]
        parts += [("z%d" % k, e0.at[block(k)], rz(k), zdev[k]) for k in (1, 2, 3)]
        return Chunk(index, even, odd, rc, parts, out)

    def y_flow(index, even, odd, rc, rx, ry, rz, out):
        e0, e2 = even
        parts = [
            ("y2", e2.at[other_half], ry[1], ydev), ("y0", e0.at[other_half], ry[0], ydev),
            ("x", e2.at[own_half], rx, xdev),
        ]
        parts += [("z%d" % k, e0.at[block(k)], rz(k), zdev[k]) for k in (1, 2, 3)]
        return Chunk(index, even, odd, rc, parts, out)

    def dead(slot, lo, n, cols):
        return w2.at[slot, lo:lo + n, cols]

    def z_flow(index, even, odd, rc, rz, ry, rx, rh, out):
        e0, e2 = even
        parts = [
            ("l2", e2.at[z_other], rz[1], zdev[1]), ("l0", e0.at[z_other], rz[0], zdev[1]),
            ("y2", e2.at[zy_other], ry[1], ydev), ("y0", e0.at[zy_other], ry[0], ydev),
            ("x", e2.at[zy_own], rx, xdev), ("h", e0.at[zyz_other], rh, zdev[2]),
        ]
        return Chunk(index, even, odd, rc, parts, out)

    def in_wi(slot, cols):
        return lambda k: wi.at[slot, (k - 1) * ROWS:k * ROWS, cols]

    def ab_even(g, cols):
        return (g.at[0, :, cols], g.at[1, :, cols]), (g.at[2, :, cols], g.at[2, :, cols])

    def c_even(cols):
        return (act.at[0, 0:D, cols], act.at[2, 0:D, cols]), (act.at[1, 0:D, cols], act.at[3, 0:D, cols])

    def pair(ref, cols):
        return ref.at[0, :, cols], ref.at[1, :, cols]

    A1 = z_flow(
        0, *ab_even(ga, first), pair(rca, first), (rza.at[0], rza.at[1]),
        (dead(0, 0, 2 * ROWS, first), rya), dead(0, 2 * ROWS, 2 * ROWS, first), dead(0, 4 * ROWS, ROWS, first),
        (0, first),
    )
    A2 = x_flow(
        1, *ab_even(ga, second), pair(rca, second), rxa, dead(0, 0, HROWS, second), in_wi(0, second), (0, second),
    )
    B1 = y_flow(
        2, *ab_even(gb, first), pair(rcb, first), dead(1, 0, HROWS, first),
        (ryb.at[0], ryb.at[1]), in_wi(0, first), (1, first),
    )
    B2 = x_flow(
        3, *ab_even(gb, second), pair(rcb, second), rxb, dead(1, 0, HROWS, second), in_wi(1, second), (1, second),
    )
    Ca = z_flow(
        4, *c_even(first), pair(rca, first),
        (dead(3, 0, HROWS, first), dead(3, HROWS, HROWS, first)),
        (dead(0, 5 * ROWS, 2 * ROWS, first), dead(1, HROWS, 2 * ROWS, first)),
        dead(1, HROWS + 2 * ROWS, 2 * ROWS, first), dead(0, 7 * ROWS, ROWS, first), (2, first),
    )
    Cb = y_flow(
        5, *c_even(second), pair(rca, second), dead(1, HROWS, HROWS, second),
        (dead(3, 0, HROWS, second), dead(3, HROWS, HROWS, second)), in_wi(3, second), (2, second),
    )

    def buffer_of(s):
        odd = lax.rem(s, 2)
        return 2 * odd + (1 - odd) * lax.div(s, 2)

    def after(s, three, two, one, zero):
        for k, step in ((3, three), (2, two), (1, one), (0, zero)):
            pl.when(s == k)(step)

    @pl.loop(0, SLOTS)
    def _(i):
        s = 3 - i

        @pl.when(s == 1)
        def _():
            A1.core_send(1).wait_send()
            A2.core_send(1).wait_send()

        for k in range(2):
            value = nn(tA[k * HROWS:k * HROWS + HROWS], act[s]).astype(BF16)
            store(ga, buffer_of(s), 0, k, value[:, 0:D // 2], True)
            store(ga, buffer_of(s), D // 2, k, value[:, D // 2:], False)

        def three():
            A1.core_send(1).start()
            A2.core_send(1).start()

        def two():
            A1.core_sum(1)
            A1.go("l2")
            A2.core_sum(1)
            A2.go("x")

        def one():
            A1.core_send(0).start()
            A2.core_send(0).start()

        def zero():
            A1.core_sum(0)
            A1.go("l0")
            A2.core_sum(0)

        after(s, three, two, one, zero)

    @pl.loop(0, SLOTS)
    def _(i):
        s = 3 - i
        place = lax.rem(s, 2) * lax.div(s, 2) + (1 - lax.rem(s, 2)) * (3 + lax.div(s, 2))
        for j in range(0, D, 256):
            part = jnp.zeros((1, 256), F32)
            for st in range(2):
                r = slice(st * S, st * S + S)
                dact = nt(dlow[r], w2[s, j:j + 256, :])
                low = (dact * dg[s, r, j:j + 256].astype(F32)).astype(BF16)
                dg[s, r, j:j + 256] = low
                part = part + col_sum(low.astype(F32))
            smx[place, 0:1, j:j + 256] = part

        @pl.when(s == 1)
        def _():
            B1.core_send(1).wait_send()
            B2.core_send(1).wait_send()

        for k in range(2):
            value = nn(tB[k * HROWS:k * HROWS + HROWS], dg[s]).astype(BF16)
            store(gb, buffer_of(s), 0, k, value, False)

        def three():
            B1.core_send(1).start()
            B2.core_send(1).start()

        def two():
            B1.core_sum(1)
            B1.go("y2")
            B2.core_sum(1)
            B2.go("x")
            add(ga.at[1, :, first], z_own, *A1.here("l2"))
            A1.go("y2")

        def one():
            B1.core_send(0).start()
            B2.core_send(0).start()

        def zero():
            B1.core_sum(0)
            B1.go("y0")
            B2.core_sum(0)

        after(s, three, two, one, zero)
        for r in (slice(0, S), slice(S, 2 * S)):
            acc[r] += nt(dg[s, r], wi[s])
        for k in range(SLOTS):
            @pl.when(s == k)
            def _():
                stash_copy(k, True).start()

    for k, who in enumerate((core, xdev, ydev, zdev[1], zdev[2], zdev[3])):
        pl.semaphore_signal(credit.at[k], inc=1, device_id=who, device_id_type=MESH)

    @pl.loop(0, 4)
    def _(i):
        r = pl.ds(pl.multiple_of(i * HALF, HALF), HALF)
        dy = acc[r, :]
        xh = xhat[r, :].astype(F32)
        dxh = dy * n1g[...]
        dres = rstd1[r, :] * (dxh - row_mean(dxh) - xh * row_mean(dxh * xh))
        acc[r, :] = dres
        xin[r, :] = dres.astype(BF16)
        smx[2, 0:1] += col_sum(dres)
        smx[2, 1:2] += col_sum(dy * xh)
        smx[2, 2:3] += col_sum(dy)

    transposed(tB, dlow)
    for r in (slice(0, HROWS), slice(HROWS, D)):
        tA[r] = nt(wo[r], dlow[...]).astype(BF16)
    for copy in rows_out:
        copy.wait()
    rows_in = fetch(x_hbm, g_hbm)
    for copy in rows_in:
        copy.start()
    for k in range(6):
        pl.semaphore_wait(credit.at[k], 1)
    add(ga.at[0, :, second], None, *A2.here("x"))
    A2.go("y")
    add(ga.at[1, :, first], zy_own, *A1.here("y2"))
    A1.go("x")
    add(ga.at[0, :, first], z_own, *A1.here("l0"))
    A1.go("y0")
    add(gb.at[1, :, first], own_half, *B1.here("y2"))
    B1.go("x")
    for k in range(2):
        gwo = nn(tB[k * HROWS:k * HROWS + HROWS], attn[...]).astype(BF16)
        for s in range(SLOTS):
            store(act, s, 0, k, gwo[:, s * QW:s * QW + QW], True)
    for st in range(2):
        r = slice(st * S, st * S + S)
        for f in (slice(0, HROWS), slice(HROWS, D)):
            tA[f, r] = nt(tA[f, r], perm[...]).astype(BF16)
    permuted(attn)
    transposed(tB, attn)
    xpT = tB

    ones = jnp.ones((16, S), BF16)
    def head_backward(s, h):
        hr = h * HD if isinstance(h, int) else pl.multiple_of(h * HD, HD)
        for b in range(2):
            c = slice(HALF * b, HALF * b + HALF)
            kT = qkv[s, pl.ds(QW + hr, HD), c]
            vT = qkv[s, pl.ds(2 * QW + hr, HD), c]
            dk = dv = None
            for st in range(2):
                qT = qkv[s, pl.ds(hr, HD), c] if st == 0 else qg[s, pl.ds(hr, HD), c]
                dOT = tA[pl.ds(pl.multiple_of(s * QW + hr, HD), HD), st * S + HALF * b:st * S + HALF * b + HALF]
                p = prob_at(s, h, b, st)[...]
                pf = p.astype(F32)
                dp = tn(vT, dOT)
                dsl = (pf * (dp - jnp.sum(dp * pf, axis=0, keepdims=True))).astype(BF16)
                if b == 0 and st == 0:
                    dsacc[...] = dsl.astype(F32)
                else:
                    dsacc[...] += dsl.astype(F32)
                dq = (nn(kT, dsl) * 0.125).astype(BF16)
                dk1 = nt(qT, dsl)
                dv1 = nt(dOT, p)
                dk = dk1 if dk is None else dk + dk1
                dv = dv1 if dv is None else dv + dv1
                if st == 0:
                    qkv[s, pl.ds(hr, HD), c] = dq
                else:
                    qg[s, pl.ds(hr, HD), c] = dq
            qkv[s, pl.ds(QW + hr, HD), c] = dk.astype(BF16)
            qkv[s, pl.ds(2 * QW + hr, HD), c] = dv.astype(BF16)
        total = jnp.zeros((8, S), F32)
        for a in range(HALF // 8):
            wide = jnp.concatenate([dsacc[8 * a:8 * a + 8, :], jnp.zeros((8, HALF), F32)], axis=1)
            total = total + (wide if a == 0 else pltpu.roll(wide, S - 8 * a, 1))
        flipped = jnp.concatenate([total[7 - i:8 - i] for i in range(8)], axis=0)
        unskew = pltpu.roll(flipped, S - 7, 1, stride=1, stride_axis=0)
        diag[pl.ds(8 * s + h, 1), :] = col_sum(unskew)

    @pl.loop(0, SLOTS)
    def _(i):
        s = 3 - i
        for k in range(SLOTS):
            @pl.when(s == k)
            def _():
                stash_copy(k, True).wait()
        head_backward(s, 0)
        dqkv = jnp.concatenate([qkv[s, k * QW:k * QW + HD] for k in range(3)], axis=0)
        for k in range(2):
            r = slice(k * HROWS, k * HROWS + HROWS)
            gq = nt(xpT[r, 0:S], dqkv)
            extra = nt(xpT[r, S:2 * S], qg[s, 0:HD])
            store(act, s, QW, k, (gq[:, 0:HD] + extra).astype(BF16), True)
            store(act, s, QW + HD, k, gq[:, HD:QW].astype(BF16), True)

        def three():
            Ca.core_send(1).start()

        def two():
            Ca.core_sum(1)
            Ca.go("l2")
            add(gb.at[0, :, second], None, *B2.here("x"))
            B2.go("y")

        def one():
            Ca.core_send(0).start()

        def zero():
            Ca.core_sum(0)
            Ca.go("l0")
            add(ga.at[0, :, second], own_half, *A2.here("y"))
            A2.go("z1", "z2", "z3")

        after(s, three, two, one, zero)

    @pl.loop(0, SLOTS)
    def _(i):
        s = 3 - i

        @pl.loop(1, SLOT_HEADS)
        def _(h):
            head_backward(s, h)

        dqkv = jnp.concatenate([qkv[s, k * QW + HD:k * QW + QW] for k in range(3)], axis=0)
        for k in range(2):
            r = slice(k * HROWS, k * HROWS + HROWS)
            gq = nt(xpT[r, 0:S], dqkv)
            extra = nt(xpT[r, S:2 * S], qg[s, HD:QW])
            store(act, s, 2 * QW, k, (gq[:, 0:2 * HD] + extra).astype(BF16), False)
            store(act, s, 2 * QW + 2 * HD, k, gq[:, 2 * HD:].astype(BF16), False)

        place = lax.rem(s, 2) * lax.div(s, 2) + (1 - lax.rem(s, 2)) * (3 + lax.div(s, 2))
        smx[place, 1:2, 0:QW] = (nt(ones, qkv[s, 0:QW]) + nt(ones, qg[s]))[0:1]
        smx[place, 1:2, QW:2 * QW] = nt(ones, qkv[s, 2 * QW:3 * QW])[0:1]
        table = lax.dot_general(
            diag[pl.ds(pl.multiple_of(8 * s, 8), 8), :], onehot, (((1,), (1,)), ((), ())),
            precision=lax.Precision.HIGHEST, preferred_element_type=F32,
        )
        smx[place, 2:5, 0:32] = table[0:3]

        def three():
            Cb.core_send(1).start()
            add(ga.at[0, :, first], zy_own, *A1.here("y0", "x"))
            A1.go("h")
            add(gb.at[0, :, first], own_half, *B1.here("y0", "x"))
            B1.go("z1", "z2", "z3")
            add(act.at[2, 0:D, first], z_own, *Ca.here("l2"))
            Ca.go("y2")

        def two():
            Cb.core_sum(1)
            Cb.go("y2")
            add(gb.at[0, :, second], own_half, *B2.here("y"))
            B2.go("z1", "z2", "z3")
            add(act.at[0, 0:D, first], z_own, *Ca.here("l0"))
            Ca.go("y0")
            add(act.at[2, 0:D, first], zy_own, *Ca.here("y2"))
            Ca.go("x")

        def one():
            Cb.core_send(0).start()
            A2.finish(block(0), "z1", "z2", "z3")
            A1.finish(zyz_own, "h")

        def zero():
            Cb.core_sum(0)
            Cb.go("y0")
            add(act.at[2, 0:D, second], own_half, *Cb.here("y2"))
            Cb.go("x")
            add(act.at[0, 0:D, first], zy_own, *Ca.here("y0", "x"))
            Ca.go("h")

        after(s, three, two, one, zero)

    def small_send(k):
        if k == 0:
            return remote(smx.at[0:3], r1, ps.at[0], pr.at[0], core)
        if k == 1:
            return remote(smy, r2, ps.at[1], pr.at[1], xdev)
        if k == 2:
            return remote(smz, r3, ps.at[2], pr.at[2], ydev)
        return remote(smw, r4.at[k - 3], ps.at[k], pr.at[k], zdev[k - 2])

    small_send(0).start()
    for s in range(SLOTS):
        dg[s, 0:S, 0:3 * QW] = nt(unperm[...], qkv[s]).astype(BF16)
        dg[s, S:2 * S, 0:QW] = nt(unperm[...], qg[s]).astype(BF16)
    small_send(0).wait_recv()
    smy[0] = smx[4] + r1[1]
    smy[1] = smx[2] + r1[2]
    small_send(1).start()
    smz[0] = smx[3] + r1[0]
    B1.finish(block(0), "z1", "z2", "z3")
    B2.finish(block(0), "z1", "z2", "z3")
    for s in range(2):
        acc[0:S] += nn(dg[s, 0:S, 0:3 * QW], wq[s])
        acc[S:2 * S] += nn(dg[s, S:2 * S, 0:QW], wq[s, 0:QW])
    small_send(1).wait_recv()
    smz[0] = smz[0] + r2[0]
    smz[1] = smy[1] + r2[1]
    small_send(2).start()
    add(act.at[0, 0:D, second], own_half, *Cb.here("y0", "x"))
    Cb.go("z1", "z2", "z3")
    for s in range(2, SLOTS):
        acc[0:S] += nn(dg[s, 0:S, 0:3 * QW], wq[s])
        acc[S:2 * S] += nn(dg[s, S:2 * S, 0:QW], wq[s, 0:QW])
    rows_out = [
        pltpu.make_async_copy(acc.at[0:S], gc_hbm, lsem.at[0]),
        pltpu.make_async_copy(acc.at[S:2 * S], gg_hbm, lsem.at[1]),
    ]
    for copy in rows_out:
        copy.start()
    small_send(2).wait_recv()
    smw[...] = smz[...] + r3[...]
    for k in (3, 4, 5):
        small_send(k).start()
    Ca.finish(zyz_own, "h")
    for k in (3, 4, 5):
        small_send(k).wait_recv()
    sm_res[...] = smw[...] + r4[0] + r4[1] + r4[2]
    Cb.finish(block(0), "z1", "z2", "z3")

    for copy in rows_out:
        copy.wait()
    for p in range(4):
        core_copy(p).wait_send()
    for i in range(len(items)):
        x_copy(i).wait_send()
        y_copy(i).wait_send()
        c_copy(i, False).wait_send()
        c_copy(i, True).wait_send()
    for k in (1, 2, 3):
        small_copy(k).wait_send()
    for k in range(6):
        small_send(k).wait_send()
    for chunk in (A1, A2, B1, B2, Ca, Cb):
        chunk.sent()


def layer(stride, *args):
    vmem = pl.BlockSpec(memory_space=pltpu.VMEM)
    smem = pl.BlockSpec(memory_space=pltpu.SMEM)
    hbm = pl.BlockSpec(memory_space=pl.ANY)
    sd = jax.ShapeDtypeStruct
    vm = pltpu.VMEM
    dma = pltpu.SemaphoreType.DMA
    return pl.pallas_call(
        functools.partial(kernel, stride),
        out_shape=(
            sd((S, D), BF16), sd((S, D), BF16), sd((S, D), F32), sd((S, D), F32),
            sd((SLOTS, 2 * S, D), BF16), sd((3, ROWS, D), F32), sd((2, 8, D), F32),
        ),
        in_specs=[smem, smem, vmem] + [hbm] * 8 + [vmem] * 9,
        out_specs=(hbm, hbm, hbm, hbm, hbm, vmem, vmem),
        scratch_shapes=[
            vm((S, S), BF16), vm((S, S), BF16), vm((2 * S, D), BF16), vm((2 * S, D), BF16),
            vm((D, 2 * S), BF16), vm((D, 2 * S), BF16), vm((2 * S, D), BF16),
            vm((SLOTS, 3 * QW, S), BF16), vm((SLOTS, QW, S), BF16), vm((2 * S, D), BF16), vm((2 * S, 1), F32),
            vm((SLOTS, 2 * S, D), BF16), vm((SLOTS, 2 * S, D), BF16), vm((2 * S, D), F32),
            vm((2, HALF, S), BF16), vm((HALF, HALF), F32), vm((32, S), F32),
            vm((SLOTS, 3 * QW, D), BF16), vm((D, D), BF16), vm((SLOTS, D, D), BF16), vm((SLOTS, D, D), BF16),
            vm((SLOTS, 8, D), F32), vm((8, D), F32),
            vm((3, D, D), BF16), vm((3, D, D), BF16), vm((2, D, D), BF16), vm((2, D, D), BF16),
            vm((2, HROWS, D // 2), BF16), vm((2 * ROWS, D // 2), BF16), vm((D, D // 2), BF16), vm((D, D // 2), BF16),
            vm((2, HROWS, D // 2), BF16),
            vm((5, 8, D), F32), vm((2, 8, D), F32), vm((2, 8, D), F32), vm((2, 8, D), F32),
            vm((3, 8, D), F32), vm((2, 8, D), F32), vm((2, 8, D), F32), vm((3, 2, 8, D), F32),
            dma((11,)), dma((7, 4)), dma((7, 4)), dma((4,)), dma((4,)), dma((3,)), dma((3,)),
            dma((6, 8)), dma((6, 8)), dma((6,)), dma((6,)), pltpu.SemaphoreType.REGULAR((6,)),
        ],
        compiler_params=pltpu.CompilerParams(
            vmem_limit_bytes=int(63.5 * (1 << 20)), collective_id=0, has_side_effects=True
        ),
    )(*args)


def hand_out(
    oc_in, og_in, gc_in, gg_in, gw, sm,
    oc, og, gc, gg, g_qkv, g_bias, g_attn, b_attn, n1g, n1s, g_in, b_in, g_out, b_out, n2g, n2s, g_table,
    wide, narrow, sems,
):
    ways = ((gc_in, wide.at[0], gc), (gg_in, wide.at[1], gg), (oc_in, narrow.at[0], oc), (og_in, narrow.at[1], og))
    arrivals = [pltpu.make_async_copy(src, via, sems.at[0, k]) for k, (src, via, _) in enumerate(ways)]
    copies = [pltpu.make_async_copy(via, dst, sems.at[1, k]) for k, (_, via, dst) in enumerate(ways)]
    for copy in arrivals:
        copy.start()
    g_out[...] = gw[0]
    g_in[...] = gw[1]
    g_attn[...] = gw[2, :, 0:QW].T
    for k in range(3):
        g_qkv[k, :, 0:HD] = gw[2, :, QW + HD * k:QW + HD * k + HD]
        g_qkv[k, :, HD:QW] = gw[2, :, 2 * (QW + HD * k):2 * (QW + HD * k) + 2 * HD]
    for arrival, copy in zip(arrivals, copies):
        arrival.wait()
        copy.start()
    b_in[...] = sm[0, 0:1].reshape(D)
    g_bias[0:1] = sm[0, 1:2, 0:QW]
    g_bias[1:2] = sm[0, 1:2, QW:2 * QW]
    g_table[...] = sm[0, 2:2 + SLOT_HEADS, 0:32]
    for k, ref in enumerate((b_attn, n1g, n1s, b_out, n2g, n2s)):
        ref[...] = sm[1, k:k + 1].reshape(D)
    for copy in copies:
        copy.wait()


def local(
    stride,
    content, query_stream, cot_content, cot_query, doc_lengths, rank_order, pred_counts, w_qkv, bias_qv,
    w_attn_out, b_attn_out, norm1_gain, norm1_shift, w_in, b_in, w_out, b_out, norm2_gain, norm2_shift, rel_table,
):
    out_c, out_g, gc, gg, _, gw, sm = layer(
        stride, doc_lengths, pred_counts, rank_order, content, query_stream, cot_content, cot_query,
        jnp.transpose(w_qkv, (0, 2, 1)).reshape(3 * QW, D), w_attn_out, w_in, w_out,
        b_in, bias_qv, rel_table.T, b_attn_out, norm1_gain, norm1_shift, b_out, norm2_gain, norm2_shift,
    )
    if stride > 1:
        groups = [list(range(k * stride, k * stride + stride)) for k in range(8)]
        gw = lax.psum_scatter(gw, "dp", scatter_dimension=1, axis_index_groups=groups, tiled=True)
        sm = lax.psum(sm, "dp") / 8.0
    rows = gw.shape[1]
    sd = jax.ShapeDtypeStruct
    vmem = pl.BlockSpec(memory_space=pltpu.VMEM)
    hbm = pl.BlockSpec(memory_space=pl.ANY)
    line = sd((D,), F32)
    outs = pl.pallas_call(
        hand_out,
        out_shape=(
            sd((S, D), BF16), sd((S, D), BF16), sd((S, D), F32), sd((S, D), F32),
            sd((3, rows, QW), F32), sd((2, QW), F32), sd((QW, rows), F32), line, line, line,
            sd((rows, D), F32), line, sd((rows, D), F32), line, line, line, sd((SLOT_HEADS, 32), F32),
        ),
        in_specs=[hbm] * 4 + [vmem] * 2,
        out_specs=[hbm] * 4 + [vmem] * 13,
        scratch_shapes=[
            pltpu.VMEM((2, S, D), F32), pltpu.VMEM((2, S, D), BF16), pltpu.SemaphoreType.DMA((2, 4)),
        ],
        compiler_params=pltpu.CompilerParams(vmem_limit_bytes=int(63.5 * (1 << 20))),
    )(out_c, out_g, gc, gg, gw, sm)
    outs = list(outs)
    outs[12] = outs[12].T
    outs[16] = outs[16].T
    return tuple(outs)


def solution(mesh):
    in_specs = (
        P(("dp", "tensor"), None),
        P(("dp", "tensor"), None),
        P(("dp", "tensor"), None),
        P(("dp", "tensor"), None),
        P("dp", None),
        P("dp", None),
        P("dp"),
        P(None, None, "tensor"),
        P(None, "tensor"),
        P("tensor", None),
        P(),
        P(),
        P(),
        P(None, "tensor"),
        P("tensor"),
        P("tensor", None),
        P(),
        P(),
        P(),
        P(None, "tensor"),
    )
    out_specs = (
        P(("dp", "tensor"), None),
        P(("dp", "tensor"), None),
        P(("dp", "tensor"), None),
        P(("dp", "tensor"), None),
        P(None, "dp", "tensor"),
        P(None, "tensor"),
        P("tensor", "dp"),
        P(),
        P(),
        P(),
        P("dp", "tensor"),
        P("tensor"),
        P("tensor", "dp"),
        P(),
        P(),
        P(),
        P(None, "tensor"),
    )
    stride = mesh.shape["dp"] // 8
    return jax.shard_map(functools.partial(local, stride), mesh=mesh, in_specs=in_specs, out_specs=out_specs, check_vma=False)
```

```python
import functools

import jax
import jax.numpy as jnp
from jax import lax
from jax.experimental import pallas as pl
from jax.experimental.pallas import tpu as pltpu
from jax.sharding import PartitionSpec as P

EDGES = (1, 2, 3, 4, 5, 6, 7, 8, 12, 16, 23, 32, 46, 64, 91)
EPSILON = 1e-05
F32 = jnp.float32
BF16 = jnp.bfloat16
S = 512
HALF = 256
D = 768
HD = 64
SLOTS = 4
SLOT_HEADS = 3
QW = SLOT_HEADS * HD
NEGATIVE = -1e30
ROWS = D // 8
HROWS = D // 2
MESH = pl.DeviceIdType.MESH
ITEMS = (
    (0, 0, 64, 0, 32),
    (0, 64, 80, 0, 48),
    (1, 0, 48, 16, 16),
    (2, 0, 96, 32, 32),
    (2, 96, 96, 32, 32),
    (3, 0, 96, 32, 32),
    (3, 96, 96, 64, 16),
)
FORWARD = {
    "p0": (("s", 0), ("K", 3),),
    "p1": (("s", 1), ("x", 0), ("s", 2),),
    "a00": (("K", 2), ("s", 3), ("x", 1),),
    "a01": (("m", 0),),
    "a02": (("x", 2), ("s", 4), ("K", 0), ("m", 1),),
    "a10": (("l", 0), ("k", 0),),
    "a11": (("s", 6), ("x", 3), ("K", 1),),
    "a20": (("k", 1), ("m", 2), ("l", 1),),
    "a22": (("c", 0),),
    "a30": (("c", 1), ("x", 4),),
    "a31": (("l", 2),),
    "a32": (("c", 2), ("s", 5),),
    "o1": (("m", 3), ("x", 6),),
    "f00": (("m", 4), ("k", 2),),
    "f10": (("x", 5),),
    "f20": (("l", 4), ("l", 3), ("m", 6),),
    "f30": (("c", 4), ("c", 3),),
    "f32": (("m", 5),),
    "g0": (("l", 6), ("k", 3),),
    "g1": (("c", 6),),
    "g2": (("l", 5),),
    "g3": (("c", 5),),
}
KINDS = "xyzxyzyxyzxy"
BACKWARD = {
    "gb3c": (("A1", "YA"),),
    "gb2a": (("A2", "ZA2"),),
    "gb2b": (("A0", "XA"),),
    "gb1a": (("A2", "ZA0"),),
    "tr": (("A0", "XL"), ("A2", "ZM"), ("B0", "XA"),),
    "do": (("B2", "ZA2"), ("B1", "YA"), ("A1", "YF"), ("A2", "ZF"),),
    "xt": (("B0", "XL"),),
    "p3c": (("B2", "ZM"),),
    "p1c": (("B1", "YF"), ("A0", "FN"),),
    "p0a": (("W", "YA"), ("B2", "ZA0"),),
    "p0c": (("C2", "ZA2"),),
    "q3b": (("C0", "XA"), ("C1", "YA"),),
    "q2a": (("B2", "ZF"),),
    "q2b": (("C2", "ZM"),),
    "q1a": (("W", "YF"),),
    "q1b": (("B1", "FN"), ("B0", "FN"),),
    "q0b": (("C1", "YF"), ("C0", "XL"), ("C2", "ZA0"),),
    "t0": (("D1", "YA"),),
    "t3": (("D0", "XA"), ("B2", "FN"),),
    "t4": (("C2", "ZF"), ("A1", "FN"), ("D1", "YF"),),
    "t5": (("A2", "FN"),),
    "t6": (("D0", "XL"), ("C0", "FN"),),
    "t7": (("C2", "FN"), ("C1", "FN"),),
    "t9": (("D1", "FN"), ("W", "FN"), ("D0", "FN"),),
}


def nn(a, b):
    return jnp.dot(a, b, preferred_element_type=F32)


def nt(a, b):
    return lax.dot_general(a, b, (((1,), (1,)), ((), ())), preferred_element_type=F32)


def tn(a, b):
    return lax.dot_general(a, b, (((0,), (0,)), ((), ())), preferred_element_type=F32)


def iota(shape, axis):
    return lax.broadcasted_iota(jnp.int32, shape, axis)


def bucket_onehot():
    lanes = iota((32, S), 1)
    offset = jnp.where(lanes < HALF, -lanes, S - lanes)
    distance = jnp.abs(offset)
    bucket = jnp.where(offset > 0, 16, 0)
    for edge in EDGES:
        bucket = bucket + (distance >= edge).astype(jnp.int32)
    return (bucket == iota((32, S), 0)).astype(F32)


def gelu_pair(v):
    w = v * 0.7071067811865476
    cdf = 0.5 + 0.5 * lax.erf(w)
    return v * cdf, cdf + w * jnp.exp2(w * w * -1.4426950408889634) * 0.5641895835477563


def row_mean(v):
    return jnp.sum(v, axis=-1, keepdims=True) * (1.0 / D)


def col_sum(v):
    return jnp.sum(v, axis=0, keepdims=True)


def kernel(
    stride,
    dl, pc, x_hbm, g_hbm, cc_hbm, cg_hbm, wq_in, wo_in, wi_in, w2_in, rank_hbm,
    b_in_hbm, bias_hbm, table_hbm, b_attn_hbm, n1g_hbm, n1s_hbm, b_out_hbm, n2g_hbm, n2s_hbm,
    oc_hbm, og_hbm, gc_hbm, gg_hbm, stash, g_out, gw_out, sm_out,
    perm, unperm, xin, hid, tA, tB, attn, qkv, qg, xhat, rstd1, act, dg, acc,
    mask, lines, wq, wo, wi, w2, wsm, vectors,
    ga, gb, rca, rcb, first_in, second_a, shared, early, e_core, e_part, e_x, e_y, e_sum, e_z, late_x, l_core, l_part, l_x, l_y, l_sum, l_z,
    rank, b_in, bias_qv, table_in, b_attn_in, n1g_in, n1s_in, b_out_in, n2g_in, n2s_in, g_res, g_w, sm_res, osem, isem,
    lsem, xs, xr, cs, cr, ss, sr, os, orr, ps, pr, credit,
):
    b_attn, n1g, n1s, b_out, n2g, n2s = (vectors.at[k:k + 1] for k in range(6))
    text = diag = lines
    t = lax.axis_index("tensor")
    d = lax.axis_index("dp")
    yb = lax.rem(lax.div(d, stride), 2)
    zb = lax.rem(lax.div(d, 2 * stride), 4)
    zbit = lax.rem(zb, 2)
    z_of = (zb, zb + 1 - 2 * zbit, lax.rem(zb + 2, 4), 3 - zb)
    core = (d, t + 1 - 2 * lax.rem(t, 2))
    xdev = (d, lax.rem(t + 2, 4))
    ydev = (d + stride - 2 * stride * yb, t)
    zdev = [None] + [(d + 2 * stride * (z_of[k] - zb), t) for k in (1, 2, 3)]

    barrier = pltpu.get_barrier_semaphore()
    for who in (core, xdev, ydev, zdev[1], zdev[2], zdev[3]):
        pl.semaphore_signal(barrier, inc=1, device_id=who, device_id_type=MESH)

    def remote(src, dst, send, recv, who):
        return pltpu.make_async_remote_copy(
            src_ref=src, dst_ref=dst, send_sem=send, recv_sem=recv, device_id=who, device_id_type=MESH
        )

    parts = (
        (wq_in, lambda s, lo, n: wq.at[s, pl.ds(lo, n)], 3 * QW),
        (wo_in, lambda s, lo, n: wo.at[pl.ds(s * QW + lo, n)], QW),
        (wi_in, lambda s, lo, n: wi.at[s, pl.ds(lo, n)], D),
        (w2_in, lambda s, lo, n: w2.at[s, pl.ds(lo, n)], D),
    )
    items = ITEMS
    zl = zbit

    def spot(i, y, z, lo=0, n=None):
        p, first, count = items[i][:3]
        at = (2 * y + z) * (parts[p][2] // 4) + first + lo
        return pl.multiple_of(at, 16), count if n is None else n

    def x_copy(i):
        src, place, _ = parts[items[i][0]]
        lo, n = spot(i, yb, zl)
        return remote(src.at[pl.ds(lo, n)], place(2, lo, n), xs.at[i, 0], xr.at[i, 0], xdev)

    def pass_on(i, k, at, slot, who):
        place = parts[items[i][0]][1]
        return remote(place(2, *at), place(slot, *at), xs.at[i, k], xr.at[i, k], who)

    def y_copy(i):
        return pass_on(i, 1, spot(i, yb, zl), 2, ydev)

    def z_copy(i):
        return pass_on(i, 2, spot(i, yb, zl), 2, zdev[1])

    def last_parts(i):
        _, _, n, nx, ny = items[i]
        src, place, _ = parts[items[i][0]]
        lo, count = spot(i, 1 - yb, 1 - zl, 0, nx)
        nz = n - nx - ny
        return (
            nx and (lambda: remote(src.at[pl.ds(lo, count)], place(2, lo, count), xs.at[i, 9], xr.at[i, 9], xdev)),
            ny and (lambda: pass_on(i, 3, spot(i, yb, 1 - zl, nx, ny), 2, ydev)),
            nz and (lambda: pass_on(i, 4, spot(i, 1 - yb, zl, nx + ny, nz), 2, zdev[1])),
        )

    def begin(copy):
        if copy:
            copy().start()

    def x_start(i):
        x_copy(i).start()
        begin(last_parts(i)[0])

    def c_copy(i, k):
        at = (spot(i, yb, zl), spot(i, 1 - yb, zl), spot(i, yb, 1 - zl), spot(i, 1 - yb, 1 - zl))[k]
        return pass_on(i, 5 + k, at, 3, core)

    def core_copy(p):
        src, place, n = parts[p]
        return remote(src, place(1, 0, n), cs.at[p], cr.at[p], core)

    def small_copy(k):
        return remote(wsm.at[2 if k == 3 else 0], wsm.at[k], ss.at[k - 1], sr.at[k - 1], (core, xdev, core)[k - 1])

    def own_copy(p):
        src, place, n = parts[p]
        return pltpu.make_async_copy(src, place(0, 0, n), lsem.at[2 + p])

    def arrived_x(i):
        x_copy(i).wait_recv()
        y_copy(i).start()
        z_copy(i).start()
        c_copy(i, 0).start()

    def arrived_yz(i):
        _, over_y, over_z = last_parts(i)
        y_copy(i).wait_recv()
        begin(over_z)
        c_copy(i, 1).start()
        z_copy(i).wait_recv()
        begin(over_y)
        c_copy(i, 2).start()

    def arrived_last(i):
        for copy in last_parts(i):
            if copy:
                copy().wait_recv()
        c_copy(i, 3).start()

    def arrived_core(i):
        for k in range(4):
            c_copy(i, k).wait_recv()

    def hook(name):
        steps = {
            "s": x_start, "x": arrived_x, "m": arrived_yz, "l": arrived_last, "c": arrived_core,
            "K": lambda p: core_copy(p).start(), "k": lambda p: core_copy(p).wait_recv(),
        }
        for what, which in FORWARD.get(name, ()):
            steps[what](which)

    def at_slot(table, run, s, before, behind):
        for k in range(SLOTS):
            name = before + str(k) + behind
            if name in table:
                pl.when(s == k)(lambda name=name: run(name))

    def hook_at(s, before, behind=""):
        at_slot(FORWARD, hook, s, before, behind)

    def fetch(one, two):
        return [
            pltpu.make_async_copy(one, xin.at[0:S], lsem.at[0]),
            pltpu.make_async_copy(two, xin.at[S:2 * S], lsem.at[1]),
        ]

    def stash_copy(s, back):
        ends = (stash.at[s], dg.at[s]) if back else (dg.at[s], stash.at[s])
        return pltpu.make_async_copy(ends[0], ends[1], lsem.at[7 + s])

    rows_in = fetch(x_hbm, g_hbm)
    for copy in rows_in:
        copy.start()
    own_copy(0).start()
    inputs_in = [
        pltpu.make_async_copy(src, dst, isem.at[k])
        for k, (src, dst) in enumerate((
            (rank_hbm, rank), (b_in_hbm, b_in), (bias_hbm, bias_qv), (table_hbm, table_in), (b_attn_hbm, b_attn_in),
            (n1g_hbm, n1g_in), (n1s_hbm, n1s_in), (b_out_hbm, b_out_in), (n2g_hbm, n2g_in), (n2s_hbm, n2s_in),
        ))
    ]
    for copy in inputs_in:
        copy.start()
    pl.semaphore_wait(barrier, 6)
    hook("p0")
    for copy in inputs_in:
        copy.wait()
    for k, ref in enumerate((b_attn_in, n1g_in, n1s_in, b_out_in, n2g_in, n2s_in)):
        vectors[k:k + 1] = ref[...].astype(F32).reshape(1, D)
    wsm[0] = jnp.zeros((8, D), F32)
    wsm[0, 0:1] = b_in[...].astype(F32).reshape(1, D)
    wsm[0, 1:3, 0:QW] = bias_qv[...].astype(F32)
    wsm[0, 3:3 + SLOT_HEADS, 0:32] = table_in[...].astype(F32)
    for k in (1, 2):
        small_copy(k).start()
    for p in (1, 2, 3):
        own_copy(p).start()
    shared[...] = jnp.zeros(shared.shape, F32)
    early[...] = jnp.zeros(early.shape, F32)
    late_x[...] = jnp.zeros(late_x.shape, F32)

    end = jnp.int32(0)
    start = jnp.int32(0)
    ends = []
    for k in range(8):
        length = dl[t, k]
        start = jnp.where(length == HALF, end, start)
        end = end + length
        ends.append(end)
    limit = (S - pc[t]).astype(F32)
    rows = iota((S, 1), 0)
    lanes = iota((1, S), 1)
    source_r = (rows + start) & (S - 1)
    source_l = (lanes + start) & (S - 1)
    perm[...] = jnp.where(source_r == lanes, 1.0, 0.0).astype(BF16)
    unperm[...] = jnp.where(((rows - start) & (S - 1)) == lanes, 1.0, 0.0).astype(BF16)
    hook("p1")
    doc_r = jnp.zeros((S, 1), F32)
    doc_l = jnp.zeros((1, S), F32)
    for e in ends:
        doc_r = doc_r + jnp.where(source_r >= e, 1.0, 0.0)
        doc_l = doc_l + jnp.where(source_l >= e, 1.0, 0.0)
    rank_row = rank[pl.ds(t, 1), :]
    sub = iota((16, S), 0)
    pieces = jnp.where(sub == 0, rank_row >> 4, jnp.where(sub == 1, rank_row & 15, 0))
    pieces = pieces.astype(F32).astype(BF16)
    ranks = nt(pieces, perm[...])
    rank_l = 16.0 * ranks[0:1] + ranks[1:2]
    ranks = nt(perm[...], pieces)
    rank_r = 16.0 * ranks[:, 0:1] + ranks[:, 1:2]
    lim_c = jnp.maximum(limit - 1.0, rank_l)
    lim_g = jnp.maximum(limit, rank_l) - 1.0
    for b in range(2):
        c = slice(HALF * b, HALF * b + HALF)
        same = doc_r[c] == doc_l[:, c]
        mask[b, :, 0:HALF] = jnp.where(same & (rank_r[c] <= lim_c[:, c]), 0.0, NEGATIVE).astype(BF16)
        mask[b, :, HALF:S] = jnp.where(same & (rank_r[c] <= lim_g[:, c]), 0.0, NEGATIVE).astype(BF16)
    onehot = bucket_onehot()

    def transposed(dst, src):
        for st in range(2):
            r = slice(st * S, st * S + S)
            dst[:, r] = src[r].T

    def permuted(dst):
        for copy in rows_in:
            copy.wait()
        for st in range(2):
            r = slice(st * S, st * S + S)
            for f in (slice(0, HROWS), slice(HROWS, D)):
                dst[r, f] = nn(perm[...], xin[r, f]).astype(BF16)

    xp = hid
    permuted(xp)
    own_copy(0).wait()

    def prob_at(s, h, b, st):
        k = 2 * b + st
        return dg.at[s, k * HALF:k * HALF + HALF, pl.ds(pl.multiple_of(h * HALF, HALF), HALF)]

    @pl.loop(0, SLOTS)
    def _(s):
        hook_at(s, "a", "0")

        @pl.when(s == 1)
        def _():
            small_copy(1).wait_recv()
            small_copy(2).wait_recv()
            small_copy(3).start()

        pl.when(s == 3)(lambda: small_copy(3).wait_recv())

        small = wsm[s].astype(BF16)
        text[pl.ds(pl.multiple_of(8 * s, 8), 8), :] = nn(small[:, 0:32], onehot.astype(BF16))
        sel = jnp.where(iota((8, 128), 0) == 1, 1.0, 0.0).astype(BF16)
        bq = tn(small[:, 0:QW], sel)[:, 0:1]
        sel = jnp.where(iota((8, 128), 0) == 2, 1.0, 0.0).astype(BF16)
        bv = tn(small[:, 0:QW], sel)[:, 0:1]
        r = nt(wq[s], xp[0:S])
        qkv[s, 0:QW] = ((r[0:QW] + bq).astype(BF16) * 0.125).astype(BF16)
        qkv[s, QW:2 * QW] = r[QW:2 * QW].astype(BF16)
        qkv[s, 2 * QW:3 * QW] = (r[2 * QW:3 * QW] + bv).astype(BF16)
        qg[s] = ((nt(wq[s, 0:QW], xp[S:2 * S]) + bq).astype(BF16) * 0.125).astype(BF16)

        hook_at(s, "a", "1")

        units = [(h, b, st) for h in range(SLOT_HEADS) for b in range(2) for st in range(2)]

        def score_at(h, b, st):
            k = 2 * b + st
            return slice(k * HALF, k * HALF + HALF), slice(h * HALF, h * HALF + HALF)

        def block_of(b):
            return slice(HALF * b, HALF * b + HALF)

        for h, b, st in units:
            q = qkv if st == 0 else qg
            lo = h * HD
            acc[score_at(h, b, st)] = tn(qkv[s, QW + lo:QW + lo + HD, block_of(b)], q[s, lo:lo + HD, block_of(b)])

        for h in range(SLOT_HEADS):
            rowvec = text[pl.ds(8 * s + 3 + h, 1), :]
            rolled = pltpu.roll(jnp.broadcast_to(rowvec, (HALF, S)), 0, 1, stride=1, stride_axis=0)
            bias = rolled[:, 0:HALF]
            for b in range(2):
                for st in range(2):
                    sc = acc[score_at(h, b, st)] + bias + mask[b, :, st * HALF:st * HALF + HALF].astype(F32)
                    e = jnp.exp(sc - jnp.max(sc, axis=0, keepdims=True))
                    p = (e * (1.0 / jnp.sum(e, axis=0, keepdims=True))).astype(BF16)
                    dg[(s,) + score_at(h, b, st)] = p

        hook_at(s, "a", "2")

        for h, b, st in units:
            lo = h * HD
            o = nn(qkv[s, 2 * QW + lo:2 * QW + lo + HD, block_of(b)], dg[(s,) + score_at(h, b, st)])
            to = slice(st * S + HALF * b, st * S + HALF * b + HALF)
            tA[pl.ds(pl.multiple_of(s * QW + lo, HD), HD), to] = o.astype(BF16)

        for k in range(SLOTS):
            @pl.when(s == k)
            def _():
                stash_copy(k, False).start()

    hook("o0")
    own_copy(1).wait()
    for st in range(2):
        r = slice(st * S, st * S + S)
        attn[r] = nt(unperm[...], tA[:, r]).astype(BF16)
    hook("o1")
    for r in (slice(k * HALF, k * HALF + HALF) for k in range(4)):
        res = xin[r].astype(F32) + nn(attn[r], wo[...]) + b_attn[...]
        cen = res - row_mean(res)
        rs = lax.rsqrt(row_mean(cen * cen) + EPSILON)
        xh = cen * rs
        xhat[r] = xh.astype(BF16)
        rstd1[r] = rs
        hid[r] = (xh * n1g[...] + n1s[...]).astype(BF16)
    transposed(tB, hid)
    rows_in = fetch(cc_hbm, cg_hbm)
    for copy in rows_in:
        copy.start()

    own_copy(2).wait()
    own_copy(3).wait()
    hook("o2")

    @pl.loop(0, SLOTS)
    def _(s):
        for k in range(SLOTS):
            @pl.when(s == k)
            def _():
                stash_copy(k, False).wait()
        for j in range(0, D, 256):
            hook_at(s, "f", str(j // 256))
            a, g = gelu_pair(nn(hid[...], wi[s, :, j:j + 256]) + wsm[s, 0:1, j:j + 256])
            act[s, :, j:j + 256] = a.astype(BF16)
            dg[s, :, j:j + 256] = g.astype(BF16)

    hook("g0")
    for j in range(0, D, 256):
        acc[:, j:j + 256] = nn(act[0], w2[0, :, j:j + 256])

    @pl.loop(1, SLOTS)
    def _(s):
        hook_at(s, "g")
        for j in range(0, D, 256):
            acc[:, j:j + 256] += nn(act[s], w2[s, :, j:j + 256])

    for copy in rows_in:
        copy.wait()

    @pl.loop(0, 4)
    def _(i):
        r = pl.ds(pl.multiple_of(i * HALF, HALF), HALF)
        res = hid[r, :].astype(F32) + acc[r, :] + b_out[...]
        cen = res - row_mean(res)
        rs = lax.rsqrt(row_mean(cen * cen) + EPSILON)
        xh = cen * rs
        cot = xin[r, :].astype(F32)
        hid[r, :] = (xh * n2g[...] + n2s[...]).astype(BF16)
        dxh = cot * n2g[...]
        dres = rs * (dxh - row_mean(dxh) - xh * row_mean(dxh * xh))
        acc[r, :] = dres
        xin[r, :] = dres.astype(BF16)
        shared[3:4] += col_sum(dres)
        shared[4:5] += col_sum(cot * xh)
        shared[5:6] += col_sum(cot)

    dlow = xin
    transposed(tA, dlow)
    rows_out = [
        pltpu.make_async_copy(hid.at[0:S], oc_hbm, lsem.at[0]),
        pltpu.make_async_copy(hid.at[S:2 * S], og_hbm, lsem.at[1]),
    ]
    for copy in rows_out:
        copy.start()

    def rows_at(lo, n):
        return pl.ds(pl.multiple_of(lo, ROWS), n)

    own_half = rows_at(yb * HROWS, HROWS)
    other_half = rows_at((1 - yb) * HROWS, HROWS)
    zlow, zhigh = zbit, lax.div(zb, 2)
    z_own = rows_at(zlow * HROWS, HROWS)
    z_other = rows_at((1 - zlow) * HROWS, HROWS)
    zy_own = rows_at(zlow * HROWS + yb * 2 * ROWS, 2 * ROWS)
    zy_other = rows_at(zlow * HROWS + (1 - yb) * 2 * ROWS, 2 * ROWS)
    zyz_own = rows_at(zlow * HROWS + yb * 2 * ROWS + zhigh * ROWS, ROWS)
    zyz_other = rows_at(zlow * HROWS + yb * 2 * ROWS + (1 - zhigh) * ROWS, ROWS)

    def block(k):
        return rows_at(yb * HROWS + z_of[k] * ROWS, ROWS)

    def store_at(dst, lo, value, z_first):
        for b in range(8):
            y, z = b % 2, b // 2
            to = ((z % 2) * 4 + y * 2 + z // 2 if z_first else y * 4 + z) * ROWS
            dst[to:to + ROWS, lo:lo + value.shape[1]] = value[b * ROWS:b * ROWS + ROWS, :]

    def store(dst, lead, lo, value, z_first):
        for b in range(8):
            y, z = b % 2, b // 2
            to = ((z % 2) * 4 + y * 2 + z // 2 if z_first else y * 4 + z) * ROWS
            dst[lead, to:to + ROWS, lo:lo + value.shape[1]] = value[b * ROWS:b * ROWS + ROWS, :]

    def add(dst, at, *sources):
        at = slice(None) if at is None else at
        total = dst[at, :]
        for src in sources:
            total = total + src[...]
        dst[at, :] = total

    class Lines:
        def __init__(self, base, given, over_core, part, over_x, over_y, whole_y, over_z):
            self.base, self.given, self.over_core, self.part = base, given, over_core, part
            self.over_x, self.over_y, self.whole_y, self.over_z = over_x, over_y, whole_y, over_z

        def send(self, k):
            sem = ps.at[self.base + k], pr.at[self.base + k]
            if k < 2:
                return remote(self.given.at[(3, 1)[k]], self.over_core.at[k], *sem, core)
            if k == 2:
                return remote(self.part.at[1], self.over_x, *sem, xdev)
            if k == 3:
                return remote(self.part.at[0], self.over_y, *sem, ydev)
            return remote(self.whole_y, self.over_z.at[k - 4], *sem, zdev[k - 3])

        def to_x(self):
            self.send(0).wait_recv()
            self.part[1] = self.given[2] + self.over_core[0]
            self.send(2).start()

        def to_y(self):
            self.send(1).wait_recv()
            self.send(2).wait_recv()
            self.part[0] = self.given[0] + self.over_core[1] + self.over_x[...]
            self.send(3).start()

        def to_z(self):
            self.send(3).wait_recv()
            self.whole_y[...] = self.part[0] + self.over_y[...]
            for k in (4, 5, 6):
                self.send(k).start()

        def total(self):
            for k in (4, 5, 6):
                self.send(k).wait_recv()
            return self.whole_y[...] + self.over_z[0] + self.over_z[1] + self.over_z[2]

    early_sum = Lines(0, early, e_core, e_part, e_x, e_y, e_sum, e_z)
    late_sum = Lines(7, late_x, l_core, l_part, l_x, l_y, l_sum, l_z)

    class Chunk:
        def __init__(self, kind, index, even, odd, rc, parts, out):
            self.kind = kind
            self.n, self.even, self.odd, self.rc, self.out = index, even, odd, rc, out
            self.moves = {}
            for k, (name, src, dst, who) in enumerate(parts):
                self.moves[name] = (src, dst, k + 2, who)

        def core_send(self, k):
            return remote(self.odd[k], self.rc[k], os.at[self.n, k], orr.at[self.n, k], core)

        def move(self, name):
            src, dst, k, who = self.moves[name]
            return remote(src, dst, os.at[self.n, k], orr.at[self.n, k], who)

        def go(self, *names):
            for name in names:
                self.move(name).start()

        def here(self, *names):
            for name in names:
                self.move(name).wait_recv()
            return [self.moves[name][1] for name in names]

        def core_sum(self, k):
            self.core_send(k).wait_recv()
            add(self.even[k], None, self.rc[k])

        def finish(self, at, *names):
            total = self.even[0][at, :].astype(F32)
            for ref in self.here(*names):
                total = total + ref[...].astype(F32)
            self.out[...] = total

        def sent(self):
            for k in (0, 1) if self.n > 5 else (0,):
                self.core_send(k).wait_send()
            for name in self.moves:
                self.move(name).wait_send()

    first, second = pl.ds(0, D // 2), pl.ds(D // 2, D // 2)
    third = [pl.ds(256 * k, 256) for k in range(3)]

    def x_flow(index, even, odd, rc, rx, ry, rz, out):
        e0, e2 = even
        parts = [("x", e2, rx, xdev), ("y", e0.at[other_half], ry, ydev)]
        parts += [("z%d" % k, e0.at[block(k)], rz(k), zdev[k]) for k in (1, 2, 3)]
        return Chunk("x", index, even, odd, rc, parts, out)

    def y_flow(index, even, odd, rc, rx, ry, rz, out):
        e0, e2 = even
        parts = [
            ("y2", e2.at[other_half], ry[1], ydev), ("y0", e0.at[other_half], ry[0], ydev),
            ("x", e2.at[own_half], rx, xdev),
        ]
        parts += [("z%d" % k, e0.at[block(k)], rz(k), zdev[k]) for k in (1, 2, 3)]
        return Chunk("y", index, even, odd, rc, parts, out)

    def z_flow(index, even, odd, rc, rz, ry, rx, rh, out):
        e0, e2 = even
        parts = [
            ("l2", e2.at[z_other], rz[1], zdev[1]), ("l0", e0.at[z_other], rz[0], zdev[1]),
            ("y2", e2.at[zy_other], ry[1], ydev), ("y0", e0.at[zy_other], ry[0], ydev),
            ("x", e2.at[zy_own], rx, xdev), ("h", e0.at[zyz_other], rh, zdev[2]),
        ]
        return Chunk("z", index, even, odd, rc, parts, out)

    def ab_even(g, cols):
        return (g.at[0, :, cols], g.at[1, :, cols]), (g.at[2, :, cols], g.at[2, :, cols])

    def c_even(cols):
        return (act.at[0, 0:D, cols], act.at[2, 0:D, cols]), (act.at[1, 0:D, cols], act.at[3, 0:D, cols])

    def pair(ref, cols):
        return ref.at[0, :, cols], ref.at[1, :, cols]

    def halves(ref):
        return ref.at[0:HROWS], ref.at[HROWS:D]

    def late(slot, k, lo, n):
        return w2.at[slot, lo:lo + n, third[k]]

    chunks = []
    for n, (g, rc) in enumerate(((ga, rca), (gb, rcb))):
        place = (lambda k, lo, c: second_a.at[lo:lo + c, third[k]]) if n == 0 else (lambda k, lo, c: late(0, k, lo, c))
        blocks = lambda k: lambda z: wi.at[n, (z - 1) * ROWS:z * ROWS, third[k]]
        for k in range(3):
            recv = first_in.at[n, k]
            base = 3 * n + k, *ab_even(g, third[k]), pair(rc, third[k])
            out = g_res.at[n, :, third[k]]
            kind = KINDS[3 * n + k]
            if kind == "x":
                chunks.append(x_flow(*base, recv, place(k, 0, HROWS), blocks(k), out))
            elif kind == "y":
                chunks.append(y_flow(*base, place(k, 0, HROWS), halves(recv), blocks(k), out))
            else:
                turns = place(k, 0, 2 * ROWS), place(k, 2 * ROWS, 2 * ROWS)
                chunks.append(z_flow(*base, halves(recv), turns, place(k, 4 * ROWS, 2 * ROWS), blocks(k)(1), out))

    def c_flow(index, k):
        kind = KINDS[index + 1]
        cols = pl.ds(128 * k, 128)
        a, b, out = w2.at[1, :, cols], w2.at[3, :, cols], g_res.at[2, :, cols]
        ends = lambda z: wi.at[3, (z - 1) * ROWS:z * ROWS, cols]
        if kind == "x":
            return x_flow(index, *c_even(cols), pair(rca, cols), a, b.at[0:HROWS], ends, out)
        if kind == "y":
            return y_flow(index, *c_even(cols), pair(rca, cols), b.at[0:HROWS], halves(a), ends, out)
        return z_flow(
            index, *c_even(cols), pair(rca, cols), halves(a), (b.at[0:2 * ROWS], b.at[2 * ROWS:4 * ROWS]),
            b.at[4 * ROWS:6 * ROWS], ends(1), out,
        )

    C0, C1, C2, D0, D1 = (c_flow(6 + k, k) for k in range(5))
    w_slots = [xhat.at[0:D, third[k]] for k in range(3)] + [hid.at[0:D, third[0]]]
    W = y_flow(
        11, (w_slots[0], w_slots[2]), (w_slots[1], w_slots[3]), (w2.at[2, :, third[0]], w2.at[2, :, third[1]]),
        wi.at[2, 0:HROWS, third[0]], halves(w2.at[2, :, third[2]]),
        lambda z: wi.at[2, HROWS + (z - 1) * ROWS:HROWS + z * ROWS, third[0]], g_w,
    )

    A0, A1, A2, B0, B1, B2 = chunks
    named = dict(A0=A0, A1=A1, A2=A2, B0=B0, B1=B1, B2=B2, C0=C0, C1=C1, C2=C2, D0=D0, D1=D1, W=W)

    def buffer_of(s):
        odd = lax.rem(s, 2)
        return 2 * odd + (1 - odd) * lax.div(s, 2)

    def after(s, three, two, one, zero):
        for k, step in ((3, three), (2, two), (1, one), (0, zero)):
            pl.when(s == k)(step)

    def x_arrived(c):
        add(c.even[0], None, *c.here("x"))
        c.go("y")

    def x_last(c):
        add(c.even[0], own_half, *c.here("y"))
        c.go("z1", "z2", "z3")

    def y_arrived(c):
        add(c.even[1], own_half, *c.here("y2"))
        c.go("x")

    def y_final(c):
        add(c.even[0], own_half, *c.here("y0", "x"))
        c.go("z1", "z2", "z3")

    def z_arrived(c, k):
        add(c.even[1 if k == 2 else 0], z_own, *c.here("l%d" % k))
        c.go("y%d" % k)

    def z_middle(c):
        add(c.even[1], zy_own, *c.here("y2"))
        c.go("x")

    def z_final(c):
        add(c.even[0], zy_own, *c.here("y0", "x"))
        c.go("h")

    def steps_of(c):
        if c.kind == "x":
            return {"XA": lambda: x_arrived(c), "XL": lambda: x_last(c), "FN": lambda: c.finish(block(0), "z1", "z2", "z3")}
        if c.kind == "y":
            return {"YA": lambda: y_arrived(c), "YF": lambda: y_final(c), "FN": lambda: c.finish(block(0), "z1", "z2", "z3")}
        return {
            "ZA2": lambda: z_arrived(c, 2), "ZA0": lambda: z_arrived(c, 0), "ZM": lambda: z_middle(c),
            "ZF": lambda: z_final(c), "FN": lambda: c.finish(zyz_own, "h"),
        }

    def turn(name):
        for which, what in BACKWARD.get(name, ()):
            steps_of(named[which])[what]()

    def turn_at(s, before, behind=""):
        at_slot(BACKWARD, turn, s, before, behind)

    def first_steps(*group):
        def odd(k):
            for c in group:
                c.core_send(k).start()

        def two():
            for c in group:
                c.core_sum(1)
                c.go({"x": "x", "y": "y2", "z": "l2"}[c.kind])

        def zero():
            for c in group:
                c.core_sum(0)
                if c.kind != "x":
                    c.go({"y": "y0", "z": "l0"}[c.kind])

        return lambda: odd(1), two, lambda: odd(0), zero

    @pl.loop(0, SLOTS)
    def _(i):
        s = 3 - i

        @pl.when(s == 1)
        def _():
            for c in (A0, A1, A2):
                c.core_send(1).wait_send()

        for k in range(3):
            value = nn(tA[...], act[s, :, 256 * k:256 * k + 256]).astype(BF16)
            store(ga, buffer_of(s), 256 * k, value, KINDS[k] == "z")
        after(s, *first_steps(A0, A1, A2))

    @pl.loop(0, SLOTS)
    def _(i):
        s = 3 - i
        turn_at(s, "gb", "a")
        for j in range(0, D, 256):
            low = (nt(dlow[...], w2[s, j:j + 256, :]) * dg[s, :, j:j + 256].astype(F32)).astype(BF16)
            dg[s, :, j:j + 256] = low
            early[s, 0:1, j:j + 256] = col_sum(low.astype(F32))

        @pl.when(s == 1)
        def _():
            for c in (B0, B1, B2):
                c.core_send(1).wait_send()

        turn_at(s, "gb", "b")
        for k in range(3):
            value = nn(tB[...], dg[s, :, 256 * k:256 * k + 256]).astype(BF16)
            store(gb, buffer_of(s), 256 * k, value, KINDS[3 + k] == "z")
        after(s, *first_steps(B0, B1, B2))
        turn_at(s, "gb", "c")
        for j in range(0, D, 256):
            acc[:, j:j + 256] += nt(dg[s], wi[s, j:j + 256, :])
        for k in range(SLOTS):
            @pl.when(s == k)
            def _():
                stash_copy(k, True).start()

    for p in range(4):
        core_copy(p).wait_send()
    for i in range(len(items)):
        for copy in (x_copy(i), y_copy(i), z_copy(i)):
            copy.wait_send()
        for copy in last_parts(i):
            if copy:
                copy().wait_send()
        for k in range(4):
            c_copy(i, k).wait_send()
    for k in (1, 2, 3):
        small_copy(k).wait_send()
    for k, who in enumerate((core, xdev, ydev, zdev[1], zdev[2], zdev[3])):
        pl.semaphore_signal(credit.at[k], inc=1, device_id=who, device_id_type=MESH)

    turn("ln")
    @pl.loop(0, 4)
    def _(i):
        r = pl.ds(pl.multiple_of(i * HALF, HALF), HALF)
        dy = acc[r, :]
        xh = xhat[r, :].astype(F32)
        dxh = dy * n1g[...]
        dres = rstd1[r, :] * (dxh - row_mean(dxh) - xh * row_mean(dxh * xh))
        acc[r, :] = dres
        xin[r, :] = dres.astype(BF16)
        shared[0:1] += col_sum(dres)
        shared[1:2] += col_sum(dy * xh)
        shared[2:3] += col_sum(dy)

    for k in range(6):
        pl.semaphore_wait(credit.at[k], 1)
    turn("tr")
    transposed(tB, dlow)
    turn("da")
    early[0, 1:7] = shared[0:6]
    for k in range(3):
        early[k + 1, 1:7] = shared[0:6]
    early_sum.send(0).start()
    early_sum.send(1).start()
    for r in (slice(0, HROWS), slice(HROWS, D)):
        tA[r] = nt(wo[r], dlow[...]).astype(BF16)
    for copy in rows_out:
        copy.wait()
    rows_in = fetch(x_hbm, g_hbm)
    for copy in rows_in:
        copy.start()
    turn("wo")
    for k in range(3):
        gwo = nn(tB[...], attn[:, 256 * k:256 * k + 256]).astype(BF16)
        for s in range(SLOTS):
            lo, hi = max(s * QW, 256 * k), min(s * QW + QW, 256 * k + 256)
            if lo < hi:
                ref, base = (xhat, 256 * s) if s < 3 else (hid, 0)
                store_at(ref, base + lo - s * QW, gwo[:, lo - 256 * k:hi - 256 * k], False)
    W.core_send(1).start()
    W.core_send(0).start()
    turn("do")
    for st in range(2):
        r = slice(st * S, st * S + S)
        for f in (slice(0, HROWS), slice(HROWS, D)):
            tA[f, r] = nt(tA[f, r], perm[...]).astype(BF16)
    _, two, _, zero = first_steps(W)
    two()
    zero()
    turn("xp")
    permuted(attn)
    turn("xt")
    transposed(tB, attn)
    xpT = tB

    ones = jnp.ones((16, S), BF16)
    def head_backward(s, h):
        at = (lambda v, m: v) if isinstance(h, int) else pl.multiple_of
        row = at(h * HD, HD)
        column = pl.ds(at(h * HALF, HALF), HALF)
        qr, kr, vr = pl.ds(row, HD), pl.ds(QW + row, HD), pl.ds(2 * QW + row, HD)
        oT = pl.ds(pl.multiple_of(s * QW + row, HD), HD)
        block_of = [slice(0, HALF), slice(HALF, S)]

        def out_grad(b, st):
            return tA[oT, st * S + HALF * b:st * S + HALF * b + HALF]

        def unit(b, st):
            return s, slice((2 * b + st) * HALF, (2 * b + st) * HALF + HALF), column

        pairs = [(b, st) for b in range(2) for st in range(2)]
        dps = [tn(qkv[s, vr, block_of[b]], out_grad(b, st)) for b, st in pairs]
        dv = [sum(nt(out_grad(b, st), dg[unit(b, st)]) for st in range(2)).astype(BF16) for b in range(2)]
        total = None
        for (b, st), dp in zip(pairs, dps):
            pf = dg[unit(b, st)].astype(F32)
            ds = (pf * (dp - jnp.sum(dp * pf, axis=0, keepdims=True))).astype(BF16)
            dg[unit(b, st)] = ds
            total = ds.astype(F32) if total is None else total + ds.astype(F32)
        skewed = jnp.zeros((8, S), F32)
        for a in range(HALF // 8):
            wide = jnp.concatenate([total[8 * a:8 * a + 8, :], jnp.zeros((8, HALF), F32)], axis=1)
            skewed = skewed + (wide if a == 0 else pltpu.roll(wide, S - 8 * a, 1))
        flipped = jnp.concatenate([skewed[7 - i:8 - i] for i in range(8)], axis=0)
        diag[pl.ds(8 * s + h, 1), :] = col_sum(pltpu.roll(flipped, S - 7, 1, stride=1, stride_axis=0))
        grads = []
        for b in range(2):
            kT = qkv[s, kr, block_of[b]]
            d0, d1 = dg[unit(b, 0)], dg[unit(b, 1)]
            dk = nt(qkv[s, qr, block_of[b]], d0) + nt(qg[s, qr, block_of[b]], d1)
            grads.append((nn(kT, d0) * 0.125, nn(kT, d1) * 0.125, dk))
        for b in range(2):
            dq_c, dq_g, dk = grads[b]
            qkv[s, qr, block_of[b]] = dq_c.astype(BF16)
            qg[s, qr, block_of[b]] = dq_g.astype(BF16)
            qkv[s, kr, block_of[b]] = dk.astype(BF16)
            qkv[s, vr, block_of[b]] = dv[b]

    @pl.loop(0, SLOTS)
    def _(i):
        s = 3 - i
        for k in range(SLOTS):
            @pl.when(s == k)
            def _():
                stash_copy(k, True).wait()

        @pl.loop(0, 2)
        def _(h):
            pl.when(h == 0)(lambda: turn_at(s, "p", "a"))
            pl.when(h == 1)(lambda: turn_at(s, "p", "b"))
            head_backward(s, h)

        turn_at(s, "p", "c")
        gq = nt(xpT[:, 0:S], qkv[s, 0:2 * HD])
        extra = nt(xpT[:, S:2 * S], qg[s, 0:2 * HD])
        store(act, s, 0, (gq + extra).astype(BF16), KINDS[7] == "z")
        dkv = jnp.concatenate([qkv[s, k * QW:k * QW + 2 * HD] for k in (1, 2)], axis=0)
        dkv = nt(xpT[:, 0:S], dkv).astype(BF16)
        store(act, s, 2 * HD, dkv[:, 0:2 * HD], KINDS[8] == "z")
        store(act, s, 4 * HD, dkv[:, 2 * HD:], KINDS[9] == "z")

        three, two, one, zero = first_steps(C0, C1, C2)

        def with_three():
            three()
            early_sum.to_x()

        def with_two():
            two()
            early_sum.to_y()

        def with_one():
            one()
            early_sum.to_z()

        after(s, with_three, with_two, with_one, zero)

    @pl.loop(0, SLOTS)
    def _(i):
        s = 3 - i

        turn_at(s, "q", "a")
        head_backward(s, 2)
        turn_at(s, "q", "b")
        dqkv = jnp.concatenate([qkv[s, k * QW + 2 * HD:k * QW + QW] for k in range(3)], axis=0)
        extra = jnp.concatenate([qg[s, 2 * HD:QW], jnp.zeros((2 * HD, S), BF16)], axis=0)
        store(act, s, D // 2, (nt(xpT[:, 0:S], dqkv) + nt(xpT[:, S:2 * S], extra)).astype(BF16), False)

        late_x[s, :, 0:QW] = (nt(ones, qkv[s, 0:QW]) + nt(ones, qg[s]))[0:1]
        late_x[s, :, QW:2 * QW] = nt(ones, qkv[s, 2 * QW:3 * QW])[0:1]
        table = lax.dot_general(
            diag[pl.ds(pl.multiple_of(8 * s, 8), 8), :], onehot, (((1,), (1,)), ((), ())),
            precision=lax.Precision.HIGHEST, preferred_element_type=F32,
        )
        for k in range(SLOT_HEADS):
            late_x[s, :, 2 * QW + 32 * k:2 * QW + 32 * k + 32] = table[k:k + 1]

        three, two, one, zero = first_steps(D0, D1)

        def with_three():
            late_sum.send(0).start()
            three()

        def with_two():
            late_sum.to_x()
            two()

        def with_one():
            late_sum.send(1).start()
            one()

        after(s, with_three, with_two, with_one, zero)

    late_sum.to_y()
    for s in range(SLOTS):
        turn("t%d" % s)
        dg[s, 0:S, 0:3 * QW] = nt(unperm[...], qkv[s]).astype(BF16)
        dg[s, S:2 * S, 0:QW] = nt(unperm[...], qg[s]).astype(BF16)
    late_sum.to_z()
    sm_res[0] = early_sum.total()

    def row_grads(s):
        for j in range(0, D, 256):
            acc[0:S, j:j + 256] += nn(dg[s, 0:S, 0:3 * QW], wq[s, :, j:j + 256])
            acc[S:2 * S, j:j + 256] += nn(dg[s, S:2 * S, 0:QW], wq[s, 0:QW, j:j + 256])

    for s in range(SLOTS):
        turn("t%d" % (SLOTS + s))
        row_grads(s)
    rows_out = [
        pltpu.make_async_copy(acc.at[0:S], gc_hbm, lsem.at[0]),
        pltpu.make_async_copy(acc.at[S:2 * S], gg_hbm, lsem.at[1]),
    ]
    for copy in rows_out:
        copy.start()
    turn("t8")
    sm_res[1, 0:1] = late_sum.total()
    sm_res[1, 1:8] = jnp.zeros((7, D), F32)
    turn("t9")
    g_res[2, :, 5 * 128:] = jnp.zeros((ROWS, 128), F32)
    results = [
        pltpu.make_async_copy(src, dst, osem.at[k])
        for k, (src, dst) in enumerate(((g_res, g_out), (g_w, gw_out), (sm_res, sm_out)))
    ]
    for copy in results:
        copy.start()

    for copy in rows_out:
        copy.wait()
    for k in range(7):
        early_sum.send(k).wait_send()
        late_sum.send(k).wait_send()
    for copy in results:
        copy.wait()
    for chunk in named.values():
        chunk.sent()


def layer(stride, *args):
    smem = pl.BlockSpec(memory_space=pltpu.SMEM)
    hbm = pl.BlockSpec(memory_space=pl.ANY)
    sd = jax.ShapeDtypeStruct
    vm = pltpu.VMEM
    dma = pltpu.SemaphoreType.DMA
    return pl.pallas_call(
        functools.partial(kernel, stride),
        out_shape=(
            sd((S, D), BF16), sd((S, D), BF16), sd((S, D), F32), sd((S, D), F32),
            sd((SLOTS, 2 * S, D), BF16), sd((3, ROWS, D), F32), sd((ROWS, 256), F32), sd((2, 8, D), F32),
        ),
        in_specs=[smem, smem] + [hbm] * 18,
        out_specs=(hbm,) * 8,
        scratch_shapes=[
            vm((S, S), BF16), vm((S, S), BF16), vm((2 * S, D), BF16), vm((2 * S, D), BF16),
            vm((D, 2 * S), BF16), vm((D, 2 * S), BF16), vm((2 * S, D), BF16),
            vm((SLOTS, 3 * QW, S), BF16), vm((SLOTS, QW, S), BF16), vm((2 * S, D), BF16), vm((2 * S, 1), F32),
            vm((SLOTS, 2 * S, D), BF16), vm((SLOTS, 2 * S, D), BF16), vm((2 * S, D), F32),
            vm((2, HALF, S), BF16), vm((32, S), F32),
            vm((SLOTS, 3 * QW, D), BF16), vm((D, D), BF16), vm((SLOTS, D, D), BF16), vm((SLOTS, D, D), BF16),
            vm((SLOTS, 8, D), F32), vm((8, D), F32),
            vm((3, D, D), BF16), vm((3, D, D), BF16), vm((2, D, D), BF16), vm((2, D, D), BF16),
            vm((2, 3, D, 256), BF16), vm((6 * ROWS, D), BF16),
            vm((8, D), F32),
            vm((SLOTS, 8, D), F32), vm((2, 8, D), F32), vm((2, 8, D), F32), vm((8, D), F32), vm((8, D), F32),
            vm((8, D), F32), vm((3, 8, D), F32),
            vm((SLOTS, 1, D), F32), vm((2, 1, D), F32), vm((2, 1, D), F32), vm((1, D), F32), vm((1, D), F32),
            vm((1, D), F32), vm((3, 1, D), F32),
            vm((SLOTS, S), jnp.int32), vm((D,), BF16), vm((2, QW), BF16), vm((SLOT_HEADS, 32), BF16),
            vm((D,), BF16), vm((D,), F32), vm((D,), F32), vm((D,), BF16), vm((D,), F32), vm((D,), F32),
            vm((3, ROWS, D), F32), vm((ROWS, 256), F32), vm((2, 8, D), F32), dma((3,)), dma((10,)),
            dma((11,)), dma((8, 10)), dma((8, 10)), dma((4,)), dma((4,)), dma((3,)), dma((3,)),
            dma((12, 8)), dma((12, 8)), dma((20,)), dma((20,)), pltpu.SemaphoreType.REGULAR((6,)),
        ],
        compiler_params=pltpu.CompilerParams(
            vmem_limit_bytes=int(63.5 * (1 << 20)), collective_id=0, has_side_effects=True
        ),
    )(*args)


def hand_out(
    oc_in, og_in, gc_in, gg_in, gw_hbm, gwo_hbm, sm_hbm,
    oc, og, gc, gg, g_qkv, g_bias, g_attn, b_attn, n1g, n1s, g_in, b_in, g_out, b_out, n2g, n2s, g_table,
    wide, narrow, gw, gwo, sm, v_qkv, v_bias, v_attn, lines, v_table, sems,
):
    def moves(pairs, base):
        copies = [pltpu.make_async_copy(src, dst, sems.at[base + k]) for k, (src, dst) in enumerate(pairs)]
        for copy in copies:
            copy.start()
        return copies

    smalls = moves(((sm_hbm, sm), (gwo_hbm, gwo), (gw_hbm, gw)), 0)
    vias = (wide.at[0], wide.at[1], narrow.at[0], narrow.at[1])
    rows_in = moves(tuple(zip((gc_in, gg_in, oc_in, og_in), vias)), 3)
    for copy in smalls:
        copy.wait()
    v_attn[...] = gwo[:, 0:QW].T
    for k in range(3):
        v_qkv[k, :, 0:2 * HD] = gw[2, :, 2 * HD * k:2 * HD * k + 2 * HD]
        v_qkv[k, :, 2 * HD:QW] = gw[2, :, D // 2 + HD * k:D // 2 + HD * k + HD]
    v_bias[0:1] = sm[1, 0:1, 0:QW]
    v_bias[1:2] = sm[1, 0:1, QW:2 * QW]
    for k in range(SLOT_HEADS):
        v_table[k:k + 1] = sm[1, 0:1, 2 * QW + 32 * k:2 * QW + 32 * k + 32]
    for k, line in enumerate(lines):
        line[...] = sm[0, k:k + 1].reshape(D)
    outs = moves(
        ((gw.at[0], g_out), (gw.at[1], g_in), (v_qkv, g_qkv), (v_attn, g_attn), (v_bias, g_bias), (v_table, g_table))
        + tuple(zip(lines, (b_in, b_attn, n1g, n1s, b_out, n2g, n2s))),
        7,
    )
    for k, (copy, via, dst) in enumerate(zip(rows_in, vias, (gc, gg, oc, og))):
        copy.wait()
        outs += moves(((via, dst),), 20 + k)
    for copy in outs:
        copy.wait()


def local(
    stride,
    content, query_stream, cot_content, cot_query, doc_lengths, rank_order, pred_counts, w_qkv, bias_qv,
    w_attn_out, b_attn_out, norm1_gain, norm1_shift, w_in, b_in, w_out, b_out, norm2_gain, norm2_shift, rel_table,
):
    out_c, out_g, gc, gg, _, gw, gwo, sm = layer(
        stride, doc_lengths, pred_counts, content, query_stream, cot_content, cot_query,
        jnp.transpose(w_qkv, (0, 2, 1)).reshape(3 * QW, D), w_attn_out, w_in, w_out,
        rank_order, b_in, bias_qv, rel_table.T, b_attn_out, norm1_gain, norm1_shift, b_out, norm2_gain, norm2_shift,
    )
    if stride > 1:
        groups = [list(range(k * stride, k * stride + stride)) for k in range(8)]
        gw = lax.psum_scatter(gw, "dp", scatter_dimension=1, axis_index_groups=groups, tiled=True)
        gwo = lax.psum_scatter(gwo, "dp", scatter_dimension=0, axis_index_groups=groups, tiled=True)
        sm = lax.psum(sm, "dp") / 8.0
    rows = gw.shape[1]
    sd = jax.ShapeDtypeStruct
    hbm = pl.BlockSpec(memory_space=pl.ANY)
    vm = pltpu.VMEM
    line = sd((D,), F32)
    outs = pl.pallas_call(
        hand_out,
        out_shape=(
            sd((S, D), BF16), sd((S, D), BF16), sd((S, D), F32), sd((S, D), F32),
            sd((3, rows, QW), F32), sd((2, QW), F32), sd((QW, rows), F32), line, line, line,
            sd((rows, D), F32), line, sd((rows, D), F32), line, line, line, sd((SLOT_HEADS, 32), F32),
        ),
        in_specs=[hbm] * 7,
        out_specs=[hbm] * 17,
        scratch_shapes=[
            vm((2, S, D), F32), vm((2, S, D), BF16), vm((3, rows, D), F32), vm((rows, 256), F32), vm((2, 8, D), F32),
            vm((3, rows, QW), F32), vm((2, QW), F32), vm((QW, rows), F32), [vm((D,), F32)] * 7,
            vm((SLOT_HEADS, 32), F32), pltpu.SemaphoreType.DMA((24,)),
        ],
        compiler_params=pltpu.CompilerParams(vmem_limit_bytes=int(63.5 * (1 << 20))),
    )(out_c, out_g, gc, gg, gw, gwo, sm)
    outs = list(outs)
    outs[12] = outs[12].T
    outs[16] = outs[16].T
    return tuple(outs)


def solution(mesh):
    in_specs = (
        P(("dp", "tensor"), None),
        P(("dp", "tensor"), None),
        P(("dp", "tensor"), None),
        P(("dp", "tensor"), None),
        P("dp", None),
        P("dp", None),
        P("dp"),
        P(None, None, "tensor"),
        P(None, "tensor"),
        P("tensor", None),
        P(),
        P(),
        P(),
        P(None, "tensor"),
        P("tensor"),
        P("tensor", None),
        P(),
        P(),
        P(),
        P(None, "tensor"),
    )
    out_specs = (
        P(("dp", "tensor"), None),
        P(("dp", "tensor"), None),
        P(("dp", "tensor"), None),
        P(("dp", "tensor"), None),
        P(None, "dp", "tensor"),
        P(None, "tensor"),
        P("tensor", "dp"),
        P(),
        P(),
        P(),
        P("dp", "tensor"),
        P("tensor"),
        P("tensor", "dp"),
        P(),
        P(),
        P(),
        P(None, "tensor"),
    )
    stride = mesh.shape["dp"] // 8
    return jax.shard_map(functools.partial(local, stride), mesh=mesh, in_specs=in_specs, out_specs=out_specs, check_vma=False)
```

```python
import functools

import jax
import jax.numpy as jnp
from jax import lax
from jax.experimental import pallas as pl
from jax.experimental.pallas import tpu as pltpu
from jax.sharding import PartitionSpec as P

EDGES = (1, 2, 3, 4, 5, 6, 7, 8, 12, 16, 23, 32, 46, 64, 91)
EPSILON = 1e-05
F32 = jnp.float32
BF16 = jnp.bfloat16
S = 512
HALF = 256
D = 768
HD = 64
SLOTS = 4
SLOT_HEADS = 3
QW = SLOT_HEADS * HD
NEGATIVE = -1e30
ROWS = D // 8
HROWS = D // 2
MESH = pl.DeviceIdType.MESH
ITEMS = (
    (0, 0, 64, 0, 32),
    (0, 64, 80, 0, 48),
    (1, 0, 48, 16, 16),
    (2, 0, 96, 32, 32),
    (2, 96, 96, 32, 32),
    (3, 0, 96, 32, 32),
    (3, 96, 96, 64, 16),
)
FORWARD = {
    "p0": (("s", 1),),
    "p1": (("K", 0),),
    "a01": (("s", 0), ("k", 0),),
    "a02": (("s", 2), ("x", 1), ("K", 3),),
    "a10": (("K", 1),),
    "a11": (("s", 4), ("x", 0),),
    "a12": (("K", 2), ("x", 2), ("s", 3), ("m", 1),),
    "a20": (("m", 0), ("m", 2), ("s", 5), ("x", 4), ("l", 1), ("l", 0), ("w", 0),),
    "a22": (("x", 3), ("u", 2), ("k", 1),),
    "a30": (("l", 2), ("w", 1), ("c", 0), ("s", 6),),
    "a32": (("m", 4),),
    "o0": (("x", 5), ("c", 1),),
    "o2": (("k", 2),),
    "f01": (("m", 3), ("v", 2),),
    "f10": (("x", 6), ("u", 3),),
    "f12": (("l", 4),),
    "f20": (("l", 3), ("w", 2),),
    "f30": (("c", 2),),
    "f31": (("m", 5),),
    "f32": (("m", 6), ("v", 3),),
    "g1": (("k", 3),),
    "g2": (("l", 6), ("l", 5), ("w", 3),),
    "g3": (("c", 3),),
}
KINDS = "xyzxyzxxyzyx"
BACKWARD = {
    "gb2b": (("A1", "YA"),),
    "gb1a": (("A2", "ZA2"), ("A0", "XA"),),
    "tr": (("B1", "YA"), ("B0", "XA"), ("A1", "YF"),),
    "do": (("A0", "XL"), ("A2", "ZM"),),
    "p3a": (("A2", "ZA0"), ("B0", "XL"),),
    "p2a": (("B2", "ZA2"),),
    "p2b": (("B1", "YF"),),
    "p2c": (("B2", "ZA0"), ("A2", "ZF"),),
    "p1b": (("B2", "ZM"),),
    "p0a": (("W", "XA"),),
    "q2a": (("C2", "ZA2"), ("B2", "ZF"), ("C1", "YA"),),
    "q1a": (("W", "XL"),),
    "q1b": (("C0", "XA"), ("A0", "FN"),),
    "q0b": (("A2", "FN"), ("C2", "ZM"), ("C1", "YF"), ("C2", "ZA0"),),
    "t0": (("D0", "YA"),),
    "t2": (("C0", "XL"), ("D1", "XA"),),
    "t3": (("C2", "ZF"),),
    "t4": (("A1", "FN"),),
    "t5": (("D0", "YF"), ("B2", "FN"),),
    "t6": (("W", "FN"), ("D1", "XL"),),
    "t7": (("C0", "FN"),),
    "t8": (("D0", "FN"), ("C1", "FN"), ("B0", "FN"),),
    "t9": (("B1", "FN"), ("C2", "FN"), ("D1", "FN"),),
}


def nn(a, b):
    return jnp.dot(a, b, preferred_element_type=F32)


def nt(a, b):
    return lax.dot_general(a, b, (((1,), (1,)), ((), ())), preferred_element_type=F32)


def tn(a, b):
    return lax.dot_general(a, b, (((0,), (0,)), ((), ())), preferred_element_type=F32)


def iota(shape, axis):
    return lax.broadcasted_iota(jnp.int32, shape, axis)


def bucket_onehot():
    lanes = iota((32, S), 1)
    offset = jnp.where(lanes < HALF, -lanes, S - lanes)
    distance = jnp.abs(offset)
    bucket = jnp.where(offset > 0, 16, 0)
    for edge in EDGES:
        bucket = bucket + (distance >= edge).astype(jnp.int32)
    return (bucket == iota((32, S), 0)).astype(F32)


def gelu_pair(v):
    w = v * 0.7071067811865476
    cdf = 0.5 + 0.5 * lax.erf(w)
    return v * cdf, cdf + w * jnp.exp2(w * w * -1.4426950408889634) * 0.5641895835477563


def row_mean(v):
    return jnp.sum(v, axis=-1, keepdims=True) * (1.0 / D)


def col_sum(v):
    return jnp.sum(v, axis=0, keepdims=True)


def kernel(
    stride,
    dl, pc, x_hbm, g_hbm, cc_hbm, cg_hbm, wq_in, wo_in, wi_in, w2_in, rank_hbm,
    b_in_hbm, bias_hbm, table_hbm, b_attn_hbm, n1g_hbm, n1s_hbm, b_out_hbm, n2g_hbm, n2s_hbm,
    oc_hbm, og_hbm, gc_hbm, gg_hbm, stash, kept, g_out, gw_out, sm_out,
    perm, unperm, xin, hid, tA, tB, attn, qkv, qg, xhat, rstd1, act, dg, acc,
    mask, lines, wq, wo, wi, w2, wsm, vectors,
    ga, gb, rca, rcb, first_in, second_a, shared, early, e_core, e_part, e_x, e_y, e_sum, e_z, late_x, l_core, l_part, l_x, l_y, l_sum, l_z,
    rank, b_in, bias_qv, table_in, b_attn_in, n1g_in, n1s_in, b_out_in, n2g_in, n2s_in, g_res, g_w, sm_res, osem, isem, gs, gr, ks, kr,
    lsem, xs, xr, cs, cr, ss, sr, os, orr, ps, pr, credit,
):
    b_attn, n1g, n1s, b_out, n2g, n2s = (vectors.at[k:k + 1] for k in range(6))
    text = diag = lines
    t = lax.axis_index("tensor")
    d = lax.axis_index("dp")
    yb = lax.rem(lax.div(d, stride), 2)
    zb = lax.rem(lax.div(d, 2 * stride), 4)
    zbit = lax.rem(zb, 2)
    z_of = (zb, zb + 1 - 2 * zbit, lax.rem(zb + 2, 4), 3 - zb)
    core = (d, t + 1 - 2 * lax.rem(t, 2))
    xdev = (d, lax.rem(t + 2, 4))
    ydev = (d + stride - 2 * stride * yb, t)
    zdev = [None] + [(d + 2 * stride * (z_of[k] - zb), t) for k in (1, 2, 3)]

    barrier = pltpu.get_barrier_semaphore()
    for who in (core, xdev, ydev, zdev[1], zdev[2], zdev[3]):
        pl.semaphore_signal(barrier, inc=1, device_id=who, device_id_type=MESH)

    def remote(src, dst, send, recv, who):
        return pltpu.make_async_remote_copy(
            src_ref=src, dst_ref=dst, send_sem=send, recv_sem=recv, device_id=who, device_id_type=MESH
        )

    parts = (
        (wq_in, lambda s, lo, n: wq.at[s, pl.ds(lo, n)], 3 * QW),
        (wo_in, lambda s, lo, n: wo.at[pl.ds(s * QW + lo, n)], QW),
        (wi_in, lambda s, lo, n: wi.at[s, pl.ds(lo, n)], D),
        (w2_in, lambda s, lo, n: w2.at[s, pl.ds(lo, n)], D),
    )
    items = ITEMS
    zl = zbit

    def spot(i, y, z, lo=0, n=None):
        p, first, count = items[i][:3]
        at = (2 * y + z) * (parts[p][2] // 4) + first + lo
        return pl.multiple_of(at, 16), count if n is None else n

    def x_copy(i):
        src, place, _ = parts[items[i][0]]
        lo, n = spot(i, yb, zl)
        return remote(src.at[pl.ds(lo, n)], place(2, lo, n), xs.at[0], xr.at[i, 0], xdev)

    def pass_on(i, k, at, slot, who):
        place = parts[items[i][0]][1]
        return remote(place(2, *at), place(slot, *at), xs.at[0], xr.at[i, k], who)

    def y_copy(i):
        return pass_on(i, 1, spot(i, yb, zl), 2, ydev)

    def z_copy(i):
        return pass_on(i, 2, spot(i, yb, zl), 2, zdev[1])

    def last_parts(i):
        _, _, n, nx, ny = items[i]
        src, place, _ = parts[items[i][0]]
        lo, count = spot(i, 1 - yb, 1 - zl, 0, nx)
        nz = n - nx - ny
        return (
            nx and (lambda: remote(src.at[pl.ds(lo, count)], place(2, lo, count), xs.at[0], xr.at[i, 5], xdev)),
            ny and (lambda: pass_on(i, 3, spot(i, yb, 1 - zl, nx, ny), 2, ydev)),
            nz and (lambda: pass_on(i, 4, spot(i, 1 - yb, zl, nx + ny, nz), 2, zdev[1])),
        )

    def begin(copy):
        if copy:
            copy().start()

    def x_start(i):
        x_copy(i).start()
        begin(last_parts(i)[0])

    def c_copy(p, k):
        place, n = parts[p][1:]
        if p < 2:
            at = 0, n
        else:
            y, z = ((yb, zl), (1 - yb, zl), (yb, 1 - zl), (1 - yb, 1 - zl))[k]
            at = pl.multiple_of((2 * y + z) * (n // 4), 16), n // 4
        return remote(place(2, *at), place(3, *at), ks.at[0], kr.at[p], core)

    def core_copy(p):
        src, place, n = parts[p]
        return remote(src, place(1, 0, n), cs.at[0], cr.at[p], core)

    def small_copy(k):
        return remote(wsm.at[2 if k == 3 else 0], wsm.at[k], ss.at[k - 1], sr.at[k - 1], (core, xdev, core)[k - 1])

    def own_copy(p):
        src, place, n = parts[p]
        return pltpu.make_async_copy(src, place(0, 0, n), lsem.at[2 + p])

    def arrived_x(i):
        x_copy(i).wait_recv()
        y_copy(i).start()
        z_copy(i).start()

    def arrived_yz(i):
        _, over_y, over_z = last_parts(i)
        y_copy(i).wait_recv()
        begin(over_z)
        z_copy(i).wait_recv()
        begin(over_y)

    def arrived_last(i):
        for copy in last_parts(i):
            if copy:
                copy().wait_recv()

    def drain(ref, sem):
        pltpu.make_async_copy(ref, ref, sem).wait()

    def arrived_core(p):
        place, n = parts[p][1:]
        drain(place(3, 0, n), kr.at[p])

    def to_core(p, which):
        for k in (0,) if p < 2 else which:
            c_copy(p, k).start()

    def hook(name):
        steps = {
            "s": x_start, "x": arrived_x, "m": arrived_yz, "l": arrived_last, "c": arrived_core,
            "u": lambda p: to_core(p, (0,)), "v": lambda p: to_core(p, (1, 2)), "w": lambda p: to_core(p, (3,)),
            "K": lambda p: core_copy(p).start(), "k": lambda p: core_copy(p).wait_recv(),
        }
        for what, which in FORWARD.get(name, ()):
            steps[what](which)

    def at_slot(table, run, s, before, behind):
        for k in range(SLOTS):
            name = before + str(k) + behind
            if name in table:
                pl.when(s == k)(lambda name=name: run(name))

    def hook_at(s, before, behind=""):
        at_slot(FORWARD, hook, s, before, behind)

    def fetch(one, two):
        return [
            pltpu.make_async_copy(one, xin.at[0:S], lsem.at[0]),
            pltpu.make_async_copy(two, xin.at[S:2 * S], lsem.at[1]),
        ]

    def kept_copy(back):
        ends = (kept, tB) if back else (tB, kept)
        return pltpu.make_async_copy(ends[0], ends[1], lsem.at[11])

    def stash_copy(s, back):
        ends = (stash.at[s], dg.at[s]) if back else (dg.at[s], stash.at[s])
        return pltpu.make_async_copy(ends[0], ends[1], lsem.at[7 + s])

    rows_in = fetch(x_hbm, g_hbm)
    for copy in rows_in:
        copy.start()
    own_copy(0).start()
    inputs_in = [
        pltpu.make_async_copy(src, dst, isem.at[k])
        for k, (src, dst) in enumerate((
            (rank_hbm, rank), (b_in_hbm, b_in), (bias_hbm, bias_qv), (table_hbm, table_in), (b_attn_hbm, b_attn_in),
            (n1g_hbm, n1g_in), (n1s_hbm, n1s_in), (b_out_hbm, b_out_in), (n2g_hbm, n2g_in), (n2s_hbm, n2s_in),
        ))
    ]
    for copy in inputs_in:
        copy.start()
    pl.semaphore_wait(barrier, 6)
    hook("p0")
    for copy in inputs_in:
        copy.wait()
    for k, ref in enumerate((b_attn_in, n1g_in, n1s_in, b_out_in, n2g_in, n2s_in)):
        vectors[k:k + 1] = ref[...].astype(F32).reshape(1, D)
    wsm[0] = jnp.zeros((8, D), F32)
    wsm[0, 0:1] = b_in[...].astype(F32).reshape(1, D)
    wsm[0, 1:3, 0:QW] = bias_qv[...].astype(F32)
    wsm[0, 3:3 + SLOT_HEADS, 0:32] = table_in[...].astype(F32)
    for k in (1, 2):
        small_copy(k).start()
    for p in (1, 2, 3):
        own_copy(p).start()
    shared[...] = jnp.zeros(shared.shape, F32)
    early[...] = jnp.zeros(early.shape, F32)
    late_x[...] = jnp.zeros(late_x.shape, F32)

    end = jnp.int32(0)
    start = jnp.int32(0)
    ends = []
    for k in range(8):
        length = dl[t, k]
        start = jnp.where(length == HALF, end, start)
        end = end + length
        ends.append(end)
    limit = (S - pc[t]).astype(F32)
    rows = iota((S, 1), 0)
    lanes = iota((1, S), 1)
    source_r = (rows + start) & (S - 1)
    source_l = (lanes + start) & (S - 1)
    perm[...] = jnp.where(source_r == lanes, 1.0, 0.0).astype(BF16)
    unperm[...] = jnp.where(((rows - start) & (S - 1)) == lanes, 1.0, 0.0).astype(BF16)
    hook("p1")
    doc_r = jnp.zeros((S, 1), F32)
    doc_l = jnp.zeros((1, S), F32)
    for e in ends:
        doc_r = doc_r + jnp.where(source_r >= e, 1.0, 0.0)
        doc_l = doc_l + jnp.where(source_l >= e, 1.0, 0.0)
    rank_row = rank[pl.ds(t, 1), :]
    sub = iota((16, S), 0)
    pieces = jnp.where(sub == 0, rank_row >> 4, jnp.where(sub == 1, rank_row & 15, 0))
    pieces = pieces.astype(F32).astype(BF16)
    ranks = nt(pieces, perm[...])
    rank_l = 16.0 * ranks[0:1] + ranks[1:2]
    ranks = nt(perm[...], pieces)
    rank_r = 16.0 * ranks[:, 0:1] + ranks[:, 1:2]
    lim_c = jnp.maximum(limit - 1.0, rank_l)
    lim_g = jnp.maximum(limit, rank_l) - 1.0
    for b in range(2):
        c = slice(HALF * b, HALF * b + HALF)
        same = doc_r[c] == doc_l[:, c]
        mask[b, :, 0:HALF] = jnp.where(same & (rank_r[c] <= lim_c[:, c]), 0.0, NEGATIVE).astype(BF16)
        mask[b, :, HALF:S] = jnp.where(same & (rank_r[c] <= lim_g[:, c]), 0.0, NEGATIVE).astype(BF16)
    onehot = bucket_onehot()

    def transposed(dst, src):
        for st in range(2):
            r = slice(st * S, st * S + S)
            dst[:, r] = src[r].T

    def permuted(dst):
        for copy in rows_in:
            copy.wait()
        for st in range(2):
            r = slice(st * S, st * S + S)
            for f in (slice(0, HROWS), slice(HROWS, D)):
                dst[r, f] = nn(perm[...], xin[r, f]).astype(BF16)

    xp = hid
    permuted(xp)
    own_copy(0).wait()

    def prob_at(s, h, b, st):
        k = 2 * b + st
        return dg.at[s, k * HALF:k * HALF + HALF, pl.ds(pl.multiple_of(h * HALF, HALF), HALF)]

    @pl.loop(0, SLOTS)
    def _(s):

        @pl.when(s == 2)
        def _():
            transposed(tB, xp)
            kept_copy(False).start()
            for st in range(2):
                r = slice(st * S, st * S + S)
                attn[r, 0:2 * QW] = nt(unperm[...], tA[0:2 * QW, r]).astype(BF16)

        hook_at(s, "a", "0")

        @pl.when(s == 1)
        def _():
            small_copy(1).wait_recv()
            small_copy(2).wait_recv()
            small_copy(3).start()

        pl.when(s == 3)(lambda: small_copy(3).wait_recv())

        small = wsm[s].astype(BF16)
        text[pl.ds(pl.multiple_of(8 * s, 8), 8), :] = nn(small[:, 0:32], onehot.astype(BF16))
        sel = jnp.where(iota((8, 128), 0) == 1, 1.0, 0.0).astype(BF16)
        bq = tn(small[:, 0:QW], sel)[:, 0:1]
        sel = jnp.where(iota((8, 128), 0) == 2, 1.0, 0.0).astype(BF16)
        bv = tn(small[:, 0:QW], sel)[:, 0:1]
        r = nt(wq[s], xp[0:S])
        qkv[s, 0:QW] = ((r[0:QW] + bq).astype(BF16) * 0.125).astype(BF16)
        qkv[s, QW:2 * QW] = r[QW:2 * QW].astype(BF16)
        qkv[s, 2 * QW:3 * QW] = (r[2 * QW:3 * QW] + bv).astype(BF16)
        qg[s] = ((nt(wq[s, 0:QW], xp[S:2 * S]) + bq).astype(BF16) * 0.125).astype(BF16)

        hook_at(s, "a", "1")

        units = [(h, b, st) for h in range(SLOT_HEADS) for b in range(2) for st in range(2)]

        def score_at(h, b, st):
            k = 2 * b + st
            return slice(k * HALF, k * HALF + HALF), slice(h * HALF, h * HALF + HALF)

        def block_of(b):
            return slice(HALF * b, HALF * b + HALF)

        for h, b, st in units:
            q = qkv if st == 0 else qg
            lo = h * HD
            acc[score_at(h, b, st)] = tn(qkv[s, QW + lo:QW + lo + HD, block_of(b)], q[s, lo:lo + HD, block_of(b)])

        for h in range(SLOT_HEADS):
            rowvec = text[pl.ds(8 * s + 3 + h, 1), :]
            rolled = pltpu.roll(jnp.broadcast_to(rowvec, (HALF, S)), 0, 1, stride=1, stride_axis=0)
            bias = rolled[:, 0:HALF]
            for b in range(2):
                for st in range(2):
                    sc = acc[score_at(h, b, st)] + bias + mask[b, :, st * HALF:st * HALF + HALF].astype(F32)
                    e = jnp.exp(sc - jnp.max(sc, axis=0, keepdims=True))
                    p = (e * (1.0 / jnp.sum(e, axis=0, keepdims=True))).astype(BF16)
                    dg[(s,) + score_at(h, b, st)] = p

        hook_at(s, "a", "2")

        for h, b, st in units:
            lo = h * HD
            o = nn(qkv[s, 2 * QW + lo:2 * QW + lo + HD, block_of(b)], dg[(s,) + score_at(h, b, st)])
            to = slice(st * S + HALF * b, st * S + HALF * b + HALF)
            tA[pl.ds(pl.multiple_of(s * QW + lo, HD), HD), to] = o.astype(BF16)

        for k in range(SLOTS):
            @pl.when(s == k)
            def _():
                stash_copy(k, False).start()

    hook("o0")
    own_copy(1).wait()
    for st in range(2):
        r = slice(st * S, st * S + S)
        attn[r, 2 * QW:] = nt(unperm[...], tA[2 * QW:, r]).astype(BF16)
    hook("o1")
    for r in (slice(k * HALF, k * HALF + HALF) for k in range(4)):
        res = xin[r].astype(F32) + nn(attn[r], wo[...]) + b_attn[...]
        cen = res - row_mean(res)
        rs = lax.rsqrt(row_mean(cen * cen) + EPSILON)
        xh = cen * rs
        xhat[r] = xh.astype(BF16)
        rstd1[r] = rs
        hid[r] = (xh * n1g[...] + n1s[...]).astype(BF16)
    kept_copy(False).wait()
    transposed(tB, hid)
    rows_in = fetch(cc_hbm, cg_hbm)
    for copy in rows_in:
        copy.start()

    own_copy(2).wait()
    own_copy(3).wait()
    hook("o2")

    @pl.loop(0, SLOTS)
    def _(s):
        for k in range(SLOTS):
            @pl.when(s == k)
            def _():
                stash_copy(k, False).wait()
        for j in range(0, D, 256):
            hook_at(s, "f", str(j // 256))
            a, g = gelu_pair(nn(hid[...], wi[s, :, j:j + 256]) + wsm[s, 0:1, j:j + 256])
            act[s, :, j:j + 256] = a.astype(BF16)
            dg[s, :, j:j + 256] = g.astype(BF16)

    hook("g0")
    for j in range(0, D, 256):
        acc[:, j:j + 256] = nn(act[0], w2[0, :, j:j + 256])

    @pl.loop(1, SLOTS)
    def _(s):
        hook_at(s, "g")
        for j in range(0, D, 256):
            acc[:, j:j + 256] += nn(act[s], w2[s, :, j:j + 256])

    for copy in rows_in:
        copy.wait()

    @pl.loop(0, 4)
    def _(i):
        r = pl.ds(pl.multiple_of(i * HALF, HALF), HALF)
        res = hid[r, :].astype(F32) + acc[r, :] + b_out[...]
        cen = res - row_mean(res)
        rs = lax.rsqrt(row_mean(cen * cen) + EPSILON)
        xh = cen * rs
        cot = xin[r, :].astype(F32)
        hid[r, :] = (xh * n2g[...] + n2s[...]).astype(BF16)
        dxh = cot * n2g[...]
        dres = rs * (dxh - row_mean(dxh) - xh * row_mean(dxh * xh))
        acc[r, :] = dres
        xin[r, :] = dres.astype(BF16)
        shared[3:4] += col_sum(dres)
        shared[4:5] += col_sum(cot * xh)
        shared[5:6] += col_sum(cot)

    dlow = xin
    transposed(tA, dlow)
    rows_out = [
        pltpu.make_async_copy(hid.at[0:S], oc_hbm, lsem.at[0]),
        pltpu.make_async_copy(hid.at[S:2 * S], og_hbm, lsem.at[1]),
    ]
    for copy in rows_out:
        copy.start()

    def rows_at(lo, n):
        return pl.ds(pl.multiple_of(lo, ROWS), n)

    own_half = rows_at(yb * HROWS, HROWS)
    other_half = rows_at((1 - yb) * HROWS, HROWS)
    zlow, zhigh = zbit, lax.div(zb, 2)
    z_own = rows_at(zlow * HROWS, HROWS)
    z_other = rows_at((1 - zlow) * HROWS, HROWS)
    zy_own = rows_at(zlow * HROWS + yb * 2 * ROWS, 2 * ROWS)
    zy_other = rows_at(zlow * HROWS + (1 - yb) * 2 * ROWS, 2 * ROWS)
    zyz_own = rows_at(zlow * HROWS + yb * 2 * ROWS + zhigh * ROWS, ROWS)
    zyz_other = rows_at(zlow * HROWS + yb * 2 * ROWS + (1 - zhigh) * ROWS, ROWS)

    def block(k):
        return rows_at(yb * HROWS + z_of[k] * ROWS, ROWS)

    def store_at(dst, lo, value, z_first):
        for b in range(8):
            y, z = b % 2, b // 2
            to = ((z % 2) * 4 + y * 2 + z // 2 if z_first else y * 4 + z) * ROWS
            dst[to:to + ROWS, lo:lo + value.shape[1]] = value[b * ROWS:b * ROWS + ROWS, :]

    def store(dst, lead, lo, value, z_first):
        for b in range(8):
            y, z = b % 2, b // 2
            to = ((z % 2) * 4 + y * 2 + z // 2 if z_first else y * 4 + z) * ROWS
            dst[lead, to:to + ROWS, lo:lo + value.shape[1]] = value[b * ROWS:b * ROWS + ROWS, :]

    def add(dst, at, *sources):
        at = slice(None) if at is None else at
        total = dst[at, :]
        for src in sources:
            total = total + src[...]
        dst[at, :] = total

    class Lines:
        def __init__(self, base, given, over_core, part, over_x, over_y, whole_y, over_z):
            self.base, self.given, self.over_core, self.part = base, given, over_core, part
            self.over_x, self.over_y, self.whole_y, self.over_z = over_x, over_y, whole_y, over_z

        def send(self, k):
            sem = ps.at[self.base + k], pr.at[self.base + k]
            if k < 2:
                return remote(self.given.at[(3, 1)[k]], self.over_core.at[k], *sem, core)
            if k == 2:
                return remote(self.part.at[1], self.over_x, *sem, xdev)
            if k == 3:
                return remote(self.part.at[0], self.over_y, *sem, ydev)
            return remote(self.whole_y, self.over_z.at[k - 4], *sem, zdev[k - 3])

        def to_x(self):
            self.send(0).wait_recv()
            self.part[1] = self.given[2] + self.over_core[0]
            self.send(2).start()

        def to_y(self):
            self.send(1).wait_recv()
            self.send(2).wait_recv()
            self.part[0] = self.given[0] + self.over_core[1] + self.over_x[...]
            self.send(3).start()

        def to_z(self):
            self.send(3).wait_recv()
            self.whole_y[...] = self.part[0] + self.over_y[...]
            for k in (4, 5, 6):
                self.send(k).start()

        def total(self):
            for k in (4, 5, 6):
                self.send(k).wait_recv()
            return self.whole_y[...] + self.over_z[0] + self.over_z[1] + self.over_z[2]

    early_sum = Lines(0, early, e_core, e_part, e_x, e_y, e_sum, e_z)
    late_sum = Lines(7, late_x, l_core, l_part, l_x, l_y, l_sum, l_z)

    def piece(z, lo=0):
        return slice(lo, lo + 3 * ROWS) if z == 0 else slice(lo + (z - 1) * ROWS, lo + z * ROWS)

    class Chunk:
        def __init__(self, kind, index, even, parts, out, ends=None):
            self.kind, self.ends = kind, ends
            self.n, self.even, self.out = index, even, out
            self.base = sum({"x": 3, "y": 4, "z": 6}[KINDS[k + (k > 5)]] for k in range(index)) if index < 11 else 0
            if index == 11:
                self.base = sum({"x": 3, "y": 4, "z": 6}[KINDS[k]] for k in range(12) if k != 6)
            slots = {"z1": 0, "z2": 0, "z3": 0}
            self.moves = {}
            for k, (name, src, dst, who) in enumerate(parts):
                if name not in slots:
                    slots[name] = len(slots) - (3 if kind == "z" else 2)
                self.moves[name] = (src, dst, slots[name], who)

        def move(self, name):
            src, dst, k, who = self.moves[name]
            return remote(src, dst, os.at[self.n // 6], orr.at[self.base + k], who)

        def go(self, *names):
            for name in names:
                self.move(name).start()

        def here(self, *names):
            for name in names:
                self.move(name).wait_recv()
            return [self.moves[name][1] for name in names]

        def finish(self, at, *names):
            total = self.even[0][at, :].astype(F32)
            if len(names) > 1:
                drain(self.ends, orr.at[self.base])
            else:
                self.here(*names)
            for ref in (self.moves[name][1] for name in names):
                total = total + ref[...].astype(F32)
            self.out[...] = total

    first, second = pl.ds(0, D // 2), pl.ds(D // 2, D // 2)
    third = [pl.ds(256 * k, 256) for k in range(3)]

    def x_flow(index, even, rx, ry, rz, out):
        e0, e2 = even
        parts = [("x", e2, rx, xdev), ("y", e0.at[other_half], ry, ydev)]
        parts += [("z%d" % k, e0.at[block(k)], rz(k), zdev[k]) for k in (1, 2, 3)]
        return Chunk("x", index, even, parts, out, rz(0))

    def y_flow(index, even, rx, ry, rz, out):
        e0, e2 = even
        parts = [
            ("y2", e2.at[other_half], ry[1], ydev), ("y0", e0.at[other_half], ry[0], ydev),
            ("x", e2.at[own_half], rx, xdev),
        ]
        parts += [("z%d" % k, e0.at[block(k)], rz(k), zdev[k]) for k in (1, 2, 3)]
        return Chunk("y", index, even, parts, out, rz(0))

    def z_flow(index, even, rz, ry, rx, rh, out):
        e0, e2 = even
        parts = [
            ("l2", e2.at[z_other], rz[1], zdev[1]), ("l0", e0.at[z_other], rz[0], zdev[1]),
            ("y2", e2.at[zy_other], ry[1], ydev), ("y0", e0.at[zy_other], ry[0], ydev),
            ("x", e2.at[zy_own], rx, xdev), ("h", e0.at[zyz_other], rh, zdev[2]),
        ]
        return Chunk("z", index, even, parts, out)

    def c_even(cols):
        return act.at[0, 0:D, cols], act.at[2, 0:D, cols]

    def pair(ref, cols):
        return ref.at[0, :, cols], ref.at[1, :, cols]

    def halves(ref):
        return ref.at[0:HROWS], ref.at[HROWS:D]

    def late(slot, k, lo, n):
        return w2.at[slot, lo:lo + n, third[k]]

    chunks = []
    for n, (g, rc) in enumerate(((ga, rca), (gb, rcb))):
        place = (lambda k, lo, c: second_a.at[lo:lo + c, third[k]]) if n == 0 else (lambda k, lo, c: late(0, k, lo, c))
        blocks = lambda k: lambda z: wi.at[n, piece(z), third[k]]
        for k in range(3):
            recv = first_in.at[n, k]
            base = 3 * n + k, pair(g, third[k])
            out = g_res.at[n, :, third[k]]
            kind = KINDS[3 * n + k]
            if kind == "x":
                chunks.append(x_flow(*base, recv, place(k, 0, HROWS), blocks(k), out))
            elif kind == "y":
                chunks.append(y_flow(*base, place(k, 0, HROWS), halves(recv), blocks(k), out))
            else:
                turns = place(k, 0, 2 * ROWS), place(k, 2 * ROWS, 2 * ROWS)
                chunks.append(z_flow(*base, halves(recv), turns, place(k, 4 * ROWS, 2 * ROWS), blocks(k)(1), out))

    def c_flow(index, k):
        kind = KINDS[index + 1]
        cols = pl.ds(128 * k, 128)
        a, b, out = w2.at[1, :, cols], w2.at[3, :, cols], g_res.at[2, :, cols]
        ends = lambda z: wi.at[3, piece(z), cols]
        if kind == "x":
            return x_flow(index, c_even(cols), a, b.at[0:HROWS], ends, out)
        if kind == "y":
            return y_flow(index, c_even(cols), b.at[0:HROWS], halves(a), ends, out)
        return z_flow(
            index, c_even(cols), halves(a), (b.at[0:2 * ROWS], b.at[2 * ROWS:4 * ROWS]),
            b.at[4 * ROWS:6 * ROWS], ends(1), out,
        )

    C0, C1, C2, D0, D1 = (c_flow(6 + k, k) for k in range(5))
    w_slots = [xhat.at[0:D, third[k]] for k in range(3)] + [hid.at[0:D, third[0]]]
    W = x_flow(
        11, (w_slots[0], w_slots[2]),
        w2.at[2, :, third[2]], wi.at[2, 0:HROWS, third[0]],
        lambda z: wi.at[2, piece(z, HROWS), third[0]], g_w,
    )

    A0, A1, A2, B0, B1, B2 = chunks
    named = dict(A0=A0, A1=A1, A2=A2, B0=B0, B1=B1, B2=B2, C0=C0, C1=C1, C2=C2, D0=D0, D1=D1, W=W)

    class Group:
        def __init__(self, index, even, odd, rc, *members):
            self.n, self.even, self.odd, self.rc, self.members = index, even, odd, rc, members

        def send(self, k):
            return remote(self.odd[k], self.rc[k], gs.at[self.n, k], gr.at[self.n, k], core)

        def sum(self, k):
            self.send(k).wait_recv()
            add(self.even[k], None, self.rc[k])
            for c in self.members:
                if k == 1:
                    c.go({"x": "x", "y": "y2", "z": "l2"}[c.kind])
                elif c.kind != "x":
                    c.go({"y": "y0", "z": "l0"}[c.kind])

        def steps(self):
            return (
                lambda: self.send(1).start(), lambda: self.sum(1), lambda: self.send(0).start(), lambda: self.sum(0),
            )

    def c_group(index, cols, *members):
        odd = act.at[1, 0:D, cols], act.at[3, 0:D, cols]
        return Group(index, c_even(cols), odd, pair(rca, cols), *members)

    every = pl.ds(0, D)
    GA = Group(0, pair(ga, every), (ga.at[2], ga.at[2]), pair(rca, every), A0, A1, A2)
    GB = Group(1, pair(gb, every), (gb.at[2], gb.at[2]), pair(rcb, every), B0, B1, B2)
    GC = c_group(2, first, C0, C1, C2)
    GD = c_group(3, pl.ds(D // 2, 256), D0, D1)
    GW = Group(
        4, (w_slots[0], w_slots[2]), (w_slots[1], w_slots[3]),
        (w2.at[2, :, third[0]], w2.at[2, :, third[1]]), W,
    )

    def buffer_of(s):
        odd = lax.rem(s, 2)
        return 2 * odd + (1 - odd) * lax.div(s, 2)

    def after(s, three, two, one, zero):
        for k, step in ((3, three), (2, two), (1, one), (0, zero)):
            pl.when(s == k)(step)

    def x_arrived(c):
        add(c.even[0], None, *c.here("x"))
        c.go("y")

    def x_last(c):
        add(c.even[0], own_half, *c.here("y"))
        c.go("z1", "z2", "z3")

    def y_arrived(c):
        add(c.even[1], own_half, *c.here("y2"))
        c.go("x")

    def y_final(c):
        add(c.even[0], own_half, *c.here("y0", "x"))
        c.go("z1", "z2", "z3")

    def z_arrived(c, k):
        add(c.even[1 if k == 2 else 0], z_own, *c.here("l%d" % k))
        c.go("y%d" % k)

    def z_middle(c):
        add(c.even[1], zy_own, *c.here("y2"))
        c.go("x")

    def z_final(c):
        add(c.even[0], zy_own, *c.here("y0", "x"))
        c.go("h")

    def steps_of(c):
        if c.kind == "x":
            return {"XA": lambda: x_arrived(c), "XL": lambda: x_last(c), "FN": lambda: c.finish(block(0), "z1", "z2", "z3")}
        if c.kind == "y":
            return {"YA": lambda: y_arrived(c), "YF": lambda: y_final(c), "FN": lambda: c.finish(block(0), "z1", "z2", "z3")}
        return {
            "ZA2": lambda: z_arrived(c, 2), "ZA0": lambda: z_arrived(c, 0), "ZM": lambda: z_middle(c),
            "ZF": lambda: z_final(c), "FN": lambda: c.finish(zyz_own, "h"),
        }

    def turn(name):
        for which, what in BACKWARD.get(name, ()):
            steps_of(named[which])[what]()

    def turn_at(s, before, behind=""):
        at_slot(BACKWARD, turn, s, before, behind)

    @pl.loop(0, SLOTS)
    def _(i):
        s = 3 - i

        pl.when(s == 1)(lambda: GA.send(1).wait_send())
        for k in range(3):
            value = nn(tA[...], act[s, :, 256 * k:256 * k + 256]).astype(BF16)
            store(ga, buffer_of(s), 256 * k, value, KINDS[k] == "z")

        def one():
            GA.send(0).start()
            GA.sum(1)

        pl.when(s == 3)(lambda: GA.send(1).start())
        pl.when(s == 1)(one)

    @pl.loop(0, SLOTS)
    def _(i):
        s = 3 - i
        turn_at(s, "gb", "a")
        for j in range(0, D, 256):
            low = (nt(dlow[...], w2[s, j:j + 256, :]) * dg[s, :, j:j + 256].astype(F32)).astype(BF16)
            dg[s, :, j:j + 256] = low
            early[s, 0:1, j:j + 256] = col_sum(low.astype(F32))

        pl.when(s == 3)(lambda: GA.sum(0))
        pl.when(s == 1)(lambda: GB.send(1).wait_send())
        turn_at(s, "gb", "b")
        for k in range(3):
            value = nn(tB[...], dg[s, :, 256 * k:256 * k + 256]).astype(BF16)
            store(gb, buffer_of(s), 256 * k, value, KINDS[3 + k] == "z")
        after(s, *GB.steps())
        turn_at(s, "gb", "c")
        for j in range(0, D, 256):
            acc[:, j:j + 256] += nt(dg[s], wi[s, j:j + 256, :])
        for k in range(SLOTS):
            @pl.when(s == k)
            def _():
                stash_copy(k, True).start()

    for sem in (xs, ks, cs):
        drain(w2.at[0:3], sem.at[0])
    for k in (1, 2, 3):
        small_copy(k).wait_send()
    for k, who in enumerate((core, xdev, ydev, zdev[1], zdev[2], zdev[3])):
        pl.semaphore_signal(credit.at[k], inc=1, device_id=who, device_id_type=MESH)

    turn("ln")
    @pl.loop(0, 4)
    def _(i):
        r = pl.ds(pl.multiple_of(i * HALF, HALF), HALF)
        dy = acc[r, :]
        xh = xhat[r, :].astype(F32)
        dxh = dy * n1g[...]
        dres = rstd1[r, :] * (dxh - row_mean(dxh) - xh * row_mean(dxh * xh))
        acc[r, :] = dres
        xin[r, :] = dres.astype(BF16)
        shared[0:1] += col_sum(dres)
        shared[1:2] += col_sum(dy * xh)
        shared[2:3] += col_sum(dy)

    for k in range(6):
        pl.semaphore_wait(credit.at[k], 1)
    turn("tr")
    transposed(tB, dlow)
    turn("da")
    early[0, 1:7] = shared[0:6]
    for k in range(3):
        early[k + 1, 1:7] = shared[0:6]
    early_sum.send(0).start()
    early_sum.send(1).start()
    for r in (slice(0, HROWS), slice(HROWS, D)):
        tA[r] = nt(wo[r], dlow[...]).astype(BF16)
    for copy in rows_out:
        copy.wait()
    turn("wo")
    for k in range(3):
        gwo = nn(tB[...], attn[:, 256 * k:256 * k + 256]).astype(BF16)
        for s in range(SLOTS):
            lo, hi = max(s * QW, 256 * k), min(s * QW + QW, 256 * k + 256)
            if lo < hi:
                ref, base = (xhat, 256 * s) if s < 3 else (hid, 0)
                store_at(ref, base + lo - s * QW, gwo[:, lo - 256 * k:hi - 256 * k], False)
    kept_copy(True).start()
    GW.send(1).start()
    GW.send(0).start()
    turn("do")
    for st in range(2):
        r = slice(st * S, st * S + S)
        for f in (slice(0, HROWS), slice(HROWS, D)):
            tA[f, r] = nt(tA[f, r], perm[...]).astype(BF16)
    GW.sum(1)
    turn("xp")
    turn("xt")
    kept_copy(True).wait()
    GW.sum(0)
    xpT = tB

    ones = jnp.ones((16, S), BF16)
    def head_backward(s, h):
        at = (lambda v, m: v) if isinstance(h, int) else pl.multiple_of
        row = at(h * HD, HD)
        column = pl.ds(at(h * HALF, HALF), HALF)
        qr, kr, vr = pl.ds(row, HD), pl.ds(QW + row, HD), pl.ds(2 * QW + row, HD)
        oT = pl.ds(pl.multiple_of(s * QW + row, HD), HD)
        block_of = [slice(0, HALF), slice(HALF, S)]

        def out_grad(b, st):
            return tA[oT, st * S + HALF * b:st * S + HALF * b + HALF]

        def unit(b, st):
            return s, slice((2 * b + st) * HALF, (2 * b + st) * HALF + HALF), column

        pairs = [(b, st) for b in range(2) for st in range(2)]
        dps = [tn(qkv[s, vr, block_of[b]], out_grad(b, st)) for b, st in pairs]
        dv = [sum(nt(out_grad(b, st), dg[unit(b, st)]) for st in range(2)).astype(BF16) for b in range(2)]
        total = None
        for (b, st), dp in zip(pairs, dps):
            pf = dg[unit(b, st)].astype(F32)
            ds = (pf * (dp - jnp.sum(dp * pf, axis=0, keepdims=True))).astype(BF16)
            dg[unit(b, st)] = ds
            total = ds.astype(F32) if total is None else total + ds.astype(F32)
        skewed = jnp.zeros((8, S), F32)
        for a in range(HALF // 8):
            wide = jnp.concatenate([total[8 * a:8 * a + 8, :], jnp.zeros((8, HALF), F32)], axis=1)
            skewed = skewed + (wide if a == 0 else pltpu.roll(wide, S - 8 * a, 1))
        flipped = jnp.concatenate([skewed[7 - i:8 - i] for i in range(8)], axis=0)
        diag[pl.ds(8 * s + h, 1), :] = col_sum(pltpu.roll(flipped, S - 7, 1, stride=1, stride_axis=0))
        grads = []
        for b in range(2):
            kT = qkv[s, kr, block_of[b]]
            d0, d1 = dg[unit(b, 0)], dg[unit(b, 1)]
            dk = nt(qkv[s, qr, block_of[b]], d0) + nt(qg[s, qr, block_of[b]], d1)
            grads.append((nn(kT, d0) * 0.125, nn(kT, d1) * 0.125, dk))
        for b in range(2):
            dq_c, dq_g, dk = grads[b]
            qkv[s, qr, block_of[b]] = dq_c.astype(BF16)
            qg[s, qr, block_of[b]] = dq_g.astype(BF16)
            qkv[s, kr, block_of[b]] = dk.astype(BF16)
            qkv[s, vr, block_of[b]] = dv[b]

    @pl.loop(0, SLOTS)
    def _(i):
        s = 3 - i
        for k in range(SLOTS):
            @pl.when(s == k)
            def _():
                stash_copy(k, True).wait()

        @pl.loop(0, 2)
        def _(h):
            pl.when(h == 0)(lambda: turn_at(s, "p", "a"))
            pl.when(h == 1)(lambda: turn_at(s, "p", "b"))
            head_backward(s, h)

        turn_at(s, "p", "c")
        gq = nt(xpT[:, 0:S], qkv[s, 0:2 * HD])
        extra = nt(xpT[:, S:2 * S], qg[s, 0:2 * HD])
        store(act, s, 0, (gq + extra).astype(BF16), KINDS[7] == "z")
        dkv = jnp.concatenate([qkv[s, k * QW:k * QW + 2 * HD] for k in (1, 2)], axis=0)
        dkv = nt(xpT[:, 0:S], dkv).astype(BF16)
        store(act, s, 2 * HD, dkv[:, 0:2 * HD], KINDS[8] == "z")
        store(act, s, 4 * HD, dkv[:, 2 * HD:], KINDS[9] == "z")

        three, two, one, zero = GC.steps()

        def with_three():
            three()
            early_sum.to_x()

        def with_two():
            two()
            early_sum.to_y()

        def with_one():
            one()
            early_sum.to_z()

        after(s, with_three, with_two, with_one, zero)

    @pl.loop(0, SLOTS)
    def _(i):
        s = 3 - i

        turn_at(s, "q", "a")
        head_backward(s, 2)
        turn_at(s, "q", "b")
        dqkv = jnp.concatenate([qkv[s, k * QW + 2 * HD:k * QW + QW] for k in range(3)], axis=0)
        extra = jnp.concatenate([qg[s, 2 * HD:QW], jnp.zeros((2 * HD, S), BF16)], axis=0)
        store(act, s, D // 2, (nt(xpT[:, 0:S], dqkv) + nt(xpT[:, S:2 * S], extra)).astype(BF16), False)

        late_x[s, :, 0:QW] = (nt(ones, qkv[s, 0:QW]) + nt(ones, qg[s]))[0:1]
        late_x[s, :, QW:2 * QW] = nt(ones, qkv[s, 2 * QW:3 * QW])[0:1]
        table = lax.dot_general(
            diag[pl.ds(pl.multiple_of(8 * s, 8), 8), :], onehot, (((1,), (1,)), ((), ())),
            precision=lax.Precision.HIGHEST, preferred_element_type=F32,
        )
        for k in range(SLOT_HEADS):
            late_x[s, :, 2 * QW + 32 * k:2 * QW + 32 * k + 32] = table[k:k + 1]

        three, two, one, zero = GD.steps()

        def with_three():
            late_sum.send(0).start()
            three()

        def with_two():
            late_sum.to_x()
            two()

        def with_one():
            late_sum.send(1).start()
            one()

        after(s, with_three, with_two, with_one, zero)

    late_sum.to_y()
    for s in range(SLOTS):
        turn("t%d" % s)
        dg[s, 0:S, 0:3 * QW] = nt(unperm[...], qkv[s]).astype(BF16)
        dg[s, S:2 * S, 0:QW] = nt(unperm[...], qg[s]).astype(BF16)
    late_sum.to_z()
    sm_res[0] = early_sum.total()

    def row_grads(s):
        for j in range(0, D, 256):
            acc[0:S, j:j + 256] += nn(dg[s, 0:S, 0:3 * QW], wq[s, :, j:j + 256])
            acc[S:2 * S, j:j + 256] += nn(dg[s, S:2 * S, 0:QW], wq[s, 0:QW, j:j + 256])

    for s in range(SLOTS):
        turn("t%d" % (SLOTS + s))
        row_grads(s)
    rows_out = [
        pltpu.make_async_copy(acc.at[0:S], gc_hbm, lsem.at[0]),
        pltpu.make_async_copy(acc.at[S:2 * S], gg_hbm, lsem.at[1]),
    ]
    for copy in rows_out:
        copy.start()
    turn("t8")
    sm_res[1, 0:1] = late_sum.total()
    sm_res[1, 1:8] = jnp.zeros((7, D), F32)
    drain(dg.at[0:3, 0:960], os.at[0])
    for group in (GA, GB):
        group.send(0).wait_send()
    for group in (GC, GD, GW):
        group.send(0).wait_send()
        group.send(1).wait_send()
    for k in range(7):
        early_sum.send(k).wait_send()
        late_sum.send(k).wait_send()
    turn("t9")
    g_res[2, :, 5 * 128:] = jnp.zeros((ROWS, 128), F32)
    results = [
        pltpu.make_async_copy(src, dst, osem.at[k])
        for k, (src, dst) in enumerate(((g_res, g_out), (g_w, gw_out), (sm_res, sm_out)))
    ]
    for copy in results:
        copy.start()

    for copy in rows_out:
        copy.wait()
    for copy in results:
        copy.wait()
    drain(dg.at[0:3, 0:560], os.at[1])


def layer(stride, *args):
    smem = pl.BlockSpec(memory_space=pltpu.SMEM)
    hbm = pl.BlockSpec(memory_space=pl.ANY)
    sd = jax.ShapeDtypeStruct
    vm = pltpu.VMEM
    dma = pltpu.SemaphoreType.DMA
    return pl.pallas_call(
        functools.partial(kernel, stride),
        out_shape=(
            sd((S, D), BF16), sd((S, D), BF16), sd((S, D), F32), sd((S, D), F32),
            sd((SLOTS, 2 * S, D), BF16), sd((D, 2 * S), BF16), sd((3, ROWS, D), F32), sd((ROWS, 256), F32), sd((2, 8, D), F32),
        ),
        in_specs=[smem, smem] + [hbm] * 18,
        out_specs=(hbm,) * 9,
        scratch_shapes=[
            vm((S, S), BF16), vm((S, S), BF16), vm((2 * S, D), BF16), vm((2 * S, D), BF16),
            vm((D, 2 * S), BF16), vm((D, 2 * S), BF16), vm((2 * S, D), BF16),
            vm((SLOTS, 3 * QW, S), BF16), vm((SLOTS, QW, S), BF16), vm((2 * S, D), BF16), vm((2 * S, 1), F32),
            vm((SLOTS, 2 * S, D), BF16), vm((SLOTS, 2 * S, D), BF16), vm((2 * S, D), F32),
            vm((2, HALF, S), BF16), vm((32, S), F32),
            vm((SLOTS, 3 * QW, D), BF16), vm((D, D), BF16), vm((SLOTS, D, D), BF16), vm((SLOTS, D, D), BF16),
            vm((SLOTS, 8, D), F32), vm((8, D), F32),
            vm((3, D, D), BF16), vm((3, D, D), BF16), vm((2, D, D), BF16), vm((2, D, D), BF16),
            vm((2, 3, D, 256), BF16), vm((6 * ROWS, D), BF16),
            vm((8, D), F32),
            vm((SLOTS, 8, D), F32), vm((2, 8, D), F32), vm((2, 8, D), F32), vm((8, D), F32), vm((8, D), F32),
            vm((8, D), F32), vm((3, 8, D), F32),
            vm((SLOTS, 1, D), F32), vm((2, 1, D), F32), vm((2, 1, D), F32), vm((1, D), F32), vm((1, D), F32),
            vm((1, D), F32), vm((3, 1, D), F32),
            vm((SLOTS, S), jnp.int32), vm((D,), BF16), vm((2, QW), BF16), vm((SLOT_HEADS, 32), BF16),
            vm((D,), BF16), vm((D,), F32), vm((D,), F32), vm((D,), BF16), vm((D,), F32), vm((D,), F32),
            vm((3, ROWS, D), F32), vm((ROWS, 256), F32), vm((2, 8, D), F32), dma((3,)), dma((10,)), dma((5, 2)), dma((5, 2)), dma((1,)), dma((4,)),
            dma((12,)), dma((1,)), dma((len(ITEMS), 6)), dma((1,)), dma((4,)), dma((3,)), dma((3,)),
            dma((2,)), dma((sum({"x": 3, "y": 4, "z": 6}[k] for k in KINDS),)), dma((14,)), dma((14,)), pltpu.SemaphoreType.REGULAR((6,)),
        ],
        compiler_params=pltpu.CompilerParams(
            vmem_limit_bytes=int(63.5 * (1 << 20)), collective_id=0, has_side_effects=True
        ),
    )(*args)


def hand_out(
    oc_in, og_in, gc_in, gg_in, gw_hbm, gwo_hbm, sm_hbm,
    oc, og, gc, gg, g_qkv, g_bias, g_attn, b_attn, n1g, n1s, g_in, b_in, g_out, b_out, n2g, n2s, g_table,
    wide, narrow, gw, gwo, sm, v_qkv, v_bias, v_attn, lines, v_table, sems,
):
    def moves(pairs, base):
        copies = [pltpu.make_async_copy(src, dst, sems.at[base + k]) for k, (src, dst) in enumerate(pairs)]
        for copy in copies:
            copy.start()
        return copies

    smalls = moves(((sm_hbm, sm), (gwo_hbm, gwo), (gw_hbm, gw)), 0)
    vias = (wide.at[0], wide.at[1], narrow.at[0], narrow.at[1])
    rows_in = moves(tuple(zip((gc_in, gg_in, oc_in, og_in), vias)), 3)
    for copy in smalls:
        copy.wait()
    v_attn[...] = gwo[:, 0:QW].T
    for k in range(3):
        v_qkv[k, :, 0:2 * HD] = gw[2, :, 2 * HD * k:2 * HD * k + 2 * HD]
        v_qkv[k, :, 2 * HD:QW] = gw[2, :, D // 2 + HD * k:D // 2 + HD * k + HD]
    v_bias[0:1] = sm[1, 0:1, 0:QW]
    v_bias[1:2] = sm[1, 0:1, QW:2 * QW]
    for k in range(SLOT_HEADS):
        v_table[k:k + 1] = sm[1, 0:1, 2 * QW + 32 * k:2 * QW + 32 * k + 32]
    for k, line in enumerate(lines):
        line[...] = sm[0, k:k + 1].reshape(D)
    outs = moves(
        ((gw.at[0], g_out), (gw.at[1], g_in), (v_qkv, g_qkv), (v_attn, g_attn), (v_bias, g_bias), (v_table, g_table))
        + tuple(zip(lines, (b_in, b_attn, n1g, n1s, b_out, n2g, n2s))),
        7,
    )
    for k, (copy, via, dst) in enumerate(zip(rows_in, vias, (gc, gg, oc, og))):
        copy.wait()
        outs += moves(((via, dst),), 20 + k)
    for copy in outs:
        copy.wait()


def local(
    stride,
    content, query_stream, cot_content, cot_query, doc_lengths, rank_order, pred_counts, w_qkv, bias_qv,
    w_attn_out, b_attn_out, norm1_gain, norm1_shift, w_in, b_in, w_out, b_out, norm2_gain, norm2_shift, rel_table,
):
    out_c, out_g, gc, gg, _, _, gw, gwo, sm = layer(
        stride, doc_lengths, pred_counts, content, query_stream, cot_content, cot_query,
        jnp.transpose(w_qkv, (0, 2, 1)).reshape(3 * QW, D), w_attn_out, w_in, w_out,
        rank_order, b_in, bias_qv, rel_table.T, b_attn_out, norm1_gain, norm1_shift, b_out, norm2_gain, norm2_shift,
    )
    if stride > 1:
        groups = [list(range(k * stride, k * stride + stride)) for k in range(8)]
        gw = lax.psum_scatter(gw, "dp", scatter_dimension=1, axis_index_groups=groups, tiled=True)
        gwo = lax.psum_scatter(gwo, "dp", scatter_dimension=0, axis_index_groups=groups, tiled=True)
        sm = lax.psum(sm, "dp") / 8.0
    rows = gw.shape[1]
    sd = jax.ShapeDtypeStruct
    hbm = pl.BlockSpec(memory_space=pl.ANY)
    vm = pltpu.VMEM
    line = sd((D,), F32)
    outs = pl.pallas_call(
        hand_out,
        out_shape=(
            sd((S, D), BF16), sd((S, D), BF16), sd((S, D), F32), sd((S, D), F32),
            sd((3, rows, QW), F32), sd((2, QW), F32), sd((QW, rows), F32), line, line, line,
            sd((rows, D), F32), line, sd((rows, D), F32), line, line, line, sd((SLOT_HEADS, 32), F32),
        ),
        in_specs=[hbm] * 7,
        out_specs=[hbm] * 17,
        scratch_shapes=[
            vm((2, S, D), F32), vm((2, S, D), BF16), vm((3, rows, D), F32), vm((rows, 256), F32), vm((2, 8, D), F32),
            vm((3, rows, QW), F32), vm((2, QW), F32), vm((QW, rows), F32), [vm((D,), F32)] * 7,
            vm((SLOT_HEADS, 32), F32), pltpu.SemaphoreType.DMA((24,)),
        ],
        compiler_params=pltpu.CompilerParams(vmem_limit_bytes=int(63.5 * (1 << 20))),
    )(out_c, out_g, gc, gg, gw, gwo, sm)
    outs = list(outs)
    outs[12] = outs[12].T
    outs[16] = outs[16].T
    return tuple(outs)


def solution(mesh):
    in_specs = (
        P(("dp", "tensor"), None),
        P(("dp", "tensor"), None),
        P(("dp", "tensor"), None),
        P(("dp", "tensor"), None),
        P("dp", None),
        P("dp", None),
        P("dp"),
        P(None, None, "tensor"),
        P(None, "tensor"),
        P("tensor", None),
        P(),
        P(),
        P(),
        P(None, "tensor"),
        P("tensor"),
        P("tensor", None),
        P(),
        P(),
        P(),
        P(None, "tensor"),
    )
    out_specs = (
        P(("dp", "tensor"), None),
        P(("dp", "tensor"), None),
        P(("dp", "tensor"), None),
        P(("dp", "tensor"), None),
        P(None, "dp", "tensor"),
        P(None, "tensor"),
        P("tensor", "dp"),
        P(),
        P(),
        P(),
        P("dp", "tensor"),
        P("tensor"),
        P("tensor", "dp"),
        P(),
        P(),
        P(),
        P(None, "tensor"),
    )
    stride = mesh.shape["dp"] // 8
    return jax.shard_map(functools.partial(local, stride), mesh=mesh, in_specs=in_specs, out_specs=out_specs, check_vma=False)
```

```python
import functools

import jax
import jax.numpy as jnp
from jax import lax
from jax.experimental import pallas as pl
from jax.experimental.pallas import tpu as pltpu
from jax.sharding import PartitionSpec as P

EDGES = (1, 2, 3, 4, 5, 6, 7, 8, 12, 16, 23, 32, 46, 64, 91)
EPSILON = 1e-05
F32 = jnp.float32
BF16 = jnp.bfloat16
S = 512
HALF = 256
D = 768
HD = 64
SLOTS = 4
SLOT_HEADS = 3
QW = SLOT_HEADS * HD
NEGATIVE = -1e30
ROWS = D // 8
HROWS = D // 2
MESH = pl.DeviceIdType.MESH
ITEMS = (
    (0, 0, 64, 0, 32),
    (0, 64, 80, 0, 48),
    (1, 0, 48, 16, 16),
    (2, 0, 96, 32, 32),
    (2, 96, 96, 32, 32),
    (3, 0, 96, 32, 32),
    (3, 96, 96, 64, 16),
)
FORWARD = {
    "p0": (("s", 1),),
    "p1": (("K", 0),),
    "a01": (("s", 0), ("k", 0),),
    "a02": (("s", 2), ("x", 1), ("K", 3),),
    "a10": (("K", 1),),
    "a11": (("s", 4), ("x", 0),),
    "a12": (("K", 2), ("x", 2), ("s", 3), ("m", 1),),
    "a20": (("m", 0), ("m", 2), ("s", 5), ("x", 4), ("l", 1), ("l", 0), ("w", 0),),
    "a22": (("x", 3), ("u", 2), ("k", 1),),
    "a30": (("l", 2), ("w", 1), ("c", 0), ("s", 6),),
    "a32": (("m", 4),),
    "o0": (("x", 5), ("c", 1),),
    "o2": (("k", 2),),
    "f01": (("m", 3), ("v", 2),),
    "f10": (("x", 6), ("u", 3),),
    "f12": (("l", 4),),
    "f20": (("l", 3), ("w", 2),),
    "f30": (("c", 2),),
    "f31": (("m", 5),),
    "f32": (("m", 6), ("v", 3),),
    "g1": (("k", 3),),
    "g2": (("l", 6), ("l", 5), ("w", 3),),
    "g3": (("c", 3),),
}
KINDS = "xyzxyzxxyzyx"
BACKWARD = {
    "gb2b": (("A1", "YA"),),
    "gb1a": (("A2", "ZA2"), ("A0", "XA"),),
    "tr": (("B1", "YA"), ("B0", "XA"), ("A1", "YF"),),
    "do": (("A0", "XL"), ("A2", "ZM"),),
    "p3a": (("A2", "ZA0"), ("B0", "XL"),),
    "p2a": (("B2", "ZA2"),),
    "p2b": (("B1", "YF"),),
    "p2c": (("B2", "ZA0"), ("A2", "ZF"),),
    "p1b": (("B2", "ZM"),),
    "p0a": (("W", "XA"),),
    "q2a": (("C2", "ZA2"), ("B2", "ZF"), ("C1", "YA"),),
    "q1a": (("W", "XL"),),
    "q1b": (("C0", "XA"), ("A0", "FN"),),
    "q0b": (("A2", "FN"), ("C2", "ZM"), ("C1", "YF"), ("C2", "ZA0"),),
    "t0": (("D0", "YA"),),
    "t2": (("C0", "XL"), ("D1", "XA"),),
    "t3": (("C2", "ZF"),),
    "t4": (("A1", "FN"),),
    "t5": (("D0", "YF"), ("B2", "FN"),),
    "t6": (("W", "FN"), ("D1", "XL"),),
    "t7": (("C0", "FN"),),
    "t8": (("D0", "FN"), ("C1", "FN"), ("B0", "FN"),),
    "t9": (("B1", "FN"), ("C2", "FN"), ("D1", "FN"),),
}


def nn(a, b):
    return jnp.dot(a, b, preferred_element_type=F32)


def nt(a, b):
    return lax.dot_general(a, b, (((1,), (1,)), ((), ())), preferred_element_type=F32)


def tn(a, b):
    return lax.dot_general(a, b, (((0,), (0,)), ((), ())), preferred_element_type=F32)


def iota(shape, axis):
    return lax.broadcasted_iota(jnp.int32, shape, axis)


def bucket_onehot():
    lanes = iota((32, S), 1)
    offset = jnp.where(lanes < HALF, -lanes, S - lanes)
    distance = jnp.abs(offset)
    bucket = jnp.where(offset > 0, 16, 0)
    for edge in EDGES:
        bucket = bucket + (distance >= edge).astype(jnp.int32)
    return (bucket == iota((32, S), 0)).astype(F32)


def gelu_pair(v):
    w = v * 0.7071067811865476
    cdf = 0.5 + 0.5 * lax.erf(w)
    return v * cdf, cdf + w * jnp.exp2(w * w * -1.4426950408889634) * 0.5641895835477563


def row_mean(v):
    return jnp.sum(v, axis=-1, keepdims=True) * (1.0 / D)


def col_sum(v):
    return jnp.sum(v, axis=0, keepdims=True)


def kernel(
    stride,
    dl, pc, x_hbm, g_hbm, cc_hbm, cg_hbm, wq_in, wo_in, wi_in, w2_in, rank_hbm,
    b_in_hbm, bias_hbm, table_hbm, b_attn_hbm, n1g_hbm, n1s_hbm, b_out_hbm, n2g_hbm, n2s_hbm,
    oc_hbm, og_hbm, gc_hbm, gg_hbm, stash, kept, g_out, gw_out, sm_out,
    perm, unperm, xin, hid, tA, tB, attn, qkv, qg, xhat, rstd1, act, dg, acc,
    mask, lines, wq, wo, wi, w2, wsm, vectors,
    ga, gb, rca, rcb, first_in, second_a, shared, early, e_core, e_part, e_x, e_y, e_sum, e_z, late_x, l_core, l_part, l_x, l_y, l_sum, l_z,
    rank, b_in, bias_qv, table_in, b_attn_in, n1g_in, n1s_in, b_out_in, n2g_in, n2s_in, g_res, g_w, sm_res, osem, isem, gs, gr, ks, kr,
    lsem, xs, xr, cs, cr, ss, sr, os, orr, ps, pr, credit,
):
    b_attn, n1g, n1s, b_out, n2g, n2s = (vectors.at[k:k + 1] for k in range(6))
    text = diag = lines
    t = lax.axis_index("tensor")
    d = lax.axis_index("dp")
    yb = lax.rem(lax.div(d, stride), 2)
    zb = lax.rem(lax.div(d, 2 * stride), 4)
    zbit = lax.rem(zb, 2)
    z_of = (zb, zb + 1 - 2 * zbit, lax.rem(zb + 2, 4), 3 - zb)
    core = (d, t + 1 - 2 * lax.rem(t, 2))
    xdev = (d, lax.rem(t + 2, 4))
    ydev = (d + stride - 2 * stride * yb, t)
    zdev = [None] + [(d + 2 * stride * (z_of[k] - zb), t) for k in (1, 2, 3)]

    barrier = pltpu.get_barrier_semaphore()
    for who in (core, xdev, ydev, zdev[1], zdev[2], zdev[3]):
        pl.semaphore_signal(barrier, inc=1, device_id=who, device_id_type=MESH)

    def remote(src, dst, send, recv, who):
        return pltpu.make_async_remote_copy(
            src_ref=src, dst_ref=dst, send_sem=send, recv_sem=recv, device_id=who, device_id_type=MESH
        )

    parts = (
        (wq_in, lambda s, lo, n: wq.at[s, pl.ds(lo, n)], 3 * QW),
        (wo_in, lambda s, lo, n: wo.at[pl.ds(s * QW + lo, n)], QW),
        (wi_in, lambda s, lo, n: wi.at[s, pl.ds(lo, n)], D),
        (w2_in, lambda s, lo, n: w2.at[s, pl.ds(lo, n)], D),
    )
    items = ITEMS
    zl = zbit

    def spot(i, y, z, lo=0, n=None):
        p, first, count = items[i][:3]
        at = (2 * y + z) * (parts[p][2] // 4) + first + lo
        return pl.multiple_of(at, 16), count if n is None else n

    def x_copy(i):
        src, place, _ = parts[items[i][0]]
        lo, n = spot(i, yb, zl)
        return remote(src.at[pl.ds(lo, n)], place(2, lo, n), xs.at[0], xr.at[i, 0], xdev)

    def pass_on(i, k, at, slot, who):
        place = parts[items[i][0]][1]
        return remote(place(2, *at), place(slot, *at), xs.at[0], xr.at[i, k], who)

    def y_copy(i):
        return pass_on(i, 1, spot(i, yb, zl), 2, ydev)

    def z_copy(i):
        return pass_on(i, 2, spot(i, yb, zl), 2, zdev[1])

    def last_parts(i):
        _, _, n, nx, ny = items[i]
        src, place, _ = parts[items[i][0]]
        lo, count = spot(i, 1 - yb, 1 - zl, 0, nx)
        nz = n - nx - ny
        return (
            nx and (lambda: remote(src.at[pl.ds(lo, count)], place(2, lo, count), xs.at[0], xr.at[i, 5], xdev)),
            ny and (lambda: pass_on(i, 3, spot(i, yb, 1 - zl, nx, ny), 2, ydev)),
            nz and (lambda: pass_on(i, 4, spot(i, 1 - yb, zl, nx + ny, nz), 2, zdev[1])),
        )

    def begin(copy):
        if copy:
            copy().start()

    def x_start(i):
        x_copy(i).start()
        begin(last_parts(i)[0])

    def c_copy(p, k):
        place, n = parts[p][1:]
        if p < 2:
            at = 0, n
        else:
            y, z = ((yb, zl), (1 - yb, zl), (yb, 1 - zl), (1 - yb, 1 - zl))[k]
            at = pl.multiple_of((2 * y + z) * (n // 4), 16), n // 4
        return remote(place(2, *at), place(3, *at), ks.at[0], kr.at[p], core)

    def core_copy(p):
        src, place, n = parts[p]
        return remote(src, place(1, 0, n), cs.at[0], cr.at[p], core)

    def small_copy(k):
        return remote(wsm.at[2 if k == 3 else 0], wsm.at[k], ss.at[k - 1], sr.at[k - 1], (core, xdev, core)[k - 1])

    def own_copy(p):
        src, place, n = parts[p]
        return pltpu.make_async_copy(src, place(0, 0, n), lsem.at[2 + p])

    def arrived_x(i):
        x_copy(i).wait_recv()
        y_copy(i).start()
        z_copy(i).start()

    def arrived_yz(i):
        _, over_y, over_z = last_parts(i)
        y_copy(i).wait_recv()
        begin(over_z)
        z_copy(i).wait_recv()
        begin(over_y)

    def arrived_last(i):
        for copy in last_parts(i):
            if copy:
                copy().wait_recv()

    def drain(ref, sem):
        pltpu.make_async_copy(ref, ref, sem).wait()

    def arrived_core(p):
        place, n = parts[p][1:]
        drain(place(3, 0, n), kr.at[p])

    def to_core(p, which):
        for k in (0,) if p < 2 else which:
            c_copy(p, k).start()

    def hook(name):
        steps = {
            "s": x_start, "x": arrived_x, "m": arrived_yz, "l": arrived_last, "c": arrived_core,
            "u": lambda p: to_core(p, (0,)), "v": lambda p: to_core(p, (1, 2)), "w": lambda p: to_core(p, (3,)),
            "K": lambda p: core_copy(p).start(), "k": lambda p: core_copy(p).wait_recv(),
        }
        for what, which in FORWARD.get(name, ()):
            steps[what](which)

    def at_slot(table, run, s, before, behind):
        for k in range(SLOTS):
            name = before + str(k) + behind
            if name in table:
                pl.when(s == k)(lambda name=name: run(name))

    def hook_at(s, before, behind=""):
        at_slot(FORWARD, hook, s, before, behind)

    def fetch(one, two):
        return [
            pltpu.make_async_copy(one, xin.at[0:S], lsem.at[0]),
            pltpu.make_async_copy(two, xin.at[S:2 * S], lsem.at[1]),
        ]

    def kept_copy(back):
        ends = (kept, tB) if back else (tB, kept)
        return pltpu.make_async_copy(ends[0], ends[1], lsem.at[11])

    def stash_copy(s, back):
        ends = (stash.at[s], dg.at[s]) if back else (dg.at[s], stash.at[s])
        return pltpu.make_async_copy(ends[0], ends[1], lsem.at[7 + s])

    rows_in = fetch(x_hbm, g_hbm)
    for copy in rows_in:
        copy.start()
    own_copy(0).start()
    inputs_in = [
        pltpu.make_async_copy(src, dst, isem.at[k])
        for k, (src, dst) in enumerate((
            (rank_hbm, rank), (b_in_hbm, b_in), (bias_hbm, bias_qv), (table_hbm, table_in), (b_attn_hbm, b_attn_in),
            (n1g_hbm, n1g_in), (n1s_hbm, n1s_in), (b_out_hbm, b_out_in), (n2g_hbm, n2g_in), (n2s_hbm, n2s_in),
        ))
    ]
    for copy in inputs_in:
        copy.start()
    pl.semaphore_wait(barrier, 6)
    hook("p0")
    for copy in inputs_in:
        copy.wait()
    for k, ref in enumerate((b_attn_in, n1g_in, n1s_in, b_out_in, n2g_in, n2s_in)):
        vectors[k:k + 1] = ref[...].astype(F32).reshape(1, D)
    wsm[0] = jnp.zeros((8, D), F32)
    wsm[0, 0:1] = b_in[...].astype(F32).reshape(1, D)
    wsm[0, 1:3, 0:QW] = bias_qv[...].astype(F32)
    wsm[0, 3:3 + SLOT_HEADS, 0:32] = table_in[...].astype(F32)
    for k in (1, 2):
        small_copy(k).start()
    for p in (1, 2, 3):
        own_copy(p).start()
    shared[...] = jnp.zeros(shared.shape, F32)
    early[...] = jnp.zeros(early.shape, F32)
    late_x[...] = jnp.zeros(late_x.shape, F32)

    end = jnp.int32(0)
    start = jnp.int32(0)
    ends = []
    for k in range(8):
        length = dl[t, k]
        start = jnp.where(length == HALF, end, start)
        end = end + length
        ends.append(end)
    limit = (S - pc[t]).astype(F32)
    rows = iota((S, 1), 0)
    lanes = iota((1, S), 1)
    source_r = (rows + start) & (S - 1)
    source_l = (lanes + start) & (S - 1)
    perm[...] = jnp.where(source_r == lanes, 1.0, 0.0).astype(BF16)
    unperm[...] = jnp.where(((rows - start) & (S - 1)) == lanes, 1.0, 0.0).astype(BF16)
    hook("p1")
    doc_r = jnp.zeros((S, 1), F32)
    doc_l = jnp.zeros((1, S), F32)
    for e in ends:
        doc_r = doc_r + jnp.where(source_r >= e, 1.0, 0.0)
        doc_l = doc_l + jnp.where(source_l >= e, 1.0, 0.0)
    rank_row = rank[pl.ds(t, 1), :]
    sub = iota((16, S), 0)
    pieces = jnp.where(sub == 0, rank_row >> 4, jnp.where(sub == 1, rank_row & 15, 0))
    pieces = pieces.astype(F32).astype(BF16)
    ranks = nt(pieces, perm[...])
    rank_l = 16.0 * ranks[0:1] + ranks[1:2]
    ranks = nt(perm[...], pieces)
    rank_r = 16.0 * ranks[:, 0:1] + ranks[:, 1:2]
    lim_c = jnp.maximum(limit - 1.0, rank_l)
    lim_g = jnp.maximum(limit, rank_l) - 1.0
    for b in range(2):
        c = slice(HALF * b, HALF * b + HALF)
        same = doc_r[c] == doc_l[:, c]
        mask[b, :, 0:HALF] = jnp.where(same & (rank_r[c] <= lim_c[:, c]), 0.0, NEGATIVE).astype(BF16)
        mask[b, :, HALF:S] = jnp.where(same & (rank_r[c] <= lim_g[:, c]), 0.0, NEGATIVE).astype(BF16)
    onehot = bucket_onehot()

    def transposed(dst, src):
        for st in range(2):
            r = slice(st * S, st * S + S)
            dst[:, r] = src[r].T

    def permuted(dst):
        for copy in rows_in:
            copy.wait()
        for st in range(2):
            r = slice(st * S, st * S + S)
            for f in (slice(0, HROWS), slice(HROWS, D)):
                dst[r, f] = nn(perm[...], xin[r, f]).astype(BF16)

    xp = hid
    permuted(xp)
    own_copy(0).wait()

    def prob_at(s, h, b, st):
        k = 2 * b + st
        return dg.at[s, k * HALF:k * HALF + HALF, pl.ds(pl.multiple_of(h * HALF, HALF), HALF)]

    @pl.loop(0, SLOTS)
    def _(s):

        @pl.when(s == 2)
        def _():
            transposed(tB, xp)
            kept_copy(False).start()
            for st in range(2):
                r = slice(st * S, st * S + S)
                attn[r, 0:2 * QW] = nt(unperm[...], tA[0:2 * QW, r]).astype(BF16)

        hook_at(s, "a", "0")

        @pl.when(s == 1)
        def _():
            small_copy(1).wait_recv()
            small_copy(2).wait_recv()
            small_copy(3).start()

        pl.when(s == 3)(lambda: small_copy(3).wait_recv())

        small = wsm[s].astype(BF16)
        text[pl.ds(pl.multiple_of(8 * s, 8), 8), :] = nn(small[:, 0:32], onehot.astype(BF16))
        sel = jnp.where(iota((8, 128), 0) == 1, 1.0, 0.0).astype(BF16)
        bq = tn(small[:, 0:QW], sel)[:, 0:1]
        sel = jnp.where(iota((8, 128), 0) == 2, 1.0, 0.0).astype(BF16)
        bv = tn(small[:, 0:QW], sel)[:, 0:1]
        r = nt(wq[s], xp[0:S])
        qkv[s, 0:QW] = ((r[0:QW] + bq).astype(BF16) * 0.125).astype(BF16)
        qkv[s, QW:2 * QW] = r[QW:2 * QW].astype(BF16)
        qkv[s, 2 * QW:3 * QW] = (r[2 * QW:3 * QW] + bv).astype(BF16)
        qg[s] = ((nt(wq[s, 0:QW], xp[S:2 * S]) + bq).astype(BF16) * 0.125).astype(BF16)

        hook_at(s, "a", "1")

        units = [(h, b, st) for h in range(SLOT_HEADS) for b in range(2) for st in range(2)]

        def score_at(h, b, st):
            k = 2 * b + st
            return slice(k * HALF, k * HALF + HALF), slice(h * HALF, h * HALF + HALF)

        def block_of(b):
            return slice(HALF * b, HALF * b + HALF)

        for h, b, st in units:
            q = qkv if st == 0 else qg
            lo = h * HD
            acc[score_at(h, b, st)] = tn(qkv[s, QW + lo:QW + lo + HD, block_of(b)], q[s, lo:lo + HD, block_of(b)])

        for h in range(SLOT_HEADS):
            rowvec = text[pl.ds(8 * s + 3 + h, 1), :]
            rolled = pltpu.roll(jnp.broadcast_to(rowvec, (HALF, S)), 0, 1, stride=1, stride_axis=0)
            bias = rolled[:, 0:HALF]
            for b in range(2):
                for st in range(2):
                    sc = acc[score_at(h, b, st)] + bias + mask[b, :, st * HALF:st * HALF + HALF].astype(F32)
                    e = jnp.exp(sc - jnp.max(sc, axis=0, keepdims=True))
                    p = (e * (1.0 / jnp.sum(e, axis=0, keepdims=True))).astype(BF16)
                    dg[(s,) + score_at(h, b, st)] = p

        hook_at(s, "a", "2")

        for h, b, st in units:
            lo = h * HD
            o = nn(qkv[s, 2 * QW + lo:2 * QW + lo + HD, block_of(b)], dg[(s,) + score_at(h, b, st)])
            to = slice(st * S + HALF * b, st * S + HALF * b + HALF)
            tA[pl.ds(pl.multiple_of(s * QW + lo, HD), HD), to] = o.astype(BF16)

        for k in range(SLOTS):
            @pl.when(s == k)
            def _():
                stash_copy(k, False).start()

    hook("o0")
    own_copy(1).wait()
    for st in range(2):
        r = slice(st * S, st * S + S)
        attn[r, 2 * QW:] = nt(unperm[...], tA[2 * QW:, r]).astype(BF16)
    hook("o1")
    for r in (slice(k * HALF, k * HALF + HALF) for k in range(4)):
        res = xin[r].astype(F32) + nn(attn[r], wo[...]) + b_attn[...]
        cen = res - row_mean(res)
        rs = lax.rsqrt(row_mean(cen * cen) + EPSILON)
        xh = cen * rs
        xhat[r] = xh.astype(BF16)
        rstd1[r] = rs
        hid[r] = (xh * n1g[...] + n1s[...]).astype(BF16)
    kept_copy(False).wait()
    transposed(tB, hid)
    rows_in = fetch(cc_hbm, cg_hbm)
    for copy in rows_in:
        copy.start()

    own_copy(2).wait()
    own_copy(3).wait()
    hook("o2")

    @pl.loop(0, SLOTS)
    def _(s):
        for k in range(SLOTS):
            @pl.when(s == k)
            def _():
                stash_copy(k, False).wait()
        for j in range(0, D, 256):
            hook_at(s, "f", str(j // 256))
            a, g = gelu_pair(nn(hid[...], wi[s, :, j:j + 256]) + wsm[s, 0:1, j:j + 256])
            act[s, :, j:j + 256] = a.astype(BF16)
            dg[s, :, j:j + 256] = g.astype(BF16)

    hook("g0")
    for j in range(0, D, 256):
        acc[:, j:j + 256] = nn(act[0], w2[0, :, j:j + 256])

    @pl.loop(1, SLOTS)
    def _(s):
        hook_at(s, "g")
        for j in range(0, D, 256):
            acc[:, j:j + 256] += nn(act[s], w2[s, :, j:j + 256])

    for copy in rows_in:
        copy.wait()

    @pl.loop(0, 4, unroll=2)
    def _(i):
        r = pl.ds(pl.multiple_of(i * HALF, HALF), HALF)
        res = hid[r, :].astype(F32) + acc[r, :] + b_out[...]
        cen = res - row_mean(res)
        rs = lax.rsqrt(row_mean(cen * cen) + EPSILON)
        xh = cen * rs
        cot = xin[r, :].astype(F32)
        hid[r, :] = (xh * n2g[...] + n2s[...]).astype(BF16)
        dxh = cot * n2g[...]
        dres = rs * (dxh - row_mean(dxh) - xh * row_mean(dxh * xh))
        acc[r, :] = dres
        xin[r, :] = dres.astype(BF16)
        shared[3:4] += col_sum(dres)
        shared[4:5] += col_sum(cot * xh)
        shared[5:6] += col_sum(cot)

    dlow = xin
    transposed(tA, dlow)
    rows_out = [
        pltpu.make_async_copy(hid.at[0:S], oc_hbm, lsem.at[0]),
        pltpu.make_async_copy(hid.at[S:2 * S], og_hbm, lsem.at[1]),
    ]
    for copy in rows_out:
        copy.start()

    def rows_at(lo, n):
        return pl.ds(pl.multiple_of(lo, ROWS), n)

    own_half = rows_at(yb * HROWS, HROWS)
    other_half = rows_at((1 - yb) * HROWS, HROWS)
    zlow, zhigh = zbit, lax.div(zb, 2)
    z_own = rows_at(zlow * HROWS, HROWS)
    z_other = rows_at((1 - zlow) * HROWS, HROWS)
    zy_own = rows_at(zlow * HROWS + yb * 2 * ROWS, 2 * ROWS)
    zy_other = rows_at(zlow * HROWS + (1 - yb) * 2 * ROWS, 2 * ROWS)
    zyz_own = rows_at(zlow * HROWS + yb * 2 * ROWS + zhigh * ROWS, ROWS)
    zyz_other = rows_at(zlow * HROWS + yb * 2 * ROWS + (1 - zhigh) * ROWS, ROWS)

    def block(k):
        return rows_at(yb * HROWS + z_of[k] * ROWS, ROWS)

    def store_at(dst, lo, value, z_first):
        for b in range(8):
            y, z = b % 2, b // 2
            to = ((z % 2) * 4 + y * 2 + z // 2 if z_first else y * 4 + z) * ROWS
            dst[to:to + ROWS, lo:lo + value.shape[1]] = value[b * ROWS:b * ROWS + ROWS, :]

    def store(dst, lead, lo, value, z_first):
        for b in range(8):
            y, z = b % 2, b // 2
            to = ((z % 2) * 4 + y * 2 + z // 2 if z_first else y * 4 + z) * ROWS
            dst[lead, to:to + ROWS, lo:lo + value.shape[1]] = value[b * ROWS:b * ROWS + ROWS, :]

    def add(dst, at, *sources):
        at = slice(None) if at is None else at
        total = dst[at, :]
        for src in sources:
            total = total + src[...]
        dst[at, :] = total

    class Lines:
        def __init__(self, base, given, over_core, part, over_x, over_y, whole_y, over_z):
            self.base, self.given, self.over_core, self.part = base, given, over_core, part
            self.over_x, self.over_y, self.whole_y, self.over_z = over_x, over_y, whole_y, over_z

        def send(self, k):
            sem = ps.at[self.base + k], pr.at[self.base + k]
            if k < 2:
                return remote(self.given.at[(3, 1)[k]], self.over_core.at[k], *sem, core)
            if k == 2:
                return remote(self.part.at[1], self.over_x, *sem, xdev)
            if k == 3:
                return remote(self.part.at[0], self.over_y, *sem, ydev)
            return remote(self.whole_y, self.over_z.at[k - 4], *sem, zdev[k - 3])

        def to_x(self):
            self.send(0).wait_recv()
            self.part[1] = self.given[2] + self.over_core[0]
            self.send(2).start()

        def to_y(self):
            self.send(1).wait_recv()
            self.send(2).wait_recv()
            self.part[0] = self.given[0] + self.over_core[1] + self.over_x[...]
            self.send(3).start()

        def to_z(self):
            self.send(3).wait_recv()
            self.whole_y[...] = self.part[0] + self.over_y[...]
            for k in (4, 5, 6):
                self.send(k).start()

        def total(self):
            for k in (4, 5, 6):
                self.send(k).wait_recv()
            return self.whole_y[...] + self.over_z[0] + self.over_z[1] + self.over_z[2]

    early_sum = Lines(0, early, e_core, e_part, e_x, e_y, e_sum, e_z)
    late_sum = Lines(7, late_x, l_core, l_part, l_x, l_y, l_sum, l_z)

    def piece(z, lo=0):
        return slice(lo, lo + 3 * ROWS) if z == 0 else slice(lo + (z - 1) * ROWS, lo + z * ROWS)

    class Chunk:
        def __init__(self, kind, index, even, parts, out, ends=None):
            self.kind, self.ends = kind, ends
            self.n, self.even, self.out = index, even, out
            self.base = sum({"x": 3, "y": 4, "z": 6}[KINDS[k + (k > 5)]] for k in range(index)) if index < 11 else 0
            if index == 11:
                self.base = sum({"x": 3, "y": 4, "z": 6}[KINDS[k]] for k in range(12) if k != 6)
            slots = {"z1": 0, "z2": 0, "z3": 0}
            self.moves = {}
            for k, (name, src, dst, who) in enumerate(parts):
                if name not in slots:
                    slots[name] = len(slots) - (3 if kind == "z" else 2)
                self.moves[name] = (src, dst, slots[name], who)

        def move(self, name):
            src, dst, k, who = self.moves[name]
            return remote(src, dst, os.at[self.n // 6], orr.at[self.base + k], who)

        def go(self, *names):
            for name in names:
                self.move(name).start()

        def here(self, *names):
            for name in names:
                self.move(name).wait_recv()
            return [self.moves[name][1] for name in names]

        def finish(self, at, *names):
            total = self.even[0][at, :].astype(F32)
            if len(names) > 1:
                drain(self.ends, orr.at[self.base])
            else:
                self.here(*names)
            for ref in (self.moves[name][1] for name in names):
                total = total + ref[...].astype(F32)
            self.out[...] = total

    first, second = pl.ds(0, D // 2), pl.ds(D // 2, D // 2)
    third = [pl.ds(256 * k, 256) for k in range(3)]

    def x_flow(index, even, rx, ry, rz, out):
        e0, e2 = even
        parts = [("x", e2, rx, xdev), ("y", e0.at[other_half], ry, ydev)]
        parts += [("z%d" % k, e0.at[block(k)], rz(k), zdev[k]) for k in (1, 2, 3)]
        return Chunk("x", index, even, parts, out, rz(0))

    def y_flow(index, even, rx, ry, rz, out):
        e0, e2 = even
        parts = [
            ("y2", e2.at[other_half], ry[1], ydev), ("y0", e0.at[other_half], ry[0], ydev),
            ("x", e2.at[own_half], rx, xdev),
        ]
        parts += [("z%d" % k, e0.at[block(k)], rz(k), zdev[k]) for k in (1, 2, 3)]
        return Chunk("y", index, even, parts, out, rz(0))

    def z_flow(index, even, rz, ry, rx, rh, out):
        e0, e2 = even
        parts = [
            ("l2", e2.at[z_other], rz[1], zdev[1]), ("l0", e0.at[z_other], rz[0], zdev[1]),
            ("y2", e2.at[zy_other], ry[1], ydev), ("y0", e0.at[zy_other], ry[0], ydev),
            ("x", e2.at[zy_own], rx, xdev), ("h", e0.at[zyz_other], rh, zdev[2]),
        ]
        return Chunk("z", index, even, parts, out)

    def c_even(cols):
        return act.at[0, 0:D, cols], act.at[2, 0:D, cols]

    def pair(ref, cols):
        return ref.at[0, :, cols], ref.at[1, :, cols]

    def halves(ref):
        return ref.at[0:HROWS], ref.at[HROWS:D]

    def late(slot, k, lo, n):
        return w2.at[slot, lo:lo + n, third[k]]

    chunks = []
    for n, (g, rc) in enumerate(((ga, rca), (gb, rcb))):
        place = (lambda k, lo, c: second_a.at[lo:lo + c, third[k]]) if n == 0 else (lambda k, lo, c: late(0, k, lo, c))
        blocks = lambda k: lambda z: wi.at[n, piece(z), third[k]]
        for k in range(3):
            recv = first_in.at[n, k]
            base = 3 * n + k, pair(g, third[k])
            out = g_res.at[n, :, third[k]]
            kind = KINDS[3 * n + k]
            if kind == "x":
                chunks.append(x_flow(*base, recv, place(k, 0, HROWS), blocks(k), out))
            elif kind == "y":
                chunks.append(y_flow(*base, place(k, 0, HROWS), halves(recv), blocks(k), out))
            else:
                turns = place(k, 0, 2 * ROWS), place(k, 2 * ROWS, 2 * ROWS)
                chunks.append(z_flow(*base, halves(recv), turns, place(k, 4 * ROWS, 2 * ROWS), blocks(k)(1), out))

    def c_flow(index, k):
        kind = KINDS[index + 1]
        cols = pl.ds(128 * k, 128)
        a, b, out = w2.at[1, :, cols], w2.at[3, :, cols], g_res.at[2, :, cols]
        ends = lambda z: wi.at[3, piece(z), cols]
        if kind == "x":
            return x_flow(index, c_even(cols), a, b.at[0:HROWS], ends, out)
        if kind == "y":
            return y_flow(index, c_even(cols), b.at[0:HROWS], halves(a), ends, out)
        return z_flow(
            index, c_even(cols), halves(a), (b.at[0:2 * ROWS], b.at[2 * ROWS:4 * ROWS]),
            b.at[4 * ROWS:6 * ROWS], ends(1), out,
        )

    C0, C1, C2, D0, D1 = (c_flow(6 + k, k) for k in range(5))
    w_slots = [xhat.at[0:D, third[k]] for k in range(3)] + [hid.at[0:D, third[0]]]
    W = x_flow(
        11, (w_slots[0], w_slots[2]),
        w2.at[2, :, third[2]], wi.at[2, 0:HROWS, third[0]],
        lambda z: wi.at[2, piece(z, HROWS), third[0]], g_w,
    )

    A0, A1, A2, B0, B1, B2 = chunks
    named = dict(A0=A0, A1=A1, A2=A2, B0=B0, B1=B1, B2=B2, C0=C0, C1=C1, C2=C2, D0=D0, D1=D1, W=W)

    class Group:
        def __init__(self, index, even, odd, rc, *members):
            self.n, self.even, self.odd, self.rc, self.members = index, even, odd, rc, members

        def send(self, k):
            return remote(self.odd[k], self.rc[k], gs.at[self.n, k], gr.at[self.n, k], core)

        def sum(self, k):
            self.send(k).wait_recv()
            add(self.even[k], None, self.rc[k])
            for c in self.members:
                if k == 1:
                    c.go({"x": "x", "y": "y2", "z": "l2"}[c.kind])
                elif c.kind != "x":
                    c.go({"y": "y0", "z": "l0"}[c.kind])

        def steps(self):
            return (
                lambda: self.send(1).start(), lambda: self.sum(1), lambda: self.send(0).start(), lambda: self.sum(0),
            )

    def c_group(index, cols, *members):
        odd = act.at[1, 0:D, cols], act.at[3, 0:D, cols]
        return Group(index, c_even(cols), odd, pair(rca, cols), *members)

    every = pl.ds(0, D)
    GA = Group(0, pair(ga, every), (ga.at[2], ga.at[2]), pair(rca, every), A0, A1, A2)
    GB = Group(1, pair(gb, every), (gb.at[2], gb.at[2]), pair(rcb, every), B0, B1, B2)
    GC = c_group(2, first, C0, C1, C2)
    GD = c_group(3, pl.ds(D // 2, 256), D0, D1)
    GW = Group(
        4, (w_slots[0], w_slots[2]), (w_slots[1], w_slots[3]),
        (w2.at[2, :, third[0]], w2.at[2, :, third[1]]), W,
    )

    def buffer_of(s):
        odd = lax.rem(s, 2)
        return 2 * odd + (1 - odd) * lax.div(s, 2)

    def after(s, three, two, one, zero):
        for k, step in ((3, three), (2, two), (1, one), (0, zero)):
            pl.when(s == k)(step)

    def x_arrived(c):
        add(c.even[0], None, *c.here("x"))
        c.go("y")

    def x_last(c):
        add(c.even[0], own_half, *c.here("y"))
        c.go("z1", "z2", "z3")

    def y_arrived(c):
        add(c.even[1], own_half, *c.here("y2"))
        c.go("x")

    def y_final(c):
        add(c.even[0], own_half, *c.here("y0", "x"))
        c.go("z1", "z2", "z3")

    def z_arrived(c, k):
        add(c.even[1 if k == 2 else 0], z_own, *c.here("l%d" % k))
        c.go("y%d" % k)

    def z_middle(c):
        add(c.even[1], zy_own, *c.here("y2"))
        c.go("x")

    def z_final(c):
        add(c.even[0], zy_own, *c.here("y0", "x"))
        c.go("h")

    def steps_of(c):
        if c.kind == "x":
            return {"XA": lambda: x_arrived(c), "XL": lambda: x_last(c), "FN": lambda: c.finish(block(0), "z1", "z2", "z3")}
        if c.kind == "y":
            return {"YA": lambda: y_arrived(c), "YF": lambda: y_final(c), "FN": lambda: c.finish(block(0), "z1", "z2", "z3")}
        return {
            "ZA2": lambda: z_arrived(c, 2), "ZA0": lambda: z_arrived(c, 0), "ZM": lambda: z_middle(c),
            "ZF": lambda: z_final(c), "FN": lambda: c.finish(zyz_own, "h"),
        }

    def turn(name):
        for which, what in BACKWARD.get(name, ()):
            steps_of(named[which])[what]()

    def turn_at(s, before, behind=""):
        at_slot(BACKWARD, turn, s, before, behind)

    @pl.loop(0, SLOTS)
    def _(i):
        s = 3 - i

        pl.when(s == 1)(lambda: GA.send(1).wait_send())
        for k in range(3):
            value = nn(tA[...], act[s, :, 256 * k:256 * k + 256]).astype(BF16)
            store(ga, buffer_of(s), 256 * k, value, KINDS[k] == "z")

        def one():
            GA.send(0).start()
            GA.sum(1)

        pl.when(s == 3)(lambda: GA.send(1).start())
        pl.when(s == 1)(one)

    @pl.loop(0, SLOTS)
    def _(i):
        s = 3 - i
        turn_at(s, "gb", "a")
        for j in range(0, D, 256):
            low = (nt(dlow[...], w2[s, j:j + 256, :]) * dg[s, :, j:j + 256].astype(F32)).astype(BF16)
            dg[s, :, j:j + 256] = low
            early[s, 0:1, j:j + 256] = col_sum(low.astype(F32))

        pl.when(s == 3)(lambda: GA.sum(0))
        pl.when(s == 1)(lambda: GB.send(1).wait_send())
        turn_at(s, "gb", "b")
        for k in range(3):
            value = nn(tB[...], dg[s, :, 256 * k:256 * k + 256]).astype(BF16)
            store(gb, buffer_of(s), 256 * k, value, KINDS[3 + k] == "z")
        after(s, *GB.steps())
        turn_at(s, "gb", "c")
        for j in range(0, D, 256):
            acc[:, j:j + 256] += nt(dg[s], wi[s, j:j + 256, :])
        for k in range(SLOTS):
            @pl.when(s == k)
            def _():
                stash_copy(k, True).start()

    for sem in (xs, ks, cs):
        drain(w2.at[0:3], sem.at[0])
    for k in (1, 2, 3):
        small_copy(k).wait_send()
    for k, who in enumerate((core, xdev, ydev, zdev[1], zdev[2], zdev[3])):
        pl.semaphore_signal(credit.at[k], inc=1, device_id=who, device_id_type=MESH)

    turn("ln")
    @pl.loop(0, 4, unroll=2)
    def _(i):
        r = pl.ds(pl.multiple_of(i * HALF, HALF), HALF)
        dy = acc[r, :]
        xh = xhat[r, :].astype(F32)
        dxh = dy * n1g[...]
        dres = rstd1[r, :] * (dxh - row_mean(dxh) - xh * row_mean(dxh * xh))
        acc[r, :] = dres
        xin[r, :] = dres.astype(BF16)
        shared[0:1] += col_sum(dres)
        shared[1:2] += col_sum(dy * xh)
        shared[2:3] += col_sum(dy)

    for k in range(6):
        pl.semaphore_wait(credit.at[k], 1)
    turn("tr")
    transposed(tB, dlow)
    turn("da")
    early[0, 1:7] = shared[0:6]
    for k in range(3):
        early[k + 1, 1:7] = shared[0:6]
    early_sum.send(0).start()
    early_sum.send(1).start()
    for r in (slice(0, HROWS), slice(HROWS, D)):
        tA[r] = nt(wo[r], dlow[...]).astype(BF16)
    for copy in rows_out:
        copy.wait()
    turn("wo")
    for k in range(3):
        gwo = nn(tB[...], attn[:, 256 * k:256 * k + 256]).astype(BF16)
        for s in range(SLOTS):
            lo, hi = max(s * QW, 256 * k), min(s * QW + QW, 256 * k + 256)
            if lo < hi:
                ref, base = (xhat, 256 * s) if s < 3 else (hid, 0)
                store_at(ref, base + lo - s * QW, gwo[:, lo - 256 * k:hi - 256 * k], False)
    kept_copy(True).start()
    GW.send(1).start()
    GW.send(0).start()
    turn("do")
    for st in range(2):
        r = slice(st * S, st * S + S)
        for f in (slice(0, HROWS), slice(HROWS, D)):
            tA[f, r] = nt(tA[f, r], perm[...]).astype(BF16)
    GW.sum(1)
    turn("xp")
    turn("xt")
    kept_copy(True).wait()
    GW.sum(0)
    xpT = tB

    ones = jnp.ones((16, S), BF16)
    def head_backward(s, h):
        at = (lambda v, m: v) if isinstance(h, int) else pl.multiple_of
        row = at(h * HD, HD)
        column = pl.ds(at(h * HALF, HALF), HALF)
        qr, kr, vr = pl.ds(row, HD), pl.ds(QW + row, HD), pl.ds(2 * QW + row, HD)
        oT = pl.ds(pl.multiple_of(s * QW + row, HD), HD)
        block_of = [slice(0, HALF), slice(HALF, S)]

        def out_grad(b, st):
            return tA[oT, st * S + HALF * b:st * S + HALF * b + HALF]

        def unit(b, st):
            return s, slice((2 * b + st) * HALF, (2 * b + st) * HALF + HALF), column

        pairs = [(b, st) for b in range(2) for st in range(2)]
        dps = [tn(qkv[s, vr, block_of[b]], out_grad(b, st)) for b, st in pairs]
        dv = [sum(nt(out_grad(b, st), dg[unit(b, st)]) for st in range(2)).astype(BF16) for b in range(2)]
        total = None
        for (b, st), dp in zip(pairs, dps):
            pf = dg[unit(b, st)].astype(F32)
            ds = (pf * (dp - jnp.sum(dp * pf, axis=0, keepdims=True))).astype(BF16)
            dg[unit(b, st)] = ds
            total = ds.astype(F32) if total is None else total + ds.astype(F32)
        skewed = jnp.zeros((8, S), F32)
        for a in range(HALF // 8):
            wide = jnp.concatenate([total[8 * a:8 * a + 8, :], jnp.zeros((8, HALF), F32)], axis=1)
            skewed = skewed + (wide if a == 0 else pltpu.roll(wide, S - 8 * a, 1))
        flipped = jnp.concatenate([skewed[7 - i:8 - i] for i in range(8)], axis=0)
        diag[pl.ds(8 * s + h, 1), :] = col_sum(pltpu.roll(flipped, S - 7, 1, stride=1, stride_axis=0))
        grads = []
        for b in range(2):
            kT = qkv[s, kr, block_of[b]]
            d0, d1 = dg[unit(b, 0)], dg[unit(b, 1)]
            dk = nt(qkv[s, qr, block_of[b]], d0) + nt(qg[s, qr, block_of[b]], d1)
            grads.append((nn(kT, d0) * 0.125, nn(kT, d1) * 0.125, dk))
        for b in range(2):
            dq_c, dq_g, dk = grads[b]
            qkv[s, qr, block_of[b]] = dq_c.astype(BF16)
            qg[s, qr, block_of[b]] = dq_g.astype(BF16)
            qkv[s, kr, block_of[b]] = dk.astype(BF16)
            qkv[s, vr, block_of[b]] = dv[b]

    @pl.loop(0, SLOTS)
    def _(i):
        s = 3 - i
        for k in range(SLOTS):
            @pl.when(s == k)
            def _():
                stash_copy(k, True).wait()

        @pl.loop(0, 2)
        def _(h):
            pl.when(h == 0)(lambda: turn_at(s, "p", "a"))
            pl.when(h == 1)(lambda: turn_at(s, "p", "b"))
            head_backward(s, h)

        turn_at(s, "p", "c")
        gq = nt(xpT[:, 0:S], qkv[s, 0:2 * HD])
        extra = nt(xpT[:, S:2 * S], qg[s, 0:2 * HD])
        store(act, s, 0, (gq + extra).astype(BF16), KINDS[7] == "z")
        dkv = jnp.concatenate([qkv[s, k * QW:k * QW + 2 * HD] for k in (1, 2)], axis=0)
        dkv = nt(xpT[:, 0:S], dkv).astype(BF16)
        store(act, s, 2 * HD, dkv[:, 0:2 * HD], KINDS[8] == "z")
        store(act, s, 4 * HD, dkv[:, 2 * HD:], KINDS[9] == "z")

        three, two, one, zero = GC.steps()

        def with_three():
            three()
            early_sum.to_x()

        def with_two():
            two()
            early_sum.to_y()

        def with_one():
            one()
            early_sum.to_z()

        after(s, with_three, with_two, with_one, zero)

    @pl.loop(0, SLOTS)
    def _(i):
        s = 3 - i

        turn_at(s, "q", "a")
        head_backward(s, 2)
        turn_at(s, "q", "b")
        dqkv = jnp.concatenate([qkv[s, k * QW + 2 * HD:k * QW + QW] for k in range(3)], axis=0)
        extra = jnp.concatenate([qg[s, 2 * HD:QW], jnp.zeros((2 * HD, S), BF16)], axis=0)
        store(act, s, D // 2, (nt(xpT[:, 0:S], dqkv) + nt(xpT[:, S:2 * S], extra)).astype(BF16), False)

        late_x[s, :, 0:QW] = (nt(ones, qkv[s, 0:QW]) + nt(ones, qg[s]))[0:1]
        late_x[s, :, QW:2 * QW] = nt(ones, qkv[s, 2 * QW:3 * QW])[0:1]
        table = lax.dot_general(
            diag[pl.ds(pl.multiple_of(8 * s, 8), 8), :], onehot, (((1,), (1,)), ((), ())),
            precision=lax.Precision.HIGHEST, preferred_element_type=F32,
        )
        for k in range(SLOT_HEADS):
            late_x[s, :, 2 * QW + 32 * k:2 * QW + 32 * k + 32] = table[k:k + 1]

        three, two, one, zero = GD.steps()

        def with_three():
            late_sum.send(0).start()
            three()

        def with_two():
            late_sum.to_x()
            two()

        def with_one():
            late_sum.send(1).start()
            one()

        after(s, with_three, with_two, with_one, zero)

    late_sum.to_y()
    for s in range(SLOTS):
        turn("t%d" % s)
        dg[s, 0:S, 0:3 * QW] = nt(unperm[...], qkv[s]).astype(BF16)
        dg[s, S:2 * S, 0:QW] = nt(unperm[...], qg[s]).astype(BF16)
    late_sum.to_z()
    sm_res[0] = early_sum.total()

    def row_grads(s):
        for j in range(0, D, 256):
            acc[0:S, j:j + 256] += nn(dg[s, 0:S, 0:3 * QW], wq[s, :, j:j + 256])
            acc[S:2 * S, j:j + 256] += nn(dg[s, S:2 * S, 0:QW], wq[s, 0:QW, j:j + 256])

    for s in range(SLOTS):
        turn("t%d" % (SLOTS + s))
        row_grads(s)
    rows_out = [
        pltpu.make_async_copy(acc.at[0:S], gc_hbm, lsem.at[0]),
        pltpu.make_async_copy(acc.at[S:2 * S], gg_hbm, lsem.at[1]),
    ]
    for copy in rows_out:
        copy.start()
    turn("t8")
    sm_res[1, 0:1] = late_sum.total()
    sm_res[1, 1:8] = jnp.zeros((7, D), F32)
    drain(dg.at[0:3, 0:960], os.at[0])
    for group in (GA, GB):
        group.send(0).wait_send()
    for group in (GC, GD, GW):
        group.send(0).wait_send()
        group.send(1).wait_send()
    for k in range(7):
        early_sum.send(k).wait_send()
        late_sum.send(k).wait_send()
    turn("t9")
    g_res[2, :, 5 * 128:] = jnp.zeros((ROWS, 128), F32)
    results = [
        pltpu.make_async_copy(src, dst, osem.at[k])
        for k, (src, dst) in enumerate(((g_res, g_out), (g_w, gw_out), (sm_res, sm_out)))
    ]
    for copy in results:
        copy.start()

    for copy in rows_out:
        copy.wait()
    for copy in results:
        copy.wait()
    drain(dg.at[0:3, 0:560], os.at[1])


def layer(stride, *args):
    smem = pl.BlockSpec(memory_space=pltpu.SMEM)
    hbm = pl.BlockSpec(memory_space=pl.ANY)
    sd = jax.ShapeDtypeStruct
    vm = pltpu.VMEM
    dma = pltpu.SemaphoreType.DMA
    return pl.pallas_call(
        functools.partial(kernel, stride),
        out_shape=(
            sd((S, D), BF16), sd((S, D), BF16), sd((S, D), F32), sd((S, D), F32),
            sd((SLOTS, 2 * S, D), BF16), sd((D, 2 * S), BF16), sd((3, ROWS, D), F32), sd((ROWS, 256), F32), sd((2, 8, D), F32),
        ),
        in_specs=[smem, smem] + [hbm] * 18,
        out_specs=(hbm,) * 9,
        scratch_shapes=[
            vm((S, S), BF16), vm((S, S), BF16), vm((2 * S, D), BF16), vm((2 * S, D), BF16),
            vm((D, 2 * S), BF16), vm((D, 2 * S), BF16), vm((2 * S, D), BF16),
            vm((SLOTS, 3 * QW, S), BF16), vm((SLOTS, QW, S), BF16), vm((2 * S, D), BF16), vm((2 * S, 1), F32),
            vm((SLOTS, 2 * S, D), BF16), vm((SLOTS, 2 * S, D), BF16), vm((2 * S, D), F32),
            vm((2, HALF, S), BF16), vm((32, S), F32),
            vm((SLOTS, 3 * QW, D), BF16), vm((D, D), BF16), vm((SLOTS, D, D), BF16), vm((SLOTS, D, D), BF16),
            vm((SLOTS, 8, D), F32), vm((8, D), F32),
            vm((3, D, D), BF16), vm((3, D, D), BF16), vm((2, D, D), BF16), vm((2, D, D), BF16),
            vm((2, 3, D, 256), BF16), vm((6 * ROWS, D), BF16),
            vm((8, D), F32),
            vm((SLOTS, 8, D), F32), vm((2, 8, D), F32), vm((2, 8, D), F32), vm((8, D), F32), vm((8, D), F32),
            vm((8, D), F32), vm((3, 8, D), F32),
            vm((SLOTS, 1, D), F32), vm((2, 1, D), F32), vm((2, 1, D), F32), vm((1, D), F32), vm((1, D), F32),
            vm((1, D), F32), vm((3, 1, D), F32),
            vm((SLOTS, S), jnp.int32), vm((D,), BF16), vm((2, QW), BF16), vm((SLOT_HEADS, 32), BF16),
            vm((D,), BF16), vm((D,), F32), vm((D,), F32), vm((D,), BF16), vm((D,), F32), vm((D,), F32),
            vm((3, ROWS, D), F32), vm((ROWS, 256), F32), vm((2, 8, D), F32), dma((3,)), dma((10,)), dma((5, 2)), dma((5, 2)), dma((1,)), dma((4,)),
            dma((12,)), dma((1,)), dma((len(ITEMS), 6)), dma((1,)), dma((4,)), dma((3,)), dma((3,)),
            dma((2,)), dma((sum({"x": 3, "y": 4, "z": 6}[k] for k in KINDS),)), dma((14,)), dma((14,)), pltpu.SemaphoreType.REGULAR((6,)),
        ],
        compiler_params=pltpu.CompilerParams(
            vmem_limit_bytes=int(63.5 * (1 << 20)), collective_id=0, has_side_effects=True
        ),
    )(*args)


def hand_out(
    oc_in, og_in, gc_in, gg_in, gw_hbm, gwo_hbm, sm_hbm,
    oc, og, gc, gg, g_qkv, g_bias, g_attn, b_attn, n1g, n1s, g_in, b_in, g_out, b_out, n2g, n2s, g_table,
    wide, narrow, gw, gwo, sm, v_qkv, v_bias, v_attn, lines, v_table, sems,
):
    def moves(pairs, base):
        copies = [pltpu.make_async_copy(src, dst, sems.at[base + k]) for k, (src, dst) in enumerate(pairs)]
        for copy in copies:
            copy.start()
        return copies

    smalls = moves(((sm_hbm, sm), (gwo_hbm, gwo), (gw_hbm, gw)), 0)
    vias = (wide.at[0], wide.at[1], narrow.at[0], narrow.at[1])
    rows_in = moves(tuple(zip((gc_in, gg_in, oc_in, og_in), vias)), 3)
    for copy in smalls:
        copy.wait()
    v_attn[...] = gwo[:, 0:QW].T
    for k in range(3):
        v_qkv[k, :, 0:2 * HD] = gw[2, :, 2 * HD * k:2 * HD * k + 2 * HD]
        v_qkv[k, :, 2 * HD:QW] = gw[2, :, D // 2 + HD * k:D // 2 + HD * k + HD]
    v_bias[0:1] = sm[1, 0:1, 0:QW]
    v_bias[1:2] = sm[1, 0:1, QW:2 * QW]
    for k in range(SLOT_HEADS):
        v_table[k:k + 1] = sm[1, 0:1, 2 * QW + 32 * k:2 * QW + 32 * k + 32]
    for k, line in enumerate(lines):
        line[...] = sm[0, k:k + 1].reshape(D)
    outs = moves(
        ((gw.at[0], g_out), (gw.at[1], g_in), (v_qkv, g_qkv), (v_attn, g_attn), (v_bias, g_bias), (v_table, g_table))
        + tuple(zip(lines, (b_in, b_attn, n1g, n1s, b_out, n2g, n2s))),
        7,
    )
    for k, (copy, via, dst) in enumerate(zip(rows_in, vias, (gc, gg, oc, og))):
        copy.wait()
        outs += moves(((via, dst),), 20 + k)
    for copy in outs:
        copy.wait()


def local(
    stride,
    content, query_stream, cot_content, cot_query, doc_lengths, rank_order, pred_counts, w_qkv, bias_qv,
    w_attn_out, b_attn_out, norm1_gain, norm1_shift, w_in, b_in, w_out, b_out, norm2_gain, norm2_shift, rel_table,
):
    out_c, out_g, gc, gg, _, _, gw, gwo, sm = layer(
        stride, doc_lengths, pred_counts, content, query_stream, cot_content, cot_query,
        jnp.transpose(w_qkv, (0, 2, 1)).reshape(3 * QW, D), w_attn_out, w_in, w_out,
        rank_order, b_in, bias_qv, rel_table.T, b_attn_out, norm1_gain, norm1_shift, b_out, norm2_gain, norm2_shift,
    )
    if stride > 1:
        groups = [list(range(k * stride, k * stride + stride)) for k in range(8)]
        gw = lax.psum_scatter(gw, "dp", scatter_dimension=1, axis_index_groups=groups, tiled=True)
        gwo = lax.psum_scatter(gwo, "dp", scatter_dimension=0, axis_index_groups=groups, tiled=True)
        sm = lax.psum(sm, "dp") / 8.0
    rows = gw.shape[1]
    sd = jax.ShapeDtypeStruct
    hbm = pl.BlockSpec(memory_space=pl.ANY)
    vm = pltpu.VMEM
    line = sd((D,), F32)
    outs = pl.pallas_call(
        hand_out,
        out_shape=(
            sd((S, D), BF16), sd((S, D), BF16), sd((S, D), F32), sd((S, D), F32),
            sd((3, rows, QW), F32), sd((2, QW), F32), sd((QW, rows), F32), line, line, line,
            sd((rows, D), F32), line, sd((rows, D), F32), line, line, line, sd((SLOT_HEADS, 32), F32),
        ),
        in_specs=[hbm] * 7,
        out_specs=[hbm] * 17,
        scratch_shapes=[
            vm((2, S, D), F32), vm((2, S, D), BF16), vm((3, rows, D), F32), vm((rows, 256), F32), vm((2, 8, D), F32),
            vm((3, rows, QW), F32), vm((2, QW), F32), vm((QW, rows), F32), [vm((D,), F32)] * 7,
            vm((SLOT_HEADS, 32), F32), pltpu.SemaphoreType.DMA((24,)),
        ],
        compiler_params=pltpu.CompilerParams(vmem_limit_bytes=int(63.5 * (1 << 20))),
    )(out_c, out_g, gc, gg, gw, gwo, sm)
    outs = list(outs)
    outs[12] = outs[12].T
    outs[16] = outs[16].T
    return tuple(outs)


def solution(mesh):
    in_specs = (
        P(("dp", "tensor"), None),
        P(("dp", "tensor"), None),
        P(("dp", "tensor"), None),
        P(("dp", "tensor"), None),
        P("dp", None),
        P("dp", None),
        P("dp"),
        P(None, None, "tensor"),
        P(None, "tensor"),
        P("tensor", None),
        P(),
        P(),
        P(),
        P(None, "tensor"),
        P("tensor"),
        P("tensor", None),
        P(),
        P(),
        P(),
        P(None, "tensor"),
    )
    out_specs = (
        P(("dp", "tensor"), None),
        P(("dp", "tensor"), None),
        P(("dp", "tensor"), None),
        P(("dp", "tensor"), None),
        P(None, "dp", "tensor"),
        P(None, "tensor"),
        P("tensor", "dp"),
        P(),
        P(),
        P(),
        P("dp", "tensor"),
        P("tensor"),
        P("tensor", "dp"),
        P(),
        P(),
        P(),
        P(None, "tensor"),
    )
    stride = mesh.shape["dp"] // 8
    return jax.shard_map(functools.partial(local, stride), mesh=mesh, in_specs=in_specs, out_specs=out_specs, check_vma=False)
```
